32 devices in a mesh: dp: 4 (over y, x), ctx: 2 (over core), tp: 4 (over z).
Axes of the slice: x: 2, y: 2, z: 4, core: 2. Of those that a mesh axis runs over, the one named last changes fastest.
Arguments:
- tokens: bfloat16 [16384, 1024], P(('dp', 'ctx')), may hold values from -6 to 6
- cotangent: bfloat16 [16384, 1024], P(('dp', 'ctx')), may hold values from -6 to 6
- lengths: int32 [4], P('dp'), may hold values from 2049 to 4096, as said below
- query_key_weight: float32 [2, 1024, 512], P(None, ('dp', 'ctx'), 'tp'), may hold values from -0.1875 to 0.1875
- query_key_mean: float32 [2, 1024, 512], P(None, ('dp', 'ctx'), 'tp'), may hold values from -40 to 40
- query_key_square: float32 [2, 1024, 512], P(None, ('dp', 'ctx'), 'tp'), may hold values from 108.1344 to 1638.4
- value_gate_weight: float32 [2, 1024, 1024], P(None, ('dp', 'ctx'), 'tp'), may hold values from -0.1875 to 0.1875
- value_gate_mean: float32 [2, 1024, 1024], P(None, ('dp', 'ctx'), 'tp'), may hold values from -40 to 40
- value_gate_square: float32 [2, 1024, 1024], P(None, ('dp', 'ctx'), 'tp'), may hold values from 108.1344 to 1638.4
- decay_in_weight: float32 [1024, 16], P(('dp', 'ctx')), may hold values from -0.1875 to 0.1875
- decay_in_mean: float32 [1024, 16], P(('dp', 'ctx')), may hold values from -40 to 40
- decay_in_square: float32 [1024, 16], P(('dp', 'ctx')), may hold values from 108.1344 to 1638.4
- decay_out_weight: float32 [16, 512], P(None, 'tp'), may hold values from -1.5 to 1.5
- decay_out_mean: float32 [16, 512], P(None, 'tp'), may hold values from -40 to 40
- decay_out_square: float32 [16, 512], P(None, 'tp'), may hold values from 108.1344 to 1638.4
- decay_bias: float32 [512], P('tp'), may hold values from 0 to 9
- decay_bias_mean: float32 [512], P('tp'), may hold values from -40 to 40
- decay_bias_square: float32 [512], P('tp'), may hold values from 108.1344 to 1638.4
- output_weight: float32 [1024, 1024], P('tp', ('dp', 'ctx')), may hold values from -0.1875 to 0.1875
- output_mean: float32 [1024, 1024], P('tp', ('dp', 'ctx')), may hold values from -40 to 40
- output_square: float32 [1024, 1024], P('tp', ('dp', 'ctx')), may hold values from 108.1344 to 1638.4
- gate_up_weight: float32 [2, 1024, 2816], P(None, ('dp', 'ctx'), 'tp'), may hold values from -0.1875 to 0.1875
- gate_up_mean: float32 [2, 1024, 2816], P(None, ('dp', 'ctx'), 'tp'), may hold values from -40 to 40
- gate_up_square: float32 [2, 1024, 2816], P(None, ('dp', 'ctx'), 'tp'), may hold values from 108.1344 to 1638.4
- down_weight: float32 [2816, 1024], P('tp', ('dp', 'ctx')), may hold values from -0.109375 to 0.109375
- down_mean: float32 [2816, 1024], P('tp', ('dp', 'ctx')), may hold values from -40 to 40
- down_square: float32 [2816, 1024], P('tp', ('dp', 'ctx')), may hold values from 108.1344 to 1638.4
- gains: float32 [2304], replicated, may hold values from 0.5 to 1.5
- gains_mean: float32 [2304], replicated, may hold values from -40 to 40
- gains_square: float32 [2304], replicated, may hold values from 108.1344 to 1638.4
Outputs:
- layer_out: bfloat16 [16384, 1024], P(('dp', 'ctx'))
- input_grad: float32 [16384, 1024], P(('dp', 'ctx'))
- query_key_mean_new: float32 [2, 1024, 512], P(None, ('dp', 'ctx'), 'tp')
- query_key_square_new: float32 [2, 1024, 512], P(None, ('dp', 'ctx'), 'tp')
- query_key_new: float32 [2, 1024, 512], P(None, ('dp', 'ctx'), 'tp')
- value_gate_mean_new: float32 [2, 1024, 1024], P(None, ('dp', 'ctx'), 'tp')
- value_gate_square_new: float32 [2, 1024, 1024], P(None, ('dp', 'ctx'), 'tp')
- value_gate_new: float32 [2, 1024, 1024], P(None, ('dp', 'ctx'), 'tp')
- decay_in_mean_new: float32 [1024, 16], P(('dp', 'ctx'))
- decay_in_square_new: float32 [1024, 16], P(('dp', 'ctx'))
- decay_in_new: float32 [1024, 16], P(('dp', 'ctx'))
- decay_out_mean_new: float32 [16, 512], P(None, 'tp')
- decay_out_square_new: float32 [16, 512], P(None, 'tp')
- decay_out_new: float32 [16, 512], P(None, 'tp')
- decay_bias_mean_new: float32 [512], P('tp')
- decay_bias_square_new: float32 [512], P('tp')
- decay_bias_new: float32 [512], P('tp')
- output_mean_new: float32 [1024, 1024], P('tp', ('dp', 'ctx'))
- output_square_new: float32 [1024, 1024], P('tp', ('dp', 'ctx'))
- output_new: float32 [1024, 1024], P('tp', ('dp', 'ctx'))
- gate_up_mean_new: float32 [2, 1024, 2816], P(None, ('dp', 'ctx'), 'tp')
- gate_up_square_new: float32 [2, 1024, 2816], P(None, ('dp', 'ctx'), 'tp')
- gate_up_new: float32 [2, 1024, 2816], P(None, ('dp', 'ctx'), 'tp')
- down_mean_new: float32 [2816, 1024], P('tp', ('dp', 'ctx'))
- down_square_new: float32 [2816, 1024], P('tp', ('dp', 'ctx'))
- down_new: float32 [2816, 1024], P('tp', ('dp', 'ctx'))
- gains_mean_new: float32 [2304], replicated
- gains_square_new: float32 [2304], replicated
- gains_new: float32 [2304], replicated
The draws below stay inside these ranges and needn't reach their ends.
Inputs may be any that keep to these rules, and one draw needn't show every extreme that they name: `lengths`: 4096 in some sequence in every draw.
All inputs are finite; a program needn't handle non-finite values.
Results may differ from the reference program's by a relative error of at most 0.012.
The reference program's roundings to bfloat16 on the way count: a program that leaves them out, or rounds other values in their place, can miss the bound.
Values may be sent and summed in bfloat16 or wider, within the bound.
No kernel may reach another device: no remote copies, remote signals or barrier semaphores. Data moves between devices by JAX's collectives and lax.ppermute only.
A program may use at most 192 MiB of HBM per device.

```python
import math
import jax
import jax.numpy as jnp
from jax import lax

D = 1024
HEADS = 4
HK = 128
HV = 256
R = 16
FF = 2816
DK = 512
DV = 1024
C = 64
STEP = 10
TOK_DEV = 2048
GROUP_TOK = 4096
TOKENS = 16384
N_DP = 4
N_CTX = 2


def draw_lengths(key, part):
    key = jax.random.fold_in(key, 11)
    key_one, key_two = jax.random.split(key)
    least = (N_CTX - 1) * TOK_DEV + 1
    most = N_CTX * TOK_DEV
    drawn = jax.random.randint(key_one, (N_DP,), least, most + 1)
    chosen = jax.random.randint(key_two, (), 0, N_DP)
    return jnp.where(jnp.arange(N_DP) == chosen, most, drawn).astype(jnp.int32)


def with_spikes(values, rng, source, target, shards_of, factor):
    def block_of(dim):
        return (jnp.arange(values.shape[dim]) // (values.shape[dim] // shards_of)).reshape((-1,) + (1,) * (values.ndim - 1 - dim))

    first = jax.random.permutation(rng, shards_of)[block_of(target)]
    other_side = (block_of(target) + shards_of // 2) % shards_of
    return jnp.where((block_of(source) == first) | (block_of(source) == other_side), factor * values, values)


def shard_levels(key, shape, shards, smallest, high):
    level = 1.0
    for axis_at, parts in shards:
        steps = jax.random.uniform(jax.random.fold_in(jax.random.fold_in(key, 6), axis_at), (parts,), jnp.float32, smallest / len(shards), high / len(shards))
        level = level * jnp.repeat(jnp.exp(steps), shape[axis_at] // parts).reshape((-1,) + (1,) * (len(shape) - 1 - axis_at))
    return level


def normal_values(rng, shape, deviation, reach, pieces=(), kind=jnp.bfloat16):
    level = shard_levels(rng, shape, pieces, -0.22, 0.18) if pieces else 1.0
    array = jax.random.normal(rng, shape, jnp.float32) * deviation * level
    return jnp.minimum(jnp.maximum(array, -reach), reach).astype(kind)


def heavy_noise(own_key, shape, scale, reach, pieces, heavy, kind=jnp.bfloat16):
    array = scale * jax.random.normal(own_key, shape, jnp.float32)
    if pieces:
        array = array * shard_levels(own_key, shape, pieces, -0.22, 0.18)
    return jnp.clip(with_spikes(array, jax.random.fold_in(own_key, 3), *heavy), -reach, reach).astype(kind)


def setup_inputs(seed: int = 0) -> dict:
    key_of = jax.random.split(jax.random.key(seed), 31)
    tokens = normal_values(key_of[0], (TOKENS, D), 1.0, 6.0, ((0, 8),))
    cotangent = heavy_noise(key_of[1], (TOKENS, D), 1.0, 6.0, ((0, 8),), (0, 1, 8, 2.0))
    lengths = draw_lengths(jax.random.fold_in(key_of[30], 71), 0)
    query_key_weight = normal_values(key_of[3], (2, D, DK), D ** -0.5, 0.1875, ((1, 8), (2, 4)), jnp.float32)
    query_key_mean = normal_values(key_of[4], (2, D, DK), (0.055 * TOKENS ** 0.5), 40.0, ((1, 8), (2, 4)), jnp.float32)
    query_key_square = jnp.clip(jnp.exp(math.log(1638.4) - 2.7181006 * jax.random.uniform(key_of[5], (2, D, DK), jnp.float32) ** shard_levels(key_of[5], (2, D, DK), ((1, 8), (2, 4)), -0.2, 0.2)), 108.1344, 1638.4)
    value_gate_weight = normal_values(key_of[6], (2, D, DV), D ** -0.5, 0.1875, ((1, 8), (2, 4)), jnp.float32)
    value_gate_mean = normal_values(key_of[7], (2, D, DV), (0.055 * TOKENS ** 0.5), 40.0, ((1, 8), (2, 4)), jnp.float32)
    value_gate_square = jnp.clip(jnp.exp(math.log(1638.4) - 2.7181006 * jax.random.uniform(key_of[8], (2, D, DV), jnp.float32) ** shard_levels(key_of[8], (2, D, DV), ((1, 8), (2, 4)), -0.2, 0.2)), 108.1344, 1638.4)
    decay_in_weight = normal_values(key_of[9], (D, R), D ** -0.5, 0.1875, ((0, 8),), jnp.float32)
    decay_in_mean = normal_values(key_of[10], (D, R), (0.055 * TOKENS ** 0.5), 40.0, ((0, 8),), jnp.float32)
    decay_in_square = jnp.clip(jnp.exp(math.log(1638.4) - 2.7181006 * jax.random.uniform(key_of[11], (D, R), jnp.float32) ** shard_levels(key_of[11], (D, R), ((0, 8),), -0.2, 0.2)), 108.1344, 1638.4)
    decay_out_weight = normal_values(key_of[12], (R, DK), R ** -0.5, 1.5, ((1, 4),), jnp.float32)
    decay_out_mean = normal_values(key_of[13], (R, DK), (0.055 * TOKENS ** 0.5), 40.0, ((1, 4),), jnp.float32)
    decay_out_square = jnp.clip(jnp.exp(math.log(1638.4) - 2.7181006 * jax.random.uniform(key_of[14], (R, DK), jnp.float32) ** shard_levels(key_of[14], (R, DK), ((1, 4),), -0.2, 0.2)), 108.1344, 1638.4)
    decay_bias = jnp.clip(9.0 * jax.random.uniform(key_of[15], (DK,), jnp.float32) ** shard_levels(key_of[15], (DK,), ((0, 4),), -0.2, 0.2), 0.0, 9.0)
    decay_bias_mean = normal_values(key_of[16], (DK,), (0.055 * TOKENS ** 0.5), 40.0, ((0, 4),), jnp.float32)
    decay_bias_square = jnp.clip(jnp.exp(math.log(1638.4) - 2.7181006 * jax.random.uniform(key_of[17], (DK,), jnp.float32) ** shard_levels(key_of[17], (DK,), ((0, 4),), -0.2, 0.2)), 108.1344, 1638.4)
    output_weight = normal_values(key_of[18], (DV, D), DV ** -0.5, 0.1875, ((0, 4), (1, 8)), jnp.float32)
    output_mean = normal_values(key_of[19], (DV, D), (0.055 * TOKENS ** 0.5), 40.0, ((0, 4), (1, 8)), jnp.float32)
    output_square = jnp.clip(jnp.exp(math.log(1638.4) - 2.7181006 * jax.random.uniform(key_of[20], (DV, D), jnp.float32) ** shard_levels(key_of[20], (DV, D), ((0, 4), (1, 8)), -0.2, 0.2)), 108.1344, 1638.4)
    gate_up_weight = normal_values(key_of[21], (2, D, FF), D ** -0.5, 0.1875, ((1, 8), (2, 4)), jnp.float32)
    gate_up_mean = normal_values(key_of[22], (2, D, FF), (0.055 * TOKENS ** 0.5), 40.0, ((1, 8), (2, 4)), jnp.float32)
    gate_up_square = jnp.clip(jnp.exp(math.log(1638.4) - 2.7181006 * jax.random.uniform(key_of[23], (2, D, FF), jnp.float32) ** shard_levels(key_of[23], (2, D, FF), ((1, 8), (2, 4)), -0.2, 0.2)), 108.1344, 1638.4)
    down_weight = normal_values(key_of[24], (FF, D), FF ** -0.5, 0.109375, ((0, 4), (1, 8)), jnp.float32)
    down_mean = normal_values(key_of[25], (FF, D), (0.055 * TOKENS ** 0.5), 40.0, ((0, 4), (1, 8)), jnp.float32)
    down_square = jnp.clip(jnp.exp(math.log(1638.4) - 2.7181006 * jax.random.uniform(key_of[26], (FF, D), jnp.float32) ** shard_levels(key_of[26], (FF, D), ((0, 4), (1, 8)), -0.2, 0.2)), 108.1344, 1638.4)
    gains = jnp.clip(1.0 + 0.1 * jax.random.normal(key_of[27], (2 * D + HV,), jnp.float32), 0.5, 1.5)
    gains_mean = normal_values(key_of[28], (2 * D + HV,), (0.055 * TOKENS ** 0.5), 40.0, (), jnp.float32)
    gains_square = jnp.clip(jnp.exp(jax.random.uniform(key_of[29], (2 * D + HV,), jnp.float32, math.log(108.1344), math.log(1638.4))), 108.1344, 1638.4)
    return dict(tokens=tokens, cotangent=cotangent, lengths=lengths, query_key_weight=query_key_weight, query_key_mean=query_key_mean, query_key_square=query_key_square, value_gate_weight=value_gate_weight, value_gate_mean=value_gate_mean, value_gate_square=value_gate_square, decay_in_weight=decay_in_weight, decay_in_mean=decay_in_mean, decay_in_square=decay_in_square, decay_out_weight=decay_out_weight, decay_out_mean=decay_out_mean, decay_out_square=decay_out_square, decay_bias=decay_bias, decay_bias_mean=decay_bias_mean, decay_bias_square=decay_bias_square, output_weight=output_weight, output_mean=output_mean, output_square=output_square, gate_up_weight=gate_up_weight, gate_up_mean=gate_up_mean, gate_up_square=gate_up_square, down_weight=down_weight, down_mean=down_mean, down_square=down_square, gains=gains, gains_mean=gains_mean, gains_square=gains_square)


NORM_EPS = 1e-06
HEAD_EPS = 1e-05
GATE_SCALE = 16.0
BETA_ONE = 0.9
BETA_TWO = 0.95
ADAM_EPS = 1e-08
WEIGHT_DECAY = 0.1
RATE_MATRIX = 0.03
RATE_RANK = 0.1
RATE_BIAS = 1.5
RATE_GAIN = 0.3
BEST_PRECISION = lax.Precision.HIGHEST

@jax.custom_vjp
def low(v):
    return lax.optimization_barrier(v.astype(jnp.bfloat16)).astype(jnp.float32)

@jax.custom_vjp
def low_back(v):
    return v

def low_keep(v):
    return (low(v), None)

def low_pass(kept, grad):
    return (grad,)

def back_keep(v):
    return (v, None)

def back_low(kept, grad):
    return (low(grad),)
low.defvjp(low_keep, low_pass)
low_back.defvjp(back_keep, back_low)

def norm_apply(values, gain, epsilon):
    return values * lax.rsqrt(lax.optimization_barrier(jnp.mean(values * values, axis=-1, keepdims=True)) + epsilon) * gain

def silu_fn(values):
    return values * jax.nn.sigmoid(values)

def gla_head(query_matrix, key_rows, value_rows, log_decay, start_state):
    total = query_matrix.shape[0]
    blocks = total // C
    query_blocks = query_matrix.reshape(blocks, C, -1)
    key_blocks = key_rows.reshape(blocks, C, -1)
    value_block_list = value_rows.reshape(blocks, C, -1)
    cumulative = jnp.cumsum(log_decay.reshape(blocks, C, -1), axis=1)
    block_total = cumulative[:, -1]
    scaled_query_rows = query_blocks * jnp.exp(cumulative)
    key_scaled = key_blocks * jnp.exp(-cumulative)
    carried_key_rows = key_blocks * jnp.exp(block_total[:, None, :] - cumulative)
    causal = (jnp.arange(C)[:, None] >= jnp.arange(C)[None, :]).astype(jnp.float32)
    scores = jnp.einsum('nck,nsk->ncs', scaled_query_rows, key_scaled, precision=BEST_PRECISION) * causal
    inner = jnp.einsum('ncs,nsv->ncv', scores, value_block_list, precision=BEST_PRECISION)
    update_terms = jnp.einsum('tfl,tfd->tld', carried_key_rows, value_block_list, precision=BEST_PRECISION)

    def advance(state, item):
        return (jnp.exp(item[0])[:, None] * state + item[1], state)
    final_state, start_offsets = lax.scan(advance, start_state, (block_total, update_terms))
    outer_product = jnp.einsum('max,mxd->mad', scaled_query_rows, start_offsets, precision=BEST_PRECISION)
    return ((inner + outer_product).reshape(total, -1), final_state)

def adamw(weight_now, grad_now, mean_now, square_now, rate_value, decay_value):
    mean_new = BETA_ONE * mean_now + (1.0 - BETA_ONE) * grad_now
    square_new = BETA_TWO * square_now + (1.0 - BETA_TWO) * grad_now * grad_now
    mean_hat = mean_new / (1.0 - BETA_ONE ** STEP)
    square_hat = square_new / (1.0 - BETA_TWO ** STEP)
    weight_new = weight_now - rate_value * (mean_hat / (jnp.sqrt(square_hat) + ADAM_EPS) + decay_value * weight_now)
    return (mean_new, square_new, weight_new)

def layer(inputs, query_key_weight, value_gate_weight, decay_in_weight, decay_out_weight, decay_bias, output_weight, gate_up_weight, down_weight, gains):
    gain_one = gains[:D]
    gain_two = gains[D:2 * D]
    gain_head = gains[2 * D:]
    normed = low(norm_apply(inputs, gain_one, NORM_EPS))

    def project(weight):
        return jnp.dot(normed, low(weight), precision=BEST_PRECISION)
    query_matrix = low_back(project(query_key_weight[0])) * HK ** (-0.5)
    key_rows = low_back(project(query_key_weight[1]))
    value_rows = low_back(project(value_gate_weight[0]))
    out_gate = low_back(project(value_gate_weight[1]))
    decay_rank = low_back(project(decay_in_weight))
    logits = jnp.dot(decay_rank, decay_out_weight, precision=BEST_PRECISION) + decay_bias
    log_decay = jax.nn.log_sigmoid(logits) / GATE_SCALE

    def split_heads(values_in, head_width):
        return values_in.reshape(N_DP, GROUP_TOK, HEADS, head_width).transpose(0, 2, 1, 3)
    start_state = jnp.zeros((N_DP, HEADS, HK, HV), jnp.float32)
    mixed_out, end_states = jax.vmap(jax.vmap(gla_head))(split_heads(query_matrix, HK), split_heads(key_rows, HK), split_heads(value_rows, HV), split_heads(log_decay, HK), start_state)
    mixed_out = mixed_out.transpose(0, 2, 1, 3).reshape(TOKENS, HEADS, HV)
    gated = low((norm_apply(mixed_out, gain_head, HEAD_EPS) * silu_fn(out_gate.reshape(TOKENS, HEADS, HV))).reshape(TOKENS, DV))
    attn_sum = low_back(jnp.dot(gated, low(output_weight), precision=BEST_PRECISION))
    middle = inputs + attn_sum
    normed_two = low(norm_apply(middle, gain_two, NORM_EPS))
    gate_values = low_back(jnp.dot(normed_two, low(gate_up_weight[0]), precision=BEST_PRECISION))
    upward = low_back(jnp.dot(normed_two, low(gate_up_weight[1]), precision=BEST_PRECISION))
    active = low(silu_fn(gate_values) * upward)
    ffn_sum = low_back(jnp.dot(active, low(down_weight), precision=BEST_PRECISION))
    return middle + ffn_sum

def reference(tokens, cotangent, lengths, query_key_weight, query_key_mean, query_key_square, value_gate_weight, value_gate_mean, value_gate_square, decay_in_weight, decay_in_mean, decay_in_square, decay_out_weight, decay_out_mean, decay_out_square, decay_bias, decay_bias_mean, decay_bias_square, output_weight, output_mean, output_square, gate_up_weight, gate_up_mean, gate_up_square, down_weight, down_mean, down_square, gains, gains_mean, gains_square):
    params = (query_key_weight, value_gate_weight, decay_in_weight, decay_out_weight, decay_bias, output_weight, gate_up_weight, down_weight, gains)
    inputs = tokens.astype(jnp.float32)
    result, pullback = jax.vjp(layer, inputs, *params)
    position = jnp.arange(TOKENS, dtype=jnp.int32)
    limit = lengths[position // GROUP_TOK]
    live_rows = (position % GROUP_TOK < limit).astype(jnp.float32)
    grads = pullback(cotangent.astype(jnp.float32) * live_rows[:, None])
    input_grad = grads[0]
    moments = ((query_key_mean, query_key_square, RATE_MATRIX, WEIGHT_DECAY), (value_gate_mean, value_gate_square, RATE_MATRIX, WEIGHT_DECAY), (decay_in_mean, decay_in_square, RATE_MATRIX, WEIGHT_DECAY), (decay_out_mean, decay_out_square, RATE_RANK, WEIGHT_DECAY), (decay_bias_mean, decay_bias_square, RATE_BIAS, 0.0), (output_mean, output_square, RATE_MATRIX, WEIGHT_DECAY), (gate_up_mean, gate_up_square, RATE_MATRIX, WEIGHT_DECAY), (down_mean, down_square, RATE_MATRIX, WEIGHT_DECAY), (gains_mean, gains_square, RATE_GAIN, 0.0))
    updated = ()
    for weight, grad, state in zip(params, grads[1:], moments):
        updated = updated + adamw(weight, grad, state[0], state[1], state[2], state[3])
    return (result.astype(jnp.bfloat16), input_grad) + updated
```

```python
import functools

import jax
import jax.numpy as jnp
from jax import lax
from jax.experimental import pallas as pl
from jax.experimental.pallas import tpu as pltpu
from jax.sharding import PartitionSpec as P

HK = 128
HV = 256
BLOCK = 128
MID = 63
ROWS = 256
FFN_ROWS = 512
STEP = 10

NORM_EPS = 1e-06
HEAD_EPS = 1e-05
GATE_SCALE = 16.0
BETA_ONE = 0.9
BETA_TWO = 0.95
ADAM_EPS = 1e-08
WEIGHT_DECAY = 0.1
RATE_MATRIX = 0.03
RATE_RANK = 0.1
RATE_BIAS = 1.5
RATE_GAIN = 0.3
VMEM_LIMIT = 60 * 1024 * 1024

F32 = jnp.float32
BF16 = jnp.bfloat16
NN = (((1,), (0,)), ((), ()))
NT = (((1,), (1,)), ((), ()))
TN = (((0,), (0,)), ((), ()))


def dot(left, right, dims=NN):
    return lax.dot_general(left, right, dims, preferred_element_type=F32)


def split_two(values):
    high = values.astype(BF16)
    return high, (values - high.astype(F32)).astype(BF16)


def dot_split(left, right, dims=NN):
    return (
        dot(left[0], right[0], dims) + dot(left[0], right[1], dims) + dot(left[1], right[0], dims)
    )


def dot_exact(matrix, values):
    high = values.astype(BF16)
    rest = values - high.astype(F32)
    middle = rest.astype(BF16)
    low = (rest - middle.astype(F32)).astype(BF16)
    return dot(matrix, high) + dot(matrix, middle) + dot(matrix, low)


def lower_mask():
    rows = lax.broadcasted_iota(jnp.int32, (BLOCK, BLOCK), 0)
    columns = lax.broadcasted_iota(jnp.int32, (BLOCK, BLOCK), 1)
    return rows >= columns


def upper_mask():
    rows = lax.broadcasted_iota(jnp.int32, (BLOCK, BLOCK), 0)
    columns = lax.broadcasted_iota(jnp.int32, (BLOCK, BLOCK), 1)
    return rows <= columns


def as_ones(mask):
    return jnp.where(mask, 1.0, 0.0).astype(BF16)


def inverse_rms(values, epsilon):
    return lax.rsqrt(jnp.mean(values * values, axis=-1, keepdims=True) + epsilon)


def sigmoid(values):
    return 1.0 / (1.0 + jnp.exp(-values))


def project_kernel(
    tokens, gain, weight, rank_weight, decay_out, bias,
    normed_out, qkv_out, gate_out, rank_out, logits_out, cum_out, state_out, total_out,
):
    heads = weight.shape[0]

    @pl.when(pl.program_id(0) == 0)
    def _():
        state_out[...] = jnp.zeros_like(state_out)
        total_out[...] = jnp.zeros_like(total_out)

    inputs = tokens[...].astype(F32)
    normed = (inputs * inverse_rms(inputs, NORM_EPS) * gain[...]).astype(BF16)
    normed_out[...] = normed
    rank = dot(normed, rank_weight[0], NT)
    rank_out[...] = rank
    lower = as_ones(lower_mask())
    for head in range(heads):
        made = dot(normed, weight[head], NT)
        query = made[:, :HK] * HK ** (-0.5)
        keys = made[:, HK : 2 * HK]
        values = made[:, 2 * HK : 2 * HK + HV]
        qkv_out[head, :, :HK] = query
        qkv_out[head, :, HK : 2 * HK] = keys
        qkv_out[head, :, 2 * HK :] = values
        gate_out[head] = made[:, 2 * HK + HV :]
        logits = (
            lax.dot_general(
                rank, decay_out[head], NN, precision=lax.Precision.HIGHEST,
                preferred_element_type=F32,
            )
            + bias[head]
        )
        logits_out[head] = logits
        log_decay = (
            jnp.minimum(logits, 0.0) - jnp.log1p(jnp.exp(-jnp.abs(logits)))
        ) / GATE_SCALE
        state = state_out[head]
        for part in range(ROWS // BLOCK):
            span = slice(part * BLOCK, (part + 1) * BLOCK)
            cum = dot_exact(lower, log_decay[span])
            cum_out[head, span] = cum
            total = cum[BLOCK - 1 :]
            carried = split_two(keys[span] * jnp.exp(total - cum))
            state = state * jnp.exp(total) + dot_split(split_two(values[span]), carried, TN)
            total_out[head] += total
        state_out[head] = state


def mix_kernel(
    own, tokens, qkv, gate, cum_in, start, out_weight, head_gain, gain,
    mixed_out, state_out, gated_out, middle_out, normed_out,
    state_ref, gated_ref,
):
    heads = start.shape[0]

    @pl.when(pl.program_id(0) == 0)
    def _():
        state_ref[...] = start[...]

    causal = lower_mask()
    for part in range(ROWS // BLOCK):
        span = slice(part * BLOCK, (part + 1) * BLOCK)
        for head in range(heads):
            query = qkv[head, span, :HK]
            keys = qkv[head, span, HK : 2 * HK]
            values = split_two(qkv[head, span, 2 * HK :])
            cum = cum_in[head, span]
            center = cum[MID : MID + 1]
            total = cum[BLOCK - 1 :]
            query_mid = split_two(query * jnp.exp(cum - center))
            key_mid = split_two(keys * jnp.exp(center - cum))
            scores = split_two(jnp.where(causal, dot_split(query_mid, key_mid, NT), 0.0))
            state = state_ref[head]
            state_out[part, head] = state
            mixed = dot_split(scores, values) + dot_split(
                split_two(query * jnp.exp(cum)), split_two(state), NT
            )
            carried = split_two(keys * jnp.exp(total - cum))
            state_ref[head] = state * jnp.exp(total) + dot_split(values, carried, TN)
            mixed_out[head, span] = mixed
            out_gate = gate[head, span]
            gated = (
                mixed * inverse_rms(mixed, HEAD_EPS) * head_gain[...] * (out_gate * sigmoid(out_gate))
            ).astype(BF16)
            gated_ref[span, head * HV : (head + 1) * HV] = gated

            @pl.when(own[0] == head)
            def _():
                gated_out[span] = gated

    width = tokens.shape[1]
    middle = tokens[...].astype(F32) + dot(
        gated_ref[...], out_weight[...].reshape(heads * HV, width)
    )
    middle_out[...] = middle
    normed_out[...] = (middle * inverse_rms(middle, NORM_EPS) * gain[...]).astype(BF16)


def ffn_kernel(
    own, normed, back, middle, weight, gain,
    active_out, back_gate_out, back_up_out, layer_out, back_middle_out, back_attn_out, gain_out,
    ffn_ref, back_ref,
):
    step, piece = pl.program_id(0), pl.program_id(1)
    units = weight.shape[1] // 3

    @pl.when((step == 0) & (piece == 0))
    def _():
        gain_out[...] = jnp.zeros_like(gain_out)

    gate_weight = weight[0, :units]
    up_weight = weight[0, units : 2 * units]
    down_weight = weight[0, 2 * units :]
    gate_values = dot(normed[...], gate_weight, NT)
    upward = dot(normed[...], up_weight, NT)
    back_active = dot(back[...], down_weight, NT)
    share = sigmoid(gate_values)
    silu = gate_values * share
    active = (silu * upward).astype(BF16)
    back_gate = (back_active * upward * (share * (1.0 + gate_values * (1.0 - share)))).astype(BF16)
    back_up = (back_active * silu).astype(BF16)
    ffn = dot(active, down_weight)
    back_normed = dot(back_gate, gate_weight) + dot(back_up, up_weight)

    @pl.when(piece == own[0])
    def _():
        active_out[...] = active
        back_gate_out[...] = back_gate
        back_up_out[...] = back_up

    @pl.when(piece == 0)
    def _():
        ffn_ref[...] = ffn
        back_ref[...] = back_normed

    @pl.when(piece > 0)
    def _():
        ffn_ref[...] += ffn
        back_ref[...] += back_normed

    @pl.when(piece == pl.num_programs(1) - 1)
    def _():
        mid = middle[...]
        layer_out[...] = (mid + ffn_ref[...]).astype(BF16)
        inverse = inverse_rms(mid, NORM_EPS)
        unit = mid * inverse
        total = back_ref[...]
        weighted = total * gain[...]
        back_middle = back[...].astype(F32) + inverse * (
            weighted - unit * jnp.mean(weighted * unit, axis=-1, keepdims=True)
        )
        back_middle_out[...] = back_middle
        back_attn_out[...] = back_middle.astype(BF16)
        gain_out[...] += jnp.sum(total * unit, axis=0, keepdims=True)


def gate_back_kernel(
    back_attn, out_weight, mixed_in, gate, query_in, cum_in, head_gain,
    back_mixed_out, back_gate_out, gain_out, state_out,
):
    heads = gate.shape[0]

    @pl.when(pl.program_id(0) == 0)
    def _():
        gain_out[...] = jnp.zeros_like(gain_out)
        state_out[...] = jnp.zeros_like(state_out)

    for head in range(heads):
        back_gated = dot(back_attn[...], out_weight[head], NT)
        mixed = mixed_in[head]
        out_gate = gate[head]
        inverse = inverse_rms(mixed, HEAD_EPS)
        unit = mixed * inverse
        share = sigmoid(out_gate)
        silu = out_gate * share
        slope = share * (1.0 + out_gate * (1.0 - share))
        back_gate_out[head] = (back_gated * unit * head_gain[...] * slope).astype(BF16)
        gain_out[...] += jnp.sum(back_gated * unit * silu, axis=0, keepdims=True)
        weighted = back_gated * head_gain[...] * silu
        back_mixed = inverse * (
            weighted - unit * jnp.mean(weighted * unit, axis=-1, keepdims=True)
        )
        back_mixed_out[head] = back_mixed
        state = state_out[head]
        for part in reversed(range(ROWS // BLOCK)):
            span = slice(part * BLOCK, (part + 1) * BLOCK)
            cum = cum_in[head, span]
            scaled = split_two(query_in[head, span] * jnp.exp(cum))
            state = state * jnp.exp(cum[BLOCK - 1 :]) + dot_split(
                split_two(back_mixed[span]), scaled, TN
            )
        state_out[head] = state


def mix_back_kernel(
    own, tokens, back_middle, qkv, cum_in, logits_in, states, back_mixed, back_gate, back_end,
    weight, rank_weight, decay_out, rank, gain,
    grad_out, input_out, decay_grad_out, bias_out, gain_out,
    state_ref, back_ref,
):
    heads = weight.shape[0]

    @pl.when(pl.program_id(0) == 0)
    def _():
        state_ref[...] = back_end[...]
        decay_grad_out[...] = jnp.zeros_like(decay_grad_out)
        bias_out[...] = jnp.zeros_like(bias_out)
        gain_out[...] = jnp.zeros_like(gain_out)

    causal = lower_mask()
    upper = as_ones(upper_mask())
    for part in reversed(range(ROWS // BLOCK)):
        span = slice(part * BLOCK, (part + 1) * BLOCK)
        rank_back = jnp.zeros((BLOCK, rank.shape[1]), F32)
        for head in range(heads):
            query = qkv[head, span, :HK]
            keys = qkv[head, span, HK : 2 * HK]
            values = split_two(qkv[head, span, 2 * HK :])
            cum = cum_in[head, span]
            center = cum[MID : MID + 1]
            total = cum[BLOCK - 1 :]
            grow, shrink = jnp.exp(cum - center), jnp.exp(center - cum)
            since, until = jnp.exp(cum), jnp.exp(total - cum)
            query_mid, key_mid = split_two(query * grow), split_two(keys * shrink)
            carried = keys * until
            carried_split = split_two(carried)
            back = split_two(back_mixed[head, span])
            scores = split_two(jnp.where(causal, dot_split(query_mid, key_mid, NT), 0.0))
            back_scores = split_two(jnp.where(causal, dot_split(back, values, NT), 0.0))
            state = states[part, head]
            back_state = state_ref[head]
            back_state_split = split_two(back_state)
            back_values = dot_split(scores, back, TN) + dot_split(
                carried_split, back_state_split, NT
            )
            back_query = (
                dot_split(back_scores, key_mid) * grow
                + dot_split(back, split_two(state)) * since
            )
            back_carried = dot_split(values, back_state_split)
            back_keys = dot_split(back_scores, query_mid, TN) * shrink + back_carried * until
            decayed = back_state * jnp.exp(total)
            back_total = jnp.sum(back_carried * carried, axis=0, keepdims=True) + jnp.sum(
                decayed * state, axis=0, keepdims=True
            )
            state_ref[head] = decayed + dot_split(back, split_two(query * since), TN)
            back_decay = (
                dot_exact(upper, query * back_query - keys * back_keys) + back_total
            )
            back_logits = back_decay * sigmoid(-logits_in[head, span]) / GATE_SCALE
            bias_out[head] += jnp.sum(back_logits, axis=0, keepdims=True)
            rank_back += lax.dot_general(
                back_logits, decay_out[head], NT, precision=lax.Precision.HIGHEST,
                preferred_element_type=F32,
            )
            decay_grad_out[head] += dot_split(split_two(rank[span]), split_two(back_logits), TN)
            back_ref[head, span, :HK] = (back_query * HK ** (-0.5)).astype(BF16)
            back_ref[head, span, HK : 2 * HK] = back_keys.astype(BF16)
            back_ref[head, span, 2 * HK : 2 * HK + HV] = back_values.astype(BF16)
            back_ref[head, span, 2 * HK + HV :] = back_gate[head, span]
        grad_out[span, 2 * HK + 2 * HV :] = rank_back.astype(BF16)

    back_normed = dot(grad_out[:, 2 * HK + 2 * HV :], rank_weight[0])
    for head in range(heads):
        back_normed += dot(back_ref[head], weight[head])

        @pl.when(own[0] == head)
        def _():
            grad_out[:, : 2 * HK + 2 * HV] = back_ref[head]

    inputs = tokens[...].astype(F32)
    inverse = inverse_rms(inputs, NORM_EPS)
    unit = inputs * inverse
    weighted = back_normed * gain[...]
    input_out[...] = back_middle[...] + inverse * (
        weighted - unit * jnp.mean(weighted * unit, axis=-1, keepdims=True)
    )
    gain_out[...] += jnp.sum(back_normed * unit, axis=0, keepdims=True)


def shaped(shape, kind=F32):
    return jax.ShapeDtypeStruct(shape, kind)


def call(kernel, grid, in_specs, out_specs, out_shape, scratch, operands, prefetch, flops, moved):
    return pl.pallas_call(
        kernel,
        grid_spec=pltpu.PrefetchScalarGridSpec(
            num_scalar_prefetch=prefetch,
            grid=grid,
            in_specs=in_specs,
            out_specs=out_specs,
            scratch_shapes=scratch,
        ),
        out_shape=out_shape,
        compiler_params=pltpu.CompilerParams(
            vmem_limit_bytes=VMEM_LIMIT, dimension_semantics=("arbitrary",) * len(grid)
        ),
        cost_estimate=pl.CostEstimate(flops=flops, bytes_accessed=moved, transcendentals=0),
    )(*operands)


def from_behind(value, axis, steps):
    count = lax.axis_size(axis)
    first, last = (max(0, -steps), min(count, count - steps))
    return lax.ppermute(value, axis, [(source, source + steps) for source in range(first, last)])


def carry(local, decay, steps):
    incoming = jnp.zeros_like(local)
    for _ in range(lax.axis_size("ctx") - 1):
        incoming = from_behind(decay * incoming + local, "ctx", steps)
    return incoming


def gather_pack(pack):
    rows, share = pack.shape
    if share % 128 == 0:
        whole = lax.all_gather(pack, ("dp", "ctx", "tp"))
        whole = whole.reshape(-1, lax.axis_size("tp"), rows, share)
        return whole.transpose(1, 2, 0, 3).reshape(whole.shape[1], rows, -1)
    return lax.all_gather(
        lax.all_gather(pack, "tp"), ("dp", "ctx"), axis=2, tiled=True
    )


def total_over(value, axes):
    return lax.psum(value, axes)


def adamw(weight_now, grad_now, mean_now, square_now, rate_value, decay_value):
    mean_new = BETA_ONE * mean_now + (1.0 - BETA_ONE) * grad_now
    square_new = BETA_TWO * square_now + (1.0 - BETA_TWO) * grad_now * grad_now
    mean_hat = mean_new / (1.0 - BETA_ONE**STEP)
    square_hat = square_new / (1.0 - BETA_TWO**STEP)
    weight_new = weight_now - rate_value * (
        mean_hat / (jnp.sqrt(square_hat) + ADAM_EPS) + decay_value * weight_now
    )
    return (mean_new, square_new, weight_new)


def three_parts(value):
    high = lax.reduce_precision(value, 8, 7)
    rest = value - high
    middle = lax.reduce_precision(rest, 8, 7)
    low = lax.reduce_precision(rest - middle, 8, 7)
    return [part.astype(BF16) for part in (high, middle, low)]


def body(
    tokens,
    cotangent,
    lengths,
    query_key_weight,
    query_key_mean,
    query_key_square,
    value_gate_weight,
    value_gate_mean,
    value_gate_square,
    decay_in_weight,
    decay_in_mean,
    decay_in_square,
    decay_out_weight,
    decay_out_mean,
    decay_out_square,
    decay_bias,
    decay_bias_mean,
    decay_bias_square,
    output_weight,
    output_mean,
    output_square,
    gate_up_weight,
    gate_up_mean,
    gate_up_square,
    down_weight,
    down_mean,
    down_square,
    gains,
    gains_mean,
    gains_square,
):
    rows, width = tokens.shape
    heads = lax.axis_size("tp")
    ranks = decay_in_weight.shape[1]
    units = down_weight.shape[0]
    steps = rows // ROWS
    own = lax.axis_index("tp").astype(jnp.int32).reshape(1)
    gain_one = gains[:width].reshape(1, width)
    gain_two = gains[width : 2 * width].reshape(1, width)
    gain_head = gains[2 * width :].reshape(1, HV)

    mixer_pack = jnp.concatenate(
        [
            query_key_weight[0].T,
            query_key_weight[1].T,
            value_gate_weight[0].T,
            value_gate_weight[1].T,
            output_weight,
            decay_in_weight.T,
        ]
    ).astype(BF16)
    ffn_pack = jnp.concatenate(
        [gate_up_weight[0].T, gate_up_weight[1].T, down_weight]
    ).astype(BF16)
    small = jnp.concatenate([decay_out_weight, decay_bias.reshape(1, HK)])
    small_full = lax.all_gather(small, "tp")
    decay_out_full = small_full[:, :ranks]
    bias_full = small_full[:, ranks:]
    mixer = gather_pack(mixer_pack)
    ffn = gather_pack(ffn_pack)

    position = lax.axis_index("ctx") * rows + jnp.arange(rows, dtype=jnp.int32)
    back_ffn = jnp.where((position < lengths[0])[:, None], cotangent, jnp.zeros_like(cotangent))

    columns = 2 * HK + 2 * HV
    row_spec = pl.BlockSpec((ROWS, width), lambda i, *_: (i, 0))
    gain_spec = pl.BlockSpec((1, width), lambda i, *_: (0, 0))
    head_gain_spec = pl.BlockSpec((1, HV), lambda i, *_: (0, 0))
    weight_spec = pl.BlockSpec(
        (heads, columns, width), lambda i, *_: (0, 0, 0), pipeline_mode=pl.Buffered(1)
    )
    rank_weight_spec = pl.BlockSpec(
        (1, ranks, width), lambda i, *_: (0, (columns + HV) // ranks, 0)
    )
    out_weight_spec = pl.BlockSpec(
        (heads, HV, width), lambda i, *_: (0, columns // HV, 0), pipeline_mode=pl.Buffered(1)
    )
    decay_out_spec = pl.BlockSpec((heads, ranks, HK), lambda i, *_: (0, 0, 0))
    bias_spec = pl.BlockSpec((heads, 1, HK), lambda i, *_: (0, 0, 0))
    state_spec = pl.BlockSpec((heads, HV, HK), lambda i, *_: (0, 0, 0))

    def by_head(size, reverse=False):
        if reverse:
            return pl.BlockSpec((heads, ROWS, size), lambda i, *_: (0, steps - 1 - i, 0))
        return pl.BlockSpec((heads, ROWS, size), lambda i, *_: (0, i, 0))

    parts = ROWS // BLOCK
    normed, qkv, out_gate, rank, logits, cum, local_state, local_total = call(
        project_kernel,
        (steps,),
        [row_spec, gain_spec, weight_spec, rank_weight_spec, decay_out_spec, bias_spec],
        [
            row_spec,
            by_head(2 * HK + HV),
            by_head(HV),
            pl.BlockSpec((ROWS, ranks), lambda i, *_: (i, 0)),
            by_head(HK),
            by_head(HK),
            state_spec,
            bias_spec,
        ],
        [
            shaped((rows, width), BF16),
            shaped((heads, rows, 2 * HK + HV)),
            shaped((heads, rows, HV)),
            shaped((rows, ranks)),
            shaped((heads, rows, HK)),
            shaped((heads, rows, HK)),
            shaped((heads, HV, HK)),
            shaped((heads, 1, HK)),
        ],
        [],
        (tokens, gain_one, mixer, mixer, decay_out_full, bias_full),
        0,
        2 * rows * width * columns * heads,
        rows * heads * 4 * 1024,
    )
    device_decay = jnp.exp(local_total)
    start_state = carry(local_state, device_decay, 1)

    mixed, states, gated_own, middle, normed_two = call(
        mix_kernel,
        (steps,),
        [
            row_spec,
            by_head(2 * HK + HV),
            by_head(HV),
            by_head(HK),
            state_spec,
            out_weight_spec,
            head_gain_spec,
            gain_spec,
        ],
        [
            by_head(HV),
            pl.BlockSpec((parts, heads, HV, HK), lambda i, *_: (i, 0, 0, 0)),
            pl.BlockSpec((ROWS, HV), lambda i, *_: (i, 0)),
            row_spec,
            row_spec,
        ],
        [
            shaped((heads, rows, HV)),
            shaped((steps * parts, heads, HV, HK)),
            shaped((rows, HV), BF16),
            shaped((rows, width)),
            shaped((rows, width), BF16),
        ],
        [pltpu.VMEM((heads, HV, HK), F32), pltpu.VMEM((ROWS, heads * HV), BF16)],
        (own, tokens, qkv, out_gate, cum, start_state, mixer, gain_head, gain_two),
        1,
        2 * rows * width * HV * heads * 3,
        rows * heads * 4 * 1024,
    )

    wide_spec = pl.BlockSpec((FFN_ROWS, width), lambda i, j, *_: (i, 0))
    own_spec = pl.BlockSpec((FFN_ROWS, units), lambda i, j, *_: (i, 0))
    wide_gain_spec = pl.BlockSpec((1, width), lambda i, j, *_: (0, 0))
    active, back_gate, back_up, layer_out, back_middle, back_attn, gain_two_part = call(
        ffn_kernel,
        (rows // FFN_ROWS, heads),
        [
            wide_spec,
            wide_spec,
            wide_spec,
            pl.BlockSpec((1, 3 * units, width), lambda i, j, *_: (j, 0, 0)),
            wide_gain_spec,
        ],
        [own_spec, own_spec, own_spec, wide_spec, wide_spec, wide_spec, wide_gain_spec],
        [
            shaped((rows, units), BF16),
            shaped((rows, units), BF16),
            shaped((rows, units), BF16),
            shaped((rows, width), BF16),
            shaped((rows, width)),
            shaped((rows, width), BF16),
            shaped((1, width)),
        ],
        [pltpu.VMEM((FFN_ROWS, width), F32), pltpu.VMEM((FFN_ROWS, width), F32)],
        (own, normed_two, back_ffn, middle, ffn, gain_two),
        1,
        12 * rows * width * units * heads,
        rows * width * 24,
    )
    ffn_grad = jnp.concatenate(
        [
            dot(back_gate, normed_two, TN),
            dot(back_up, normed_two, TN),
            dot(active, back_ffn, TN),
        ]
    )
    ffn_share = lax.psum_scatter(ffn_grad, ("dp", "ctx"), scatter_dimension=1, tiled=True)
    output_grad = dot(gated_own, back_attn, TN)
    output_share = lax.psum_scatter(output_grad, ("dp", "ctx"), scatter_dimension=1, tiled=True)

    back_row_spec = pl.BlockSpec((ROWS, width), lambda i, *_: (steps - 1 - i, 0))
    back_mixed, back_out_gate, head_gain_part, collected = call(
        gate_back_kernel,
        (steps,),
        [
            back_row_spec,
            out_weight_spec,
            by_head(HV, True),
            by_head(HV, True),
            by_head(HK, True),
            by_head(HK, True),
            head_gain_spec,
        ],
        [by_head(HV, True), by_head(HV, True), head_gain_spec, state_spec],
        [
            shaped((heads, rows, HV)),
            shaped((heads, rows, HV), BF16),
            shaped((1, HV)),
            shaped((heads, HV, HK)),
        ],
        [],
        (back_attn, mixer, mixed, out_gate, qkv, cum, gain_head),
        0,
        2 * rows * width * HV * heads,
        rows * heads * 4 * 1024,
    )
    back_end = carry(collected, device_decay, -1)

    grad_columns = columns + ranks
    mixer_back, input_grad, decay_out_grad, bias_grad, gain_one_part = call(
        mix_back_kernel,
        (steps,),
        [
            back_row_spec,
            back_row_spec,
            by_head(2 * HK + HV, True),
            by_head(HK, True),
            by_head(HK, True),
            pl.BlockSpec((parts, heads, HV, HK), lambda i, *_: (steps - 1 - i, 0, 0, 0)),
            by_head(HV, True),
            by_head(HV, True),
            state_spec,
            weight_spec,
            rank_weight_spec,
            decay_out_spec,
            pl.BlockSpec((ROWS, ranks), lambda i, *_: (steps - 1 - i, 0)),
            gain_spec,
        ],
        [
            pl.BlockSpec((ROWS, grad_columns), lambda i, *_: (steps - 1 - i, 0)),
            back_row_spec,
            decay_out_spec,
            bias_spec,
            gain_spec,
        ],
        [
            shaped((rows, grad_columns), BF16),
            shaped((rows, width)),
            shaped((heads, ranks, HK)),
            shaped((heads, 1, HK)),
            shaped((1, width)),
        ],
        [pltpu.VMEM((heads, HV, HK), F32), pltpu.VMEM((heads, ROWS, columns), BF16)],
        (
            own, tokens, back_middle, qkv, cum, logits, states, back_mixed, back_out_gate, back_end,
            mixer, mixer, decay_out_full, rank, gain_one,
        ),
        1,
        2 * rows * width * columns * heads * 2,
        rows * heads * 4 * 2048,
    )
    mixer_grad = dot(mixer_back, normed, TN)
    mixer_share = lax.psum_scatter(mixer_grad, ("dp", "ctx"), scatter_dimension=1, tiled=True)
    decay_out_own = lax.dynamic_index_in_dim(decay_out_grad, own[0], 0, keepdims=False)
    bias_own = lax.dynamic_index_in_dim(bias_grad, own[0], 0, keepdims=False)
    sums = jnp.concatenate(
        [
            gain_one_part.reshape(-1),
            gain_two_part.reshape(-1),
            head_gain_part.reshape(-1),
            bias_own.reshape(-1),
            decay_out_own.reshape(-1),
        ]
    )
    sums = total_over(sums, ("dp", "ctx"))
    gain_count = gains.shape[0]
    gains_grad = sums[:gain_count]
    bias_total = sums[gain_count : gain_count + HK]
    decay_out_total = sums[gain_count + HK :].reshape(ranks, HK)

    query_key_share = jnp.stack([mixer_share[:HK].T, mixer_share[HK : 2 * HK].T])
    value_gate_share = jnp.stack(
        [mixer_share[2 * HK : 2 * HK + HV].T, mixer_share[2 * HK + HV : columns].T]
    )
    decay_in_share = mixer_share[columns:].T
    gate_up_share = jnp.stack([ffn_share[:units].T, ffn_share[units : 2 * units].T])
    down_share = ffn_share[2 * units :]

    updated = adamw(
        query_key_weight,
        query_key_share,
        query_key_mean,
        query_key_square,
        RATE_MATRIX,
        WEIGHT_DECAY,
    )
    updated = updated + adamw(
        value_gate_weight,
        value_gate_share,
        value_gate_mean,
        value_gate_square,
        RATE_MATRIX,
        WEIGHT_DECAY,
    )
    updated = updated + adamw(
        decay_in_weight, decay_in_share, decay_in_mean, decay_in_square, RATE_MATRIX, WEIGHT_DECAY
    )
    updated = updated + adamw(
        decay_out_weight, decay_out_total, decay_out_mean, decay_out_square, RATE_RANK, WEIGHT_DECAY
    )
    updated = updated + adamw(
        decay_bias, bias_total, decay_bias_mean, decay_bias_square, RATE_BIAS, 0.0
    )
    updated = updated + adamw(
        output_weight, output_share, output_mean, output_square, RATE_MATRIX, WEIGHT_DECAY
    )
    updated = updated + adamw(
        gate_up_weight, gate_up_share, gate_up_mean, gate_up_square, RATE_MATRIX, WEIGHT_DECAY
    )
    updated = updated + adamw(
        down_weight, down_share, down_mean, down_square, RATE_MATRIX, WEIGHT_DECAY
    )
    updated = updated + adamw(gains, gains_grad, gains_mean, gains_square, RATE_GAIN, 0.0)
    return (layer_out, input_grad) + updated


def solution(mesh):
    tokens_at = P(("dp", "ctx"), None)
    split_at = P(None, ("dp", "ctx"), "tp")
    deep_at = P("tp", ("dp", "ctx"))
    rank_out_at = P(None, "tp")
    kinds = (split_at, split_at, tokens_at, rank_out_at, P("tp"), deep_at, split_at, deep_at, P())
    params = tuple(kind for kind in kinds for _ in range(3))
    return jax.shard_map(
        body,
        mesh=mesh,
        in_specs=(tokens_at, tokens_at, P("dp")) + params,
        out_specs=(tokens_at, tokens_at) + params,
        check_vma=False,
    )
```

```python
import functools

import jax
import jax.numpy as jnp
from jax import lax
from jax.experimental import pallas as pl
from jax.experimental.pallas import tpu as pltpu
from jax.sharding import PartitionSpec as P

HK = 128
HV = 256
BLOCK = 128
LANES = 128
GROUPS = 8
MID = 63
DECAY_ROWS = 32
ROWS = 256
FFN_ROWS = 512
FFN_PARTS = 2
STEP = 10

NORM_EPS = 1e-06
HEAD_EPS = 1e-05
GATE_SCALE = 16.0
BETA_ONE = 0.9
BETA_TWO = 0.95
ADAM_EPS = 1e-08
WEIGHT_DECAY = 0.1
RATE_MATRIX = 0.03
RATE_RANK = 0.1
RATE_BIAS = 1.5
RATE_GAIN = 0.3
VMEM_LIMIT = 60 * 1024 * 1024

F32 = jnp.float32
BF16 = jnp.bfloat16
NN = (((1,), (0,)), ((), ()))
NT = (((1,), (1,)), ((), ()))
TN = (((0,), (0,)), ((), ()))


def dot(left, right, dims=NN):
    return lax.dot_general(left, right, dims, preferred_element_type=F32)


def split_two(values):
    high = values.astype(BF16)
    return high, (values - high.astype(F32)).astype(BF16)


def dot_split(left, right, dims=NN):
    axis = 1 - dims[0][0][0]
    size = left[0].shape[axis]
    both = dot(jnp.concatenate(left, axis=axis), right[0], dims)
    return both[:size] + both[size:] + dot(left[0], right[1], dims)


def dot_exact(matrix, values):
    high = values.astype(BF16)
    rest = values - high.astype(F32)
    middle = rest.astype(BF16)
    low = (rest - middle.astype(F32)).astype(BF16)
    return dot(matrix, high) + dot(matrix, middle) + dot(matrix, low)


def lower_mask():
    rows = lax.broadcasted_iota(jnp.int32, (BLOCK, BLOCK), 0)
    columns = lax.broadcasted_iota(jnp.int32, (BLOCK, BLOCK), 1)
    return rows >= columns


def upper_mask():
    rows = lax.broadcasted_iota(jnp.int32, (BLOCK, BLOCK), 0)
    columns = lax.broadcasted_iota(jnp.int32, (BLOCK, BLOCK), 1)
    return rows <= columns


def as_ones(mask):
    return jnp.where(mask, 1.0, 0.0).astype(BF16)


def inverse_rms(values, epsilon):
    return lax.rsqrt(jnp.mean(values * values, axis=-1, keepdims=True) + epsilon)


def sigmoid(values):
    return 0.5 + 0.5 * jnp.tanh(0.5 * values)


def fill(info, first, second, pieces):
    heads = first.shape[1]
    for head in range(heads):
        slot = info[2 * GROUPS + head]
        for group in range(GROUPS):
            lanes = slice(group * LANES, (group + 1) * LANES)
            place = info[GROUPS + group]
            for source_index, source in enumerate((first, second)):

                @pl.when(info[group] == source_index)
                def _():
                    for target, start, count in pieces:
                        if target.shape[0] == count and head > 0:
                            continue
                        at = head * count
                        target[at : at + count, lanes] = source[
                            place, slot, start : start + count
                        ]


def project_kernel(
    info, tokens, gain, first, second, decay_out,
    normed_out, kv_out, rank_out, logits_out, cum_out, state_out, total_out, weight, rank_weight,
):
    heads = first.shape[1]
    size = HK + HV
    ranks = rank_out.shape[1]

    @pl.when(pl.program_id(0) == 0)
    def _():
        state_out[...] = jnp.zeros_like(state_out)
        total_out[...] = jnp.zeros_like(total_out)
        fill(info, first, second, ((weight, 0, size), (rank_weight, size, ranks)))

    inputs = tokens[...].astype(F32)
    normed = (inputs * inverse_rms(inputs, NORM_EPS) * gain[...]).astype(BF16)
    normed_out[...] = normed
    rank = dot(normed, rank_weight[...], NT)
    rank_out[...] = rank
    lower = as_ones(lower_mask())
    made = dot(normed, weight[...], NT)
    for head in range(heads):
        slot = info[2 * GROUPS + head]
        keys = made[:, head * size : head * size + HK]
        values = made[:, head * size + HK : (head + 1) * size]
        kv_out[head, :, :HK] = keys
        kv_out[head, :, HK:] = values
        logits = (
            lax.dot_general(
                rank, decay_out[slot, :ranks], NN, precision=lax.Precision.HIGHEST,
                preferred_element_type=F32,
            )
            + decay_out[slot, ranks : ranks + 1]
        )
        logits_out[head] = logits
        log_decay = (
            jnp.minimum(logits, 0.0) - jnp.log1p(jnp.exp(-jnp.abs(logits)))
        ) / GATE_SCALE
        state = state_out[head]
        for part in range(ROWS // BLOCK):
            span = slice(part * BLOCK, (part + 1) * BLOCK)
            cum = dot_exact(lower, log_decay[span])
            cum_out[head, span] = cum
            total = cum[BLOCK - 1 :]
            carried = split_two(keys[span] * jnp.exp(total - cum))
            state = state * jnp.exp(total) + dot_split(split_two(values[span]), carried, TN)
            total_out[head] += total
        state_out[head] = state


def mix_kernel(
    info, tokens, normed, kv, cum_in, start, first, second, head_gain, gain,
    query_out, gate_out, mixed_out, state_out, gated_out, middle_out, normed_out, weight, out_weight,
    state_ref, gated_ref,
):
    heads = start.shape[0]
    size = HK + HV

    @pl.when(pl.program_id(0) == 0)
    def _():
        state_ref[...] = start[...]
        fill(info, first, second, ((weight, 0, size), (out_weight, size, HV)))

    made = dot(normed[...], weight[...], NT)
    causal = lower_mask()
    for part in range(ROWS // BLOCK):
        span = slice(part * BLOCK, (part + 1) * BLOCK)
        for head in range(heads):
            query = made[span, head * size : head * size + HK] * HK ** (-0.5)
            out_gate = made[span, head * size + HK : (head + 1) * size]
            query_out[head, span] = query
            gate_out[head, span] = out_gate
            keys = kv[head, span, :HK]
            values = split_two(kv[head, span, HK:])
            cum = cum_in[head, span]
            center = cum[MID : MID + 1]
            total = cum[BLOCK - 1 :]
            query_mid = split_two(query * jnp.exp(cum - center))
            key_mid = split_two(keys * jnp.exp(center - cum))
            scores = split_two(jnp.where(causal, dot_split(query_mid, key_mid, NT), 0.0))
            state = state_ref[head]
            state_out[part, head] = state
            mixed = dot_split(scores, values) + dot_split(
                split_two(query * jnp.exp(cum)), split_two(state), NT
            )
            carried = split_two(keys * jnp.exp(total - cum))
            state_ref[head] = state * jnp.exp(total) + dot_split(values, carried, TN)
            mixed_out[head, span] = mixed
            gated = (
                mixed * inverse_rms(mixed, HEAD_EPS) * head_gain[...] * (out_gate * sigmoid(out_gate))
            ).astype(BF16)
            gated_ref[span, head * HV : (head + 1) * HV] = gated

            @pl.when(info[2 * GROUPS + heads] == head)
            def _():
                gated_out[span] = gated

    middle = tokens[...].astype(F32) + dot(gated_ref[...], out_weight[...])
    middle_out[...] = middle
    normed_out[...] = (middle * inverse_rms(middle, NORM_EPS) * gain[...]).astype(BF16)


def ffn_kernel(
    weight_pieces, info, normed, back, middle, weight, gain,
    active_out, back_gate_out, back_up_out, layer_out, back_middle_out, back_attn_out, gain_out,
    ffn_ref, back_ref,
):
    step, piece = pl.program_id(0), pl.program_id(1)
    units = weight.shape[2] // 3

    @pl.when((step == 0) & (piece == 0))
    def _():
        ffn_ref[...] = jnp.zeros_like(ffn_ref)
        back_ref[...] = jnp.zeros_like(back_ref)
        gain_out[...] = jnp.zeros_like(gain_out)

    def rows_of(start):
        return jnp.concatenate(
            [weight[group, 0, start : start + units] for group in range(GROUPS)], axis=1
        )

    gate_weight, up_weight, down_weight = rows_of(0), rows_of(units), rows_of(2 * units)
    count = normed.shape[0] // FFN_PARTS
    spans = [slice(part * count, (part + 1) * count) for part in range(FFN_PARTS)]
    made = [
        (
            dot(normed[span], gate_weight, NT),
            dot(normed[span], up_weight, NT),
            dot(back[span], down_weight, NT),
        )
        for span in spans
    ]
    for span, (gate_values, upward, back_active) in zip(spans, made):
        share = sigmoid(gate_values)
        silu = gate_values * share
        active = (silu * upward).astype(BF16)
        back_gate = (
            back_active * upward * (share * (1.0 + gate_values * (1.0 - share)))
        ).astype(BF16)
        back_up = (back_active * silu).astype(BF16)
        ffn = dot(active, down_weight)
        back_normed = dot(back_gate, gate_weight) + dot(back_up, up_weight)
        keep = jnp.where(piece > 0, 1.0, 0.0)
        ffn_ref[span] = ffn_ref[span] * keep + ffn
        back_ref[span] = back_ref[span] * keep + back_normed

        @pl.when(piece == info[2 * GROUPS + weight_pieces])
        def _():
            active_out[span] = active
            back_gate_out[span] = back_gate
            back_up_out[span] = back_up

    @pl.when(piece == pl.num_programs(1) - 1)
    def _():
        mid = middle[...]
        layer_out[...] = (mid + ffn_ref[...]).astype(BF16)
        inverse = inverse_rms(mid, NORM_EPS)
        unit = mid * inverse
        total = back_ref[...]
        weighted = total * gain[...]
        back_middle = back[...].astype(F32) + inverse * (
            weighted - unit * jnp.mean(weighted * unit, axis=-1, keepdims=True)
        )
        back_middle_out[...] = back_middle
        back_attn_out[...] = back_middle.astype(BF16)
        gain_out[...] += jnp.sum(total * unit, axis=0, keepdims=True)


def gate_back_kernel(
    back_attn, out_weight, mixed_in, gate, query_in, cum_in, head_gain,
    back_mixed_out, back_gate_out, gain_out, state_out,
):
    heads = gate.shape[0]

    @pl.when(pl.program_id(0) == 0)
    def _():
        gain_out[...] = jnp.zeros_like(gain_out)
        state_out[...] = jnp.zeros_like(state_out)

    for head in range(heads):
        back_gated = dot(back_attn[...], out_weight[head * HV : (head + 1) * HV], NT)
        mixed = mixed_in[head]
        out_gate = gate[head]
        inverse = inverse_rms(mixed, HEAD_EPS)
        unit = mixed * inverse
        share = sigmoid(out_gate)
        silu = out_gate * share
        slope = share * (1.0 + out_gate * (1.0 - share))
        back_gate_out[head] = (back_gated * unit * head_gain[...] * slope).astype(BF16)
        gain_out[...] += jnp.sum(back_gated * unit * silu, axis=0, keepdims=True)
        weighted = back_gated * head_gain[...] * silu
        back_mixed = inverse * (
            weighted - unit * jnp.mean(weighted * unit, axis=-1, keepdims=True)
        )
        back_mixed_out[head] = back_mixed
        state = state_out[head]
        for part in reversed(range(ROWS // BLOCK)):
            span = slice(part * BLOCK, (part + 1) * BLOCK)
            cum = cum_in[head, span]
            scaled = split_two(query_in[head, span] * jnp.exp(cum))
            state = state * jnp.exp(cum[BLOCK - 1 :]) + dot_split(
                split_two(back_mixed[span]), scaled, TN
            )
        state_out[head] = state


def mix_back_kernel(
    info, tokens, back_middle, query_in, kv, cum_in, logits_in, states, back_mixed, back_gate,
    back_end, query_weight, key_weight, rank_weight, decay_out, rank, gain,
    grad_out, input_out, decay_grad_out, bias_out, gain_out,
    state_ref, query_ref, key_ref,
):
    heads = back_end.shape[0]
    size = HK + HV
    ranks = rank.shape[1]

    @pl.when(pl.program_id(0) == 0)
    def _():
        state_ref[...] = back_end[...]
        decay_grad_out[...] = jnp.zeros_like(decay_grad_out)
        bias_out[...] = jnp.zeros_like(bias_out)
        gain_out[...] = jnp.zeros_like(gain_out)

    causal = lower_mask()
    upper = as_ones(upper_mask())
    for part in reversed(range(ROWS // BLOCK)):
        span = slice(part * BLOCK, (part + 1) * BLOCK)
        rank_back = jnp.zeros((BLOCK, rank.shape[1]), F32)
        for head in range(heads):
            slot = info[2 * GROUPS + head]
            query = query_in[head, span]
            keys = kv[head, span, :HK]
            values = split_two(kv[head, span, HK:])
            cum = cum_in[head, span]
            center = cum[MID : MID + 1]
            total = cum[BLOCK - 1 :]
            grow, shrink = jnp.exp(cum - center), jnp.exp(center - cum)
            since, until = jnp.exp(cum), jnp.exp(total - cum)
            query_mid, key_mid = split_two(query * grow), split_two(keys * shrink)
            carried = keys * until
            carried_split = split_two(carried)
            back = split_two(back_mixed[head, span])
            scores = split_two(jnp.where(causal, dot_split(query_mid, key_mid, NT), 0.0))
            back_scores = split_two(jnp.where(causal, dot_split(back, values, NT), 0.0))
            state = states[part, head]
            back_state = state_ref[head]
            back_state_split = split_two(back_state)
            back_values = dot_split(scores, back, TN) + dot_split(
                carried_split, back_state_split, NT
            )
            back_query = (
                dot_split(back_scores, key_mid) * grow
                + dot_split(back, split_two(state)) * since
            )
            back_carried = dot_split(values, back_state_split)
            back_keys = dot_split(back_scores, query_mid, TN) * shrink + back_carried * until
            decayed = back_state * jnp.exp(total)
            back_total = jnp.sum(back_carried * carried, axis=0, keepdims=True) + jnp.sum(
                decayed * state, axis=0, keepdims=True
            )
            state_ref[head] = decayed + dot_split(back, split_two(query * since), TN)
            back_decay = (
                dot_exact(upper, query * back_query - keys * back_keys) + back_total
            )
            back_logits = back_decay * sigmoid(-logits_in[head, span]) / GATE_SCALE
            bias_out[head] += jnp.sum(back_logits, axis=0, keepdims=True)
            rank_back += lax.dot_general(
                back_logits, decay_out[slot, :ranks], NT, precision=lax.Precision.HIGHEST,
                preferred_element_type=F32,
            )
            decay_grad_out[head] += dot_split(split_two(rank[span]), split_two(back_logits), TN)
            at = head * size
            query_ref[span, at : at + HK] = (back_query * HK ** (-0.5)).astype(BF16)
            query_ref[span, at + HK : at + size] = back_gate[head, span]
            key_ref[span, at : at + HK] = back_keys.astype(BF16)
            key_ref[span, at + HK : at + size] = back_values.astype(BF16)
        grad_out[span, 2 * size :] = rank_back.astype(BF16)

    back_normed = (
        dot(grad_out[:, 2 * size :], rank_weight[...])
        + dot(query_ref[...], query_weight[...])
        + dot(key_ref[...], key_weight[...])
    )
    for head in range(heads):

        @pl.when(info[2 * GROUPS + heads] == head)
        def _():
            grad_out[:, :size] = query_ref[:, head * size : (head + 1) * size]
            grad_out[:, size : 2 * size] = key_ref[:, head * size : (head + 1) * size]

    inputs = tokens[...].astype(F32)
    inverse = inverse_rms(inputs, NORM_EPS)
    unit = inputs * inverse
    weighted = back_normed * gain[...]
    input_out[...] = back_middle[...] + inverse * (
        weighted - unit * jnp.mean(weighted * unit, axis=-1, keepdims=True)
    )
    gain_out[...] += jnp.sum(back_normed * unit, axis=0, keepdims=True)


def shaped(shape, kind=F32):
    return jax.ShapeDtypeStruct(shape, kind)


def call(kernel, grid, in_specs, out_specs, out_shape, scratch, operands, prefetch, flops, moved):
    return pl.pallas_call(
        kernel,
        grid_spec=pltpu.PrefetchScalarGridSpec(
            num_scalar_prefetch=prefetch,
            grid=grid,
            in_specs=in_specs,
            out_specs=out_specs,
            scratch_shapes=scratch,
        ),
        out_shape=out_shape,
        compiler_params=pltpu.CompilerParams(
            vmem_limit_bytes=VMEM_LIMIT, dimension_semantics=("arbitrary",) * len(grid)
        ),
        cost_estimate=pl.CostEstimate(flops=flops, bytes_accessed=moved, transcendentals=0),
    )(*operands)


def from_behind(value, axis, steps):
    count = lax.axis_size(axis)
    first, last = (max(0, -steps), min(count, count - steps))
    return lax.ppermute(value, axis, [(source, source + steps) for source in range(first, last)])


def carry(local, decay, steps):
    incoming = jnp.zeros_like(local)
    for _ in range(lax.axis_size("ctx") - 1):
        incoming = from_behind(decay * incoming + local, "ctx", steps)
    return incoming


def staged():
    return lax.axis_size("dp") == 4 and lax.axis_size("ctx") == 2


def swap(value, axis, distance):
    count = lax.axis_size(axis)
    return lax.ppermute(value, axis, [(source, source ^ distance) for source in range(count)])


def shift(value, axis, distance):
    count = lax.axis_size(axis)
    return lax.ppermute(
        value, axis, [(source, (source + distance) % count) for source in range(count)]
    )


def gather_plain(pack):
    rows = pack.shape[0]
    whole = lax.all_gather(lax.all_gather(pack, "tp"), ("dp", "ctx"), axis=2, tiled=True)
    return whole.reshape(whole.shape[0], rows, GROUPS, LANES).transpose(2, 0, 1, 3)


def gather_slots(pack):
    count = lax.axis_size("tp")
    line = jnp.stack([pack] + [shift(pack, "tp", distance) for distance in range(1, count)])
    across, beyond = swap(line, "dp", 1), swap(line, "dp", 2)
    half = count // 2
    far = jnp.concatenate([swap(across[:half], "dp", 2), swap(beyond[half:], "dp", 1)])
    first = jnp.stack([line, across, beyond, far])
    return first, swap(first, "ctx", 1)


def gather_pair(pack):
    if staged():
        return gather_slots(pack)
    whole = gather_plain(pack)
    half = GROUPS // 2
    return whole[:half], whole[half:]


def gather_info():
    count = lax.axis_size("tp")
    own = lax.axis_index("tp")
    group = jnp.arange(GROUPS, dtype=jnp.int32)
    heads = jnp.arange(count, dtype=jnp.int32)
    if staged():
        which = (group % 2) ^ lax.axis_index("ctx")
        place = (group // 2) ^ lax.axis_index("dp")
        slot = lax.rem(own - heads + count, count)
    else:
        which, place, slot = group // (GROUPS // 2), group % (GROUPS // 2), heads
    return jnp.concatenate([which, place, slot, own.reshape(1)]).astype(jnp.int32)


def gather_whole(pack):
    if staged():
        rows, share = pack.shape
        whole = lax.all_gather(pack, ("dp", "ctx", "tp"))
        return whole.reshape(-1, lax.axis_size("tp"), rows, share)
    return gather_plain(pack)


def scatter_rows(value):
    if not staged():
        return lax.psum_scatter(value, ("dp", "ctx"), scatter_dimension=0, tiled=True)
    device, core = lax.axis_index("dp"), lax.axis_index("ctx")
    row, column = device // 2, device % 2

    def pick(array, axis, index):
        return lax.dynamic_index_in_dim(array, index, axis, keepdims=False)

    columns = value.shape[1]
    value = value.reshape(2, 2, 2, -1, columns)
    value = pick(value, 2, core) + swap(pick(value, 2, 1 - core), "ctx", 1)
    half = value.shape[2] // 2
    upper, lower = value[:, :, :half], value[:, :, half:]
    upper = pick(upper, 1, column) + swap(pick(upper, 1, 1 - column), "dp", 1)
    lower = pick(lower, 0, row) + swap(pick(lower, 0, 1 - row), "dp", 2)
    upper = pick(upper, 0, row) + swap(pick(upper, 0, 1 - row), "dp", 2)
    lower = pick(lower, 0, column) + swap(pick(lower, 0, 1 - column), "dp", 1)
    return jnp.concatenate([upper, lower])


def total_over(value):
    if not staged():
        return lax.psum(value, ("dp", "ctx"))
    for axis, distance in (("ctx", 1), ("dp", 1), ("dp", 2)):
        value = value + swap(value, axis, distance)
    return value


def adamw(weight_now, grad_now, mean_now, square_now, rate_value, decay_value):
    mean_new = BETA_ONE * mean_now + (1.0 - BETA_ONE) * grad_now
    square_new = BETA_TWO * square_now + (1.0 - BETA_TWO) * grad_now * grad_now
    mean_hat = mean_new / (1.0 - BETA_ONE**STEP)
    square_hat = square_new / (1.0 - BETA_TWO**STEP)
    weight_new = weight_now - rate_value * (
        mean_hat / (jnp.sqrt(square_hat) + ADAM_EPS) + decay_value * weight_now
    )
    return (mean_new, square_new, weight_new)


def three_parts(value):
    high = lax.reduce_precision(value, 8, 7)
    rest = value - high
    middle = lax.reduce_precision(rest, 8, 7)
    low = lax.reduce_precision(rest - middle, 8, 7)
    return [part.astype(BF16) for part in (high, middle, low)]


def body(
    tokens,
    cotangent,
    lengths,
    query_key_weight,
    query_key_mean,
    query_key_square,
    value_gate_weight,
    value_gate_mean,
    value_gate_square,
    decay_in_weight,
    decay_in_mean,
    decay_in_square,
    decay_out_weight,
    decay_out_mean,
    decay_out_square,
    decay_bias,
    decay_bias_mean,
    decay_bias_square,
    output_weight,
    output_mean,
    output_square,
    gate_up_weight,
    gate_up_mean,
    gate_up_square,
    down_weight,
    down_mean,
    down_square,
    gains,
    gains_mean,
    gains_square,
):
    rows, width = tokens.shape
    heads = lax.axis_size("tp")
    ranks = decay_in_weight.shape[1]
    units = down_weight.shape[0]
    steps = rows // ROWS
    info = gather_info()
    gain_one = gains[:width].reshape(1, width)
    gain_two = gains[width : 2 * width].reshape(1, width)
    gain_head = gains[2 * width :].reshape(1, HV)
    size = HK + HV

    small = jnp.concatenate(
        [
            decay_out_weight,
            decay_bias.reshape(1, HK),
            jnp.zeros((DECAY_ROWS - ranks - 1, HK), F32),
        ]
    )
    key_parts = [
        query_key_weight[1].T.astype(BF16),
        value_gate_weight[0].T.astype(BF16),
        decay_in_weight.T.astype(BF16),
    ]
    if staged():
        key_first, key_second = gather_pair(jnp.concatenate(key_parts + three_parts(small)))
        sent = key_first[0, :, size + ranks :].astype(F32).reshape(heads, 3, DECAY_ROWS, HK)
        decay_out_full = sent[:, 0] + sent[:, 1] + sent[:, 2]
    else:
        key_first, key_second = gather_pair(jnp.concatenate(key_parts))
        decay_out_full = lax.all_gather(small, "tp")
    query_first, query_second = gather_pair(
        jnp.concatenate(
            [query_key_weight[0].T, value_gate_weight[1].T, output_weight]
        ).astype(BF16)
    )
    ffn = gather_whole(
        jnp.concatenate([gate_up_weight[0].T, gate_up_weight[1].T, down_weight]).astype(BF16)
    )

    position = lax.axis_index("ctx") * rows + jnp.arange(rows, dtype=jnp.int32)
    back_ffn = jnp.where((position < lengths[0])[:, None], cotangent, jnp.zeros_like(cotangent))

    columns = 2 * size
    row_spec = pl.BlockSpec((ROWS, width), lambda i, *_: (i, 0))
    gain_spec = pl.BlockSpec((1, width), lambda i, *_: (0, 0))
    head_gain_spec = pl.BlockSpec((1, HV), lambda i, *_: (0, 0))
    state_spec = pl.BlockSpec((heads, HV, HK), lambda i, *_: (0, 0, 0))
    bias_spec = pl.BlockSpec((heads, 1, HK), lambda i, *_: (0, 0, 0))

    def fixed(array):
        return pl.BlockSpec(
            array.shape, lambda i, *_: (0,) * len(array.shape), pipeline_mode=pl.Buffered(1)
        )

    def by_head(length, reverse=False):
        if reverse:
            return pl.BlockSpec((heads, ROWS, length), lambda i, *_: (0, steps - 1 - i, 0))
        return pl.BlockSpec((heads, ROWS, length), lambda i, *_: (0, i, 0))

    weight_shape = shaped((heads * size, width), BF16)
    rank_shape = shaped((ranks, width), BF16)
    out_weight_shape = shaped((heads * HV, width), BF16)
    parts = ROWS // BLOCK
    normed, kv, rank, logits, cum, local_state, local_total, key_weight, rank_weight = call(
        project_kernel,
        (steps,),
        [row_spec, gain_spec, fixed(key_first), fixed(key_second), fixed(decay_out_full)],
        [
            row_spec,
            by_head(size),
            pl.BlockSpec((ROWS, ranks), lambda i, *_: (i, 0)),
            by_head(HK),
            by_head(HK),
            state_spec,
            bias_spec,
            fixed(weight_shape),
            fixed(rank_shape),
        ],
        [
            shaped((rows, width), BF16),
            shaped((heads, rows, size)),
            shaped((rows, ranks)),
            shaped((heads, rows, HK)),
            shaped((heads, rows, HK)),
            shaped((heads, HV, HK)),
            shaped((heads, 1, HK)),
            weight_shape,
            rank_shape,
        ],
        [],
        (info, tokens, gain_one, key_first, key_second, decay_out_full),
        1,
        2 * rows * width * size * heads,
        rows * heads * 4 * 1024,
    )
    device_decay = jnp.exp(local_total)
    start_state = carry(local_state, device_decay, 1)

    query, out_gate, mixed, states, gated_own, middle, normed_two, query_weight, out_weight = call(
        mix_kernel,
        (steps,),
        [
            row_spec,
            row_spec,
            by_head(size),
            by_head(HK),
            state_spec,
            fixed(query_first),
            fixed(query_second),
            head_gain_spec,
            gain_spec,
        ],
        [
            by_head(HK),
            by_head(HV),
            by_head(HV),
            pl.BlockSpec((parts, heads, HV, HK), lambda i, *_: (i, 0, 0, 0)),
            pl.BlockSpec((ROWS, HV), lambda i, *_: (i, 0)),
            row_spec,
            row_spec,
            fixed(weight_shape),
            fixed(out_weight_shape),
        ],
        [
            shaped((heads, rows, HK)),
            shaped((heads, rows, HV)),
            shaped((heads, rows, HV)),
            shaped((steps * parts, heads, HV, HK)),
            shaped((rows, HV), BF16),
            shaped((rows, width)),
            shaped((rows, width), BF16),
            weight_shape,
            out_weight_shape,
        ],
        [pltpu.VMEM((heads, HV, HK), F32), pltpu.VMEM((ROWS, heads * HV), BF16)],
        (
            info, tokens, normed, kv, cum, start_state, query_first, query_second,
            gain_head, gain_two,
        ),
        1,
        2 * rows * width * (size + 2 * HV) * heads,
        rows * heads * 4 * 1024,
    )

    wide_spec = pl.BlockSpec((FFN_ROWS, width), lambda i, j, *_: (i, 0))
    own_spec = pl.BlockSpec((FFN_ROWS, units), lambda i, j, *_: (i, 0))
    wide_gain_spec = pl.BlockSpec((1, width), lambda i, j, *_: (0, 0))
    active, back_gate, back_up, layer_out, back_middle, back_attn, gain_two_part = call(
        functools.partial(ffn_kernel, heads),
        (rows // FFN_ROWS, heads),
        [
            wide_spec,
            wide_spec,
            wide_spec,
            pl.BlockSpec((GROUPS, 1, 3 * units, LANES), lambda i, j, *_: (0, j, 0, 0)),
            wide_gain_spec,
        ],
        [own_spec, own_spec, own_spec, wide_spec, wide_spec, wide_spec, wide_gain_spec],
        [
            shaped((rows, units), BF16),
            shaped((rows, units), BF16),
            shaped((rows, units), BF16),
            shaped((rows, width), BF16),
            shaped((rows, width)),
            shaped((rows, width), BF16),
            shaped((1, width)),
        ],
        [pltpu.VMEM((FFN_ROWS, width), F32), pltpu.VMEM((FFN_ROWS, width), F32)],
        (info, normed_two, back_ffn, middle, ffn, gain_two),
        1,
        12 * rows * width * units * heads,
        rows * width * 24,
    )
    early_grad = jnp.concatenate(
        [
            dot(back_gate, normed_two, TN),
            dot(back_up, normed_two, TN),
            dot(active, back_ffn, TN),
            dot(gated_own, back_attn, TN),
        ]
    )
    early_grad, back_attn = lax.optimization_barrier((early_grad, back_attn))
    early_share = lax.psum_scatter(early_grad, ("dp", "ctx"), scatter_dimension=1, tiled=True)

    back_row_spec = pl.BlockSpec((ROWS, width), lambda i, *_: (steps - 1 - i, 0))
    back_mixed, back_out_gate, head_gain_part, collected = call(
        gate_back_kernel,
        (steps,),
        [
            back_row_spec,
            fixed(out_weight),
            by_head(HV, True),
            by_head(HV, True),
            by_head(HK, True),
            by_head(HK, True),
            head_gain_spec,
        ],
        [by_head(HV, True), by_head(HV, True), head_gain_spec, state_spec],
        [
            shaped((heads, rows, HV)),
            shaped((heads, rows, HV), BF16),
            shaped((1, HV)),
            shaped((heads, HV, HK)),
        ],
        [],
        (back_attn, out_weight, mixed, out_gate, query, cum, gain_head),
        0,
        2 * rows * width * HV * heads,
        rows * heads * 4 * 1024,
    )
    back_end = carry(collected, device_decay, -1)

    grad_columns = columns + ranks
    mixer_back, input_grad, decay_out_grad, bias_grad, gain_one_part = call(
        mix_back_kernel,
        (steps,),
        [
            back_row_spec,
            back_row_spec,
            by_head(HK, True),
            by_head(size, True),
            by_head(HK, True),
            by_head(HK, True),
            pl.BlockSpec((parts, heads, HV, HK), lambda i, *_: (steps - 1 - i, 0, 0, 0)),
            by_head(HV, True),
            by_head(HV, True),
            state_spec,
            fixed(query_weight),
            fixed(key_weight),
            fixed(rank_weight),
            fixed(decay_out_full),
            pl.BlockSpec((ROWS, ranks), lambda i, *_: (steps - 1 - i, 0)),
            gain_spec,
        ],
        [
            pl.BlockSpec((ROWS, grad_columns), lambda i, *_: (steps - 1 - i, 0)),
            back_row_spec,
            pl.BlockSpec((heads, ranks, HK), lambda i, *_: (0, 0, 0)),
            bias_spec,
            gain_spec,
        ],
        [
            shaped((rows, grad_columns), BF16),
            shaped((rows, width)),
            shaped((heads, ranks, HK)),
            shaped((heads, 1, HK)),
            shaped((1, width)),
        ],
        [
            pltpu.VMEM((heads, HV, HK), F32),
            pltpu.VMEM((ROWS, heads * size), BF16),
            pltpu.VMEM((ROWS, heads * size), BF16),
        ],
        (
            info, tokens, back_middle, query, kv, cum, logits, states, back_mixed, back_out_gate,
            back_end, query_weight, key_weight, rank_weight, decay_out_full, rank, gain_one,
        ),
        1,
        2 * rows * width * columns * heads * 2,
        rows * heads * 4 * 2048,
    )
    own = info[-1]
    decay_out_own = lax.dynamic_index_in_dim(decay_out_grad, own, 0, keepdims=False)
    bias_own = lax.dynamic_index_in_dim(bias_grad, own, 0, keepdims=False)
    sums = jnp.concatenate(
        [
            gain_one_part.reshape(-1),
            gain_two_part.reshape(-1),
            head_gain_part.reshape(-1),
            bias_own.reshape(-1),
            decay_out_own.reshape(-1),
        ]
    )
    sums = total_over(sums)
    mixer_share = scatter_rows(dot(normed, mixer_back, TN))
    gain_count = gains.shape[0]
    gains_grad = sums[:gain_count]
    bias_total = sums[gain_count : gain_count + HK]
    decay_out_total = sums[gain_count + HK :].reshape(ranks, HK)

    query_key_share = jnp.stack([mixer_share[:, :HK], mixer_share[:, size : size + HK]])
    value_gate_share = jnp.stack([mixer_share[:, size + HK : columns], mixer_share[:, HK:size]])
    decay_in_share = mixer_share[:, columns:]
    gate_up_share = jnp.stack([early_share[:units].T, early_share[units : 2 * units].T])
    down_share = early_share[2 * units : 3 * units]
    output_share = early_share[3 * units :]

    updated = adamw(
        query_key_weight,
        query_key_share,
        query_key_mean,
        query_key_square,
        RATE_MATRIX,
        WEIGHT_DECAY,
    )
    updated = updated + adamw(
        value_gate_weight,
        value_gate_share,
        value_gate_mean,
        value_gate_square,
        RATE_MATRIX,
        WEIGHT_DECAY,
    )
    updated = updated + adamw(
        decay_in_weight, decay_in_share, decay_in_mean, decay_in_square, RATE_MATRIX, WEIGHT_DECAY
    )
    updated = updated + adamw(
        decay_out_weight, decay_out_total, decay_out_mean, decay_out_square, RATE_RANK, WEIGHT_DECAY
    )
    updated = updated + adamw(
        decay_bias, bias_total, decay_bias_mean, decay_bias_square, RATE_BIAS, 0.0
    )
    updated = updated + adamw(
        output_weight, output_share, output_mean, output_square, RATE_MATRIX, WEIGHT_DECAY
    )
    updated = updated + adamw(
        gate_up_weight, gate_up_share, gate_up_mean, gate_up_square, RATE_MATRIX, WEIGHT_DECAY
    )
    updated = updated + adamw(
        down_weight, down_share, down_mean, down_square, RATE_MATRIX, WEIGHT_DECAY
    )
    updated = updated + adamw(gains, gains_grad, gains_mean, gains_square, RATE_GAIN, 0.0)
    return (layer_out, input_grad) + updated


def solution(mesh):
    tokens_at = P(("dp", "ctx"), None)
    split_at = P(None, ("dp", "ctx"), "tp")
    deep_at = P("tp", ("dp", "ctx"))
    rank_out_at = P(None, "tp")
    kinds = (split_at, split_at, tokens_at, rank_out_at, P("tp"), deep_at, split_at, deep_at, P())
    params = tuple(kind for kind in kinds for _ in range(3))
    return jax.shard_map(
        body,
        mesh=mesh,
        in_specs=(tokens_at, tokens_at, P("dp")) + params,
        out_specs=(tokens_at, tokens_at) + params,
        check_vma=False,
    )
```

```python
import functools

import jax
import jax.numpy as jnp
from jax import lax
from jax.experimental import pallas as pl
from jax.experimental.pallas import tpu as pltpu
from jax.sharding import PartitionSpec as P

HK = 128
HV = 256
BLOCK = 128
LANES = 128
GROUPS = 8
MID = 63
DECAY_ROWS = 32
ROWS = 256
FFN_ROWS = 512
FFN_PARTS = 2
STEP = 10

NORM_EPS = 1e-06
HEAD_EPS = 1e-05
GATE_SCALE = 16.0
BETA_ONE = 0.9
BETA_TWO = 0.95
ADAM_EPS = 1e-08
WEIGHT_DECAY = 0.1
RATE_MATRIX = 0.03
RATE_RANK = 0.1
RATE_BIAS = 1.5
RATE_GAIN = 0.3
VMEM_LIMIT = 60 * 1024 * 1024

F32 = jnp.float32
BF16 = jnp.bfloat16
NN = (((1,), (0,)), ((), ()))
NT = (((1,), (1,)), ((), ()))
TN = (((0,), (0,)), ((), ()))


def dot(left, right, dims=NN):
    return lax.dot_general(left, right, dims, preferred_element_type=F32)


def split_two(values):
    high = values.astype(BF16)
    return high, (values - high.astype(F32)).astype(BF16)


def dot_split(left, right, dims=NN):
    axis = 1 - dims[0][0][0]
    size = left[0].shape[axis]
    both = dot(jnp.concatenate(left, axis=axis), right[0], dims)
    return both[:size] + both[size:] + dot(left[0], right[1], dims)


def dot_exact(matrix, values):
    high = values.astype(BF16)
    rest = values - high.astype(F32)
    middle = rest.astype(BF16)
    low = (rest - middle.astype(F32)).astype(BF16)
    return dot(matrix, high) + dot(matrix, middle) + dot(matrix, low)


def lower_mask():
    rows = lax.broadcasted_iota(jnp.int32, (BLOCK, BLOCK), 0)
    columns = lax.broadcasted_iota(jnp.int32, (BLOCK, BLOCK), 1)
    return rows >= columns


def upper_mask():
    rows = lax.broadcasted_iota(jnp.int32, (BLOCK, BLOCK), 0)
    columns = lax.broadcasted_iota(jnp.int32, (BLOCK, BLOCK), 1)
    return rows <= columns


def as_ones(mask):
    return jnp.where(mask, 1.0, 0.0).astype(BF16)


def inverse_rms(values, epsilon):
    return lax.rsqrt(jnp.mean(values * values, axis=-1, keepdims=True) + epsilon)


def sigmoid(values):
    return 0.5 + 0.5 * jnp.tanh(0.5 * values)


def fill(info, first, second, pieces):
    heads = first.shape[1]
    for head in range(heads):
        slot = info[2 * GROUPS + head]
        for group in range(GROUPS):
            lanes = slice(group * LANES, (group + 1) * LANES)
            place = info[GROUPS + group]
            for source_index, source in enumerate((first, second)):

                @pl.when(info[group] == source_index)
                def _():
                    for target, start, count in pieces:
                        if target.shape[0] == count and head > 0:
                            continue
                        at = head * count
                        target[at : at + count, lanes] = source[
                            place, slot, start : start + count
                        ]


def project_kernel(
    info, tokens, gain, first, second, decay_out,
    normed_out, kv_out, rank_out, logits_out, cum_out, state_out, total_out, weight, rank_weight,
):
    heads = first.shape[1]
    size = HK + HV
    ranks = rank_out.shape[1]

    @pl.when(pl.program_id(0) == 0)
    def _():
        state_out[...] = jnp.zeros_like(state_out)
        total_out[...] = jnp.zeros_like(total_out)
        fill(info, first, second, ((weight, 0, size), (rank_weight, size, ranks)))

    inputs = tokens[...].astype(F32)
    normed = (inputs * inverse_rms(inputs, NORM_EPS) * gain[...]).astype(BF16)
    normed_out[...] = normed
    rank = dot(normed, rank_weight[...], NT)
    rank_out[...] = rank
    lower = as_ones(lower_mask())
    made = dot(normed, weight[...], NT)
    every = range(heads)
    keys = [made[:, head * size : head * size + HK] for head in every]
    values = [made[:, head * size + HK : (head + 1) * size] for head in every]
    logits = []
    for head in every:
        slot = info[2 * GROUPS + head]
        logits.append(
            lax.dot_general(
                rank, decay_out[slot, :ranks], NN, precision=lax.Precision.HIGHEST,
                preferred_element_type=F32,
            )
            + decay_out[slot, ranks : ranks + 1]
        )
    for head in every:
        kv_out[head, :, :HK] = keys[head]
        kv_out[head, :, HK:] = values[head]
        logits_out[head] = logits[head]
    log_decay = [
        (jnp.minimum(item, 0.0) - jnp.log1p(jnp.exp(-jnp.abs(item)))) / GATE_SCALE
        for item in logits
    ]
    for part in range(ROWS // BLOCK):
        span = slice(part * BLOCK, (part + 1) * BLOCK)
        cum = [dot_exact(lower, log_decay[head][span]) for head in every]
        total = [item[BLOCK - 1 :] for item in cum]
        carried = [
            split_two(keys[head][span] * jnp.exp(total[head] - cum[head])) for head in every
        ]
        value_parts = [split_two(values[head][span]) for head in every]
        added = [dot_split(value_parts[head], carried[head], TN) for head in every]
        for head in every:
            cum_out[head, span] = cum[head]
            state_out[head] = state_out[head] * jnp.exp(total[head]) + added[head]
            total_out[head] += total[head]


def mix_kernel(
    info, tokens, normed, kv, cum_in, start, first, second, head_gain, gain,
    query_out, gate_out, mixed_out, state_out, gated_out, middle_out, normed_out, weight, out_weight,
    state_ref, gated_ref,
):
    heads = start.shape[0]
    size = HK + HV

    @pl.when(pl.program_id(0) == 0)
    def _():
        state_ref[...] = start[...]
        fill(info, first, second, ((weight, 0, size), (out_weight, size, HV)))

    made = dot(normed[...], weight[...], NT)
    causal = lower_mask()
    every = range(heads)
    for part in range(ROWS // BLOCK):
        span = slice(part * BLOCK, (part + 1) * BLOCK)
        query = [made[span, head * size : head * size + HK] * HK ** (-0.5) for head in every]
        out_gate = [made[span, head * size + HK : (head + 1) * size] for head in every]
        keys = [kv[head, span, :HK] for head in every]
        cum = [cum_in[head, span] for head in every]
        center = [item[MID : MID + 1] for item in cum]
        total = [item[BLOCK - 1 :] for item in cum]
        query_mid = [split_two(query[head] * jnp.exp(cum[head] - center[head])) for head in every]
        key_mid = [split_two(keys[head] * jnp.exp(center[head] - cum[head])) for head in every]
        scores = [dot_split(query_mid[head], key_mid[head], NT) for head in every]
        since = [split_two(query[head] * jnp.exp(cum[head])) for head in every]
        states = [state_ref[head] for head in every]
        carried = [split_two(keys[head] * jnp.exp(total[head] - cum[head])) for head in every]
        values = [split_two(kv[head, span, HK:]) for head in every]
        outer = [dot_split(since[head], split_two(states[head]), NT) for head in every]
        added = [dot_split(values[head], carried[head], TN) for head in every]
        scores = [split_two(jnp.where(causal, item, 0.0)) for item in scores]
        mixed = [dot_split(scores[head], values[head]) + outer[head] for head in every]
        for head in every:
            query_out[head, span] = query[head]
            gate_out[head, span] = out_gate[head]
            state_out[part, head] = states[head]
            state_ref[head] = states[head] * jnp.exp(total[head]) + added[head]
            mixed_out[head, span] = mixed[head]
        for head in every:
            gated_ref[span, head * HV : (head + 1) * HV] = (
                mixed[head]
                * inverse_rms(mixed[head], HEAD_EPS)
                * head_gain[...]
                * (out_gate[head] * sigmoid(out_gate[head]))
            ).astype(BF16)

    for head in every:

        @pl.when(info[2 * GROUPS + heads] == head)
        def _():
            gated_out[...] = gated_ref[:, head * HV : (head + 1) * HV]

    middle = tokens[...].astype(F32) + dot(gated_ref[...], out_weight[...])
    middle_out[...] = middle
    normed_out[...] = (middle * inverse_rms(middle, NORM_EPS) * gain[...]).astype(BF16)


def ffn_kernel(
    weight_pieces, info, normed, back, middle, weight, gain,
    active_out, back_gate_out, back_up_out, layer_out, back_middle_out, back_attn_out, gain_out,
    ffn_ref, back_ref, active_ref, back_gate_ref, back_up_ref,
):
    step, piece = pl.program_id(0), pl.program_id(1)
    units = weight.shape[2] // 3

    @pl.when((step == 0) & (piece == 0))
    def _():
        ffn_ref[...] = jnp.zeros_like(ffn_ref)
        back_ref[...] = jnp.zeros_like(back_ref)
        gain_out[...] = jnp.zeros_like(gain_out)

    def rows_of(start):
        return jnp.concatenate(
            [weight[group, 0, start : start + units] for group in range(GROUPS)], axis=1
        )

    gate_weight, up_weight, down_weight = rows_of(0), rows_of(units), rows_of(2 * units)
    count = normed.shape[0] // FFN_PARTS
    spans = [slice(part * count, (part + 1) * count) for part in range(FFN_PARTS)]
    made = [
        (
            dot(normed[span], gate_weight, NT),
            dot(normed[span], up_weight, NT),
            dot(back[span], down_weight, NT),
        )
        for span in spans
    ]
    for span, (gate_values, upward, back_active) in zip(spans, made):
        share = sigmoid(gate_values)
        silu = gate_values * share
        active = (silu * upward).astype(BF16)
        back_gate = (
            back_active * upward * (share * (1.0 + gate_values * (1.0 - share)))
        ).astype(BF16)
        back_up = (back_active * silu).astype(BF16)
        ffn = dot(active, down_weight)
        back_normed = dot(back_gate, gate_weight) + dot(back_up, up_weight)
        keep = jnp.where(piece > 0, 1.0, 0.0)
        ffn_ref[span] = ffn_ref[span] * keep + ffn
        back_ref[span] = back_ref[span] * keep + back_normed
        active_ref[span] = active
        back_gate_ref[span] = back_gate
        back_up_ref[span] = back_up

    @pl.when(piece == info[2 * GROUPS + weight_pieces])
    def _():
        active_out[...] = active_ref[...]
        back_gate_out[...] = back_gate_ref[...]
        back_up_out[...] = back_up_ref[...]

    @pl.when(piece == pl.num_programs(1) - 1)
    def _():
        mid = middle[...]
        layer_out[...] = (mid + ffn_ref[...]).astype(BF16)
        inverse = inverse_rms(mid, NORM_EPS)
        unit = mid * inverse
        total = back_ref[...]
        weighted = total * gain[...]
        back_middle = back[...].astype(F32) + inverse * (
            weighted - unit * jnp.mean(weighted * unit, axis=-1, keepdims=True)
        )
        back_middle_out[...] = back_middle
        back_attn_out[...] = back_middle.astype(BF16)
        gain_out[...] += jnp.sum(total * unit, axis=0, keepdims=True)


def gate_back_kernel(
    back_attn, out_weight, mixed_in, gate, query_in, cum_in, head_gain,
    back_mixed_out, back_gate_out, gain_out, state_out,
):
    heads = gate.shape[0]

    @pl.when(pl.program_id(0) == 0)
    def _():
        gain_out[...] = jnp.zeros_like(gain_out)
        state_out[...] = jnp.zeros_like(state_out)

    every = range(heads)
    back_gated = [
        dot(back_attn[...], out_weight[head * HV : (head + 1) * HV], NT) for head in every
    ]
    scaled = [query_in[head] * jnp.exp(cum_in[head]) for head in every]
    back_mixed = []
    for head in every:
        mixed = mixed_in[head]
        out_gate = gate[head]
        inverse = inverse_rms(mixed, HEAD_EPS)
        unit = mixed * inverse
        share = sigmoid(out_gate)
        silu = out_gate * share
        slope = share * (1.0 + out_gate * (1.0 - share))
        shaped_back = back_gated[head] * unit
        back_gate_out[head] = (shaped_back * head_gain[...] * slope).astype(BF16)
        gain_out[...] += jnp.sum(shaped_back * silu, axis=0, keepdims=True)
        weighted = back_gated[head] * head_gain[...] * silu
        item = inverse * (weighted - unit * jnp.mean(weighted * unit, axis=-1, keepdims=True))
        back_mixed_out[head] = item
        back_mixed.append(item)
    for part in reversed(range(ROWS // BLOCK)):
        span = slice(part * BLOCK, (part + 1) * BLOCK)
        added = [
            dot_split(split_two(back_mixed[head][span]), split_two(scaled[head][span]), TN)
            for head in every
        ]
        for head in every:
            last = cum_in[head, (part + 1) * BLOCK - 1 : (part + 1) * BLOCK]
            state_out[head] = state_out[head] * jnp.exp(last) + added[head]


def mix_back_kernel(
    homes, info, tokens, back_middle, query_in, kv, cum_in, logits_in, states, back_mixed, back_gate,
    back_end, query_weight, key_weight, rank_weight, decay_out, rank, gain,
    grad_out, input_out, decay_grad_out, bias_out, gain_out,
    state_ref, query_ref, key_ref, grad_ref,
):
    heads = back_end.shape[0]
    size = HK + HV
    ranks = rank.shape[1]

    @pl.when(pl.program_id(0) == 0)
    def _():
        state_ref[...] = back_end[...]
        grad_out[...] = jnp.zeros_like(grad_out)
        decay_grad_out[...] = jnp.zeros_like(decay_grad_out)
        bias_out[...] = jnp.zeros_like(bias_out)
        gain_out[...] = jnp.zeros_like(gain_out)

    causal = lower_mask()
    upper = as_ones(upper_mask())
    every = range(heads)
    for part in reversed(range(ROWS // BLOCK)):
        span = slice(part * BLOCK, (part + 1) * BLOCK)
        query = [query_in[head, span] for head in every]
        keys = [kv[head, span, :HK] for head in every]
        cum = [cum_in[head, span] for head in every]
        center = [item[MID : MID + 1] for item in cum]
        total = [item[BLOCK - 1 :] for item in cum]
        grow = [jnp.exp(cum[head] - center[head]) for head in every]
        shrink = [jnp.exp(center[head] - cum[head]) for head in every]
        query_mid = [split_two(query[head] * grow[head]) for head in every]
        key_mid = [split_two(keys[head] * shrink[head]) for head in every]
        values = [split_two(kv[head, span, HK:]) for head in every]
        back = [split_two(back_mixed[head, span]) for head in every]
        scores = [dot_split(query_mid[head], key_mid[head], NT) for head in every]
        back_scores = [dot_split(back[head], values[head], NT) for head in every]
        since = [jnp.exp(cum[head]) for head in every]
        until = [jnp.exp(total[head] - cum[head]) for head in every]
        carried = [keys[head] * until[head] for head in every]
        back_state = [state_ref[head] for head in every]
        back_state_parts = [split_two(item) for item in back_state]
        back_carried = [dot_split(values[head], back_state_parts[head]) for head in every]
        back_since = [dot_split(back[head], split_two(states[part, head])) for head in every]
        added = [
            dot_split(back[head], split_two(query[head] * since[head]), TN) for head in every
        ]
        outer = [
            dot_split(split_two(carried[head]), back_state_parts[head], NT) for head in every
        ]
        scores = [split_two(jnp.where(causal, item, 0.0)) for item in scores]
        back_scores = [split_two(jnp.where(causal, item, 0.0)) for item in back_scores]
        back_query = [
            dot_split(back_scores[head], key_mid[head]) * grow[head]
            + back_since[head] * since[head]
            for head in every
        ]
        back_keys = [
            dot_split(back_scores[head], query_mid[head], TN) * shrink[head]
            + back_carried[head] * until[head]
            for head in every
        ]
        back_values = [dot_split(scores[head], back[head], TN) + outer[head] for head in every]
        back_total = []
        for head in every:
            decayed = back_state[head] * jnp.exp(total[head])
            back_total.append(
                jnp.sum(back_carried[head] * carried[head], axis=0, keepdims=True)
                + jnp.sum(decayed * states[part, head], axis=0, keepdims=True)
            )
            state_ref[head] = decayed + added[head]
        back_logits = [
            (
                dot_exact(upper, query[head] * back_query[head] - keys[head] * back_keys[head])
                + back_total[head]
            )
            * sigmoid(-logits_in[head, span])
            / GATE_SCALE
            for head in every
        ]
        rank_parts = split_two(rank[span])
        rank_back = jnp.zeros((BLOCK, ranks), F32)
        for head in every:
            slot = info[2 * GROUPS + head]
            rank_back += lax.dot_general(
                back_logits[head], decay_out[slot, :ranks], NT, precision=lax.Precision.HIGHEST,
                preferred_element_type=F32,
            )
            bias_out[head] += jnp.sum(back_logits[head], axis=0, keepdims=True)
            decay_grad_out[head] += dot_split(rank_parts, split_two(back_logits[head]), TN)
            at = head * size
            query_ref[span, at : at + HK] = (back_query[head] * HK ** (-0.5)).astype(BF16)
            query_ref[span, at + HK : at + size] = back_gate[head, span]
            key_ref[span, at : at + HK] = back_keys[head].astype(BF16)
            key_ref[span, at + HK : at + size] = back_values[head].astype(BF16)
        grad_ref[span, 2 * size :] = rank_back.astype(BF16)

    for head in every:

        @pl.when(info[2 * GROUPS + heads] == head)
        def _():
            grad_ref[:, :size] = query_ref[:, head * size : (head + 1) * size]
            grad_ref[:, size : 2 * size] = key_ref[:, head * size : (head + 1) * size]

    back_normed = (
        dot(grad_ref[:, 2 * size :], rank_weight[...])
        + dot(query_ref[...], query_weight[...])
        + dot(key_ref[...], key_weight[...])
    )
    inputs = tokens[...].astype(F32)
    inverse = inverse_rms(inputs, NORM_EPS)
    unit = inputs * inverse
    normed = (unit * gain[...]).astype(BF16)
    weight_grad = dot(normed, grad_ref[...], TN)
    for group in range(GROUPS):
        grad_out[info[group], homes[group]] += weight_grad[group * LANES : (group + 1) * LANES]
    weighted = back_normed * gain[...]
    input_out[...] = back_middle[...] + inverse * (
        weighted - unit * jnp.mean(weighted * unit, axis=-1, keepdims=True)
    )
    gain_out[...] += jnp.sum(back_normed * unit, axis=0, keepdims=True)


def shaped(shape, kind=F32):
    return jax.ShapeDtypeStruct(shape, kind)


def call(kernel, grid, in_specs, out_specs, out_shape, scratch, operands, prefetch, flops, moved):
    return pl.pallas_call(
        kernel,
        grid_spec=pltpu.PrefetchScalarGridSpec(
            num_scalar_prefetch=prefetch,
            grid=grid,
            in_specs=in_specs,
            out_specs=out_specs,
            scratch_shapes=scratch,
        ),
        out_shape=out_shape,
        compiler_params=pltpu.CompilerParams(
            vmem_limit_bytes=VMEM_LIMIT, dimension_semantics=("arbitrary",) * len(grid)
        ),
        cost_estimate=pl.CostEstimate(flops=flops, bytes_accessed=moved, transcendentals=0),
    )(*operands)


def from_behind(value, axis, steps):
    count = lax.axis_size(axis)
    first, last = (max(0, -steps), min(count, count - steps))
    return lax.ppermute(value, axis, [(source, source + steps) for source in range(first, last)])


def carry(local, decay, steps):
    incoming = jnp.zeros_like(local)
    for _ in range(lax.axis_size("ctx") - 1):
        incoming = from_behind(decay * incoming + local, "ctx", steps)
    return incoming


def staged():
    return lax.axis_size("dp") == 4 and lax.axis_size("ctx") == 2


def swap(value, axis, distance):
    count = lax.axis_size(axis)
    return lax.ppermute(value, axis, [(source, source ^ distance) for source in range(count)])


def shift(value, axis, distance):
    count = lax.axis_size(axis)
    return lax.ppermute(
        value, axis, [(source, (source + distance) % count) for source in range(count)]
    )


def gather_plain(pack):
    rows = pack.shape[0]
    whole = lax.all_gather(lax.all_gather(pack, "tp"), ("dp", "ctx"), axis=2, tiled=True)
    return whole.reshape(whole.shape[0], rows, GROUPS, LANES).transpose(2, 0, 1, 3)


def gather_line(pack):
    count = lax.axis_size("tp")
    return jnp.stack([pack] + [shift(pack, "tp", distance) for distance in range(1, count)])


def gather_square(line):
    return jnp.stack([line] + [swap(line, "dp", distance) for distance in range(1, 4)])


def gather_slots(key_pack, query_pack):
    key_line = gather_line(key_pack)
    query_pack, key_line = lax.optimization_barrier((query_pack, key_line))
    key_first = gather_square(key_line)
    query_line = gather_line(query_pack)
    query_line, key_first = lax.optimization_barrier((query_line, key_first))
    query_first = gather_square(query_line)
    return (
        key_first,
        swap(key_first, "ctx", 1),
        query_first,
        swap(query_first, "ctx", 1),
    )


def gather_pair(pack):
    whole = gather_plain(pack)
    half = GROUPS // 2
    return whole[:half], whole[half:]


def gather_homes():
    if staged():
        return [group // 2 for group in range(GROUPS)]
    return [group % (GROUPS // 2) for group in range(GROUPS)]


def gather_info():
    count = lax.axis_size("tp")
    own = lax.axis_index("tp")
    group = jnp.arange(GROUPS, dtype=jnp.int32)
    heads = jnp.arange(count, dtype=jnp.int32)
    if staged():
        which = (group % 2) ^ lax.axis_index("ctx")
        place = (group // 2) ^ lax.axis_index("dp")
        slot = lax.rem(own - heads + count, count)
    else:
        which, place, slot = group // (GROUPS // 2), group % (GROUPS // 2), heads
    return jnp.concatenate([which, place, slot, own.reshape(1)]).astype(jnp.int32)


def gather_whole(pack):
    if staged():
        rows, share = pack.shape
        whole = lax.all_gather(pack, ("dp", "ctx", "tp"))
        return whole.reshape(-1, lax.axis_size("tp"), rows, share)
    return gather_plain(pack)


def scatter_rows(value):
    columns = value.shape[-1]
    if not staged():
        return lax.psum_scatter(
            value.reshape(-1, columns), ("dp", "ctx"), scatter_dimension=0, tiled=True
        )
    device = lax.axis_index("dp")
    row, column = device // 2, device % 2

    def pick(array, axis, index):
        return lax.dynamic_index_in_dim(array, index, axis, keepdims=False)

    value = (value[0] + swap(value[1], "ctx", 1)).reshape(2, 2, LANES, columns)
    half = LANES // 2
    upper, lower = value[:, :, :half], value[:, :, half:]
    upper = pick(upper, 1, column) + swap(pick(upper, 1, 1 - column), "dp", 1)
    lower = pick(lower, 0, row) + swap(pick(lower, 0, 1 - row), "dp", 2)
    upper = pick(upper, 0, row) + swap(pick(upper, 0, 1 - row), "dp", 2)
    lower = pick(lower, 0, column) + swap(pick(lower, 0, 1 - column), "dp", 1)
    return jnp.concatenate([upper, lower])


def total_over(value):
    if not staged():
        return lax.psum(value, ("dp", "ctx"))
    for axis, distance in (("ctx", 1), ("dp", 1), ("dp", 2)):
        value = value + swap(value, axis, distance)
    return value


def adamw(weight_now, grad_now, mean_now, square_now, rate_value, decay_value):
    mean_new = BETA_ONE * mean_now + (1.0 - BETA_ONE) * grad_now
    square_new = BETA_TWO * square_now + (1.0 - BETA_TWO) * grad_now * grad_now
    mean_hat = mean_new / (1.0 - BETA_ONE**STEP)
    square_hat = square_new / (1.0 - BETA_TWO**STEP)
    weight_new = weight_now - rate_value * (
        mean_hat / (jnp.sqrt(square_hat) + ADAM_EPS) + decay_value * weight_now
    )
    return (mean_new, square_new, weight_new)


def three_parts(value):
    high = lax.reduce_precision(value, 8, 7)
    rest = value - high
    middle = lax.reduce_precision(rest, 8, 7)
    low = lax.reduce_precision(rest - middle, 8, 7)
    return [part.astype(BF16) for part in (high, middle, low)]


def body(
    tokens,
    cotangent,
    lengths,
    query_key_weight,
    query_key_mean,
    query_key_square,
    value_gate_weight,
    value_gate_mean,
    value_gate_square,
    decay_in_weight,
    decay_in_mean,
    decay_in_square,
    decay_out_weight,
    decay_out_mean,
    decay_out_square,
    decay_bias,
    decay_bias_mean,
    decay_bias_square,
    output_weight,
    output_mean,
    output_square,
    gate_up_weight,
    gate_up_mean,
    gate_up_square,
    down_weight,
    down_mean,
    down_square,
    gains,
    gains_mean,
    gains_square,
):
    rows, width = tokens.shape
    heads = lax.axis_size("tp")
    ranks = decay_in_weight.shape[1]
    units = down_weight.shape[0]
    steps = rows // ROWS
    info = gather_info()
    gain_one = gains[:width].reshape(1, width)
    gain_two = gains[width : 2 * width].reshape(1, width)
    gain_head = gains[2 * width :].reshape(1, HV)
    size = HK + HV

    small = jnp.concatenate(
        [
            decay_out_weight,
            decay_bias.reshape(1, HK),
            jnp.zeros((DECAY_ROWS - ranks - 1, HK), F32),
        ]
    )
    key_parts = [
        query_key_weight[1].T.astype(BF16),
        value_gate_weight[0].T.astype(BF16),
        decay_in_weight.T.astype(BF16),
    ]
    query_pack = jnp.concatenate(
        [query_key_weight[0].T, value_gate_weight[1].T, output_weight]
    ).astype(BF16)
    if staged():
        key_first, key_second, query_first, query_second = gather_slots(
            jnp.concatenate(key_parts + three_parts(small)), query_pack
        )
        sent = key_first[0, :, size + ranks :].astype(F32).reshape(heads, 3, DECAY_ROWS, HK)
        decay_out_full = sent[:, 0] + sent[:, 1] + sent[:, 2]
    else:
        key_first, key_second = gather_pair(jnp.concatenate(key_parts))
        query_first, query_second = gather_pair(query_pack)
        decay_out_full = lax.all_gather(small, "tp")
    ffn = gather_whole(
        jnp.concatenate([gate_up_weight[0].T, gate_up_weight[1].T, down_weight]).astype(BF16)
    )

    position = lax.axis_index("ctx") * rows + jnp.arange(rows, dtype=jnp.int32)
    back_ffn = jnp.where((position < lengths[0])[:, None], cotangent, jnp.zeros_like(cotangent))

    columns = 2 * size
    row_spec = pl.BlockSpec((ROWS, width), lambda i, *_: (i, 0))
    gain_spec = pl.BlockSpec((1, width), lambda i, *_: (0, 0))
    head_gain_spec = pl.BlockSpec((1, HV), lambda i, *_: (0, 0))
    state_spec = pl.BlockSpec((heads, HV, HK), lambda i, *_: (0, 0, 0))
    bias_spec = pl.BlockSpec((heads, 1, HK), lambda i, *_: (0, 0, 0))

    def fixed(array):
        return pl.BlockSpec(
            array.shape, lambda i, *_: (0,) * len(array.shape), pipeline_mode=pl.Buffered(1)
        )

    def by_head(length, reverse=False):
        if reverse:
            return pl.BlockSpec((heads, ROWS, length), lambda i, *_: (0, steps - 1 - i, 0))
        return pl.BlockSpec((heads, ROWS, length), lambda i, *_: (0, i, 0))

    weight_shape = shaped((heads * size, width), BF16)
    rank_shape = shaped((ranks, width), BF16)
    out_weight_shape = shaped((heads * HV, width), BF16)
    parts = ROWS // BLOCK
    normed, kv, rank, logits, cum, local_state, local_total, key_weight, rank_weight = call(
        project_kernel,
        (steps,),
        [row_spec, gain_spec, fixed(key_first), fixed(key_second), fixed(decay_out_full)],
        [
            row_spec,
            by_head(size),
            pl.BlockSpec((ROWS, ranks), lambda i, *_: (i, 0)),
            by_head(HK),
            by_head(HK),
            state_spec,
            bias_spec,
            fixed(weight_shape),
            fixed(rank_shape),
        ],
        [
            shaped((rows, width), BF16),
            shaped((heads, rows, size)),
            shaped((rows, ranks)),
            shaped((heads, rows, HK)),
            shaped((heads, rows, HK)),
            shaped((heads, HV, HK)),
            shaped((heads, 1, HK)),
            weight_shape,
            rank_shape,
        ],
        [],
        (info, tokens, gain_one, key_first, key_second, decay_out_full),
        1,
        2 * rows * width * size * heads,
        rows * heads * 4 * 1024,
    )
    device_decay = jnp.exp(local_total)
    start_state = carry(local_state, device_decay, 1)

    query, out_gate, mixed, states, gated_own, middle, normed_two, query_weight, out_weight = call(
        mix_kernel,
        (steps,),
        [
            row_spec,
            row_spec,
            by_head(size),
            by_head(HK),
            state_spec,
            fixed(query_first),
            fixed(query_second),
            head_gain_spec,
            gain_spec,
        ],
        [
            by_head(HK),
            by_head(HV),
            by_head(HV),
            pl.BlockSpec((parts, heads, HV, HK), lambda i, *_: (i, 0, 0, 0)),
            pl.BlockSpec((ROWS, HV), lambda i, *_: (i, 0)),
            row_spec,
            row_spec,
            fixed(weight_shape),
            fixed(out_weight_shape),
        ],
        [
            shaped((heads, rows, HK)),
            shaped((heads, rows, HV)),
            shaped((heads, rows, HV)),
            shaped((steps * parts, heads, HV, HK)),
            shaped((rows, HV), BF16),
            shaped((rows, width)),
            shaped((rows, width), BF16),
            weight_shape,
            out_weight_shape,
        ],
        [pltpu.VMEM((heads, HV, HK), F32), pltpu.VMEM((ROWS, heads * HV), BF16)],
        (
            info, tokens, normed, kv, cum, start_state, query_first, query_second,
            gain_head, gain_two,
        ),
        1,
        2 * rows * width * (size + 2 * HV) * heads,
        rows * heads * 4 * 1024,
    )

    wide_spec = pl.BlockSpec((FFN_ROWS, width), lambda i, j, *_: (i, 0))
    own_spec = pl.BlockSpec((FFN_ROWS, units), lambda i, j, *_: (i, 0))
    wide_gain_spec = pl.BlockSpec((1, width), lambda i, j, *_: (0, 0))
    active, back_gate, back_up, layer_out, back_middle, back_attn, gain_two_part = call(
        functools.partial(ffn_kernel, heads),
        (rows // FFN_ROWS, heads),
        [
            wide_spec,
            wide_spec,
            wide_spec,
            pl.BlockSpec((GROUPS, 1, 3 * units, LANES), lambda i, j, *_: (0, j, 0, 0)),
            wide_gain_spec,
        ],
        [own_spec, own_spec, own_spec, wide_spec, wide_spec, wide_spec, wide_gain_spec],
        [
            shaped((rows, units), BF16),
            shaped((rows, units), BF16),
            shaped((rows, units), BF16),
            shaped((rows, width), BF16),
            shaped((rows, width)),
            shaped((rows, width), BF16),
            shaped((1, width)),
        ],
        [
            pltpu.VMEM((FFN_ROWS, width), F32),
            pltpu.VMEM((FFN_ROWS, width), F32),
            pltpu.VMEM((FFN_ROWS, units), BF16),
            pltpu.VMEM((FFN_ROWS, units), BF16),
            pltpu.VMEM((FFN_ROWS, units), BF16),
        ],
        (info, normed_two, back_ffn, middle, ffn, gain_two),
        1,
        12 * rows * width * units * heads,
        rows * width * 24,
    )
    early_grad = jnp.concatenate(
        [
            dot(back_gate, normed_two, TN),
            dot(back_up, normed_two, TN),
            dot(active, back_ffn, TN),
            dot(gated_own, back_attn, TN),
        ]
    )
    early_grad, back_attn = lax.optimization_barrier((early_grad, back_attn))
    early_share = lax.psum_scatter(early_grad, ("dp", "ctx"), scatter_dimension=1, tiled=True)

    back_row_spec = pl.BlockSpec((ROWS, width), lambda i, *_: (steps - 1 - i, 0))
    back_mixed, back_out_gate, head_gain_part, collected = call(
        gate_back_kernel,
        (steps,),
        [
            back_row_spec,
            fixed(out_weight),
            by_head(HV, True),
            by_head(HV, True),
            by_head(HK, True),
            by_head(HK, True),
            head_gain_spec,
        ],
        [by_head(HV, True), by_head(HV, True), head_gain_spec, state_spec],
        [
            shaped((heads, rows, HV)),
            shaped((heads, rows, HV), BF16),
            shaped((1, HV)),
            shaped((heads, HV, HK)),
        ],
        [],
        (back_attn, out_weight, mixed, out_gate, query, cum, gain_head),
        0,
        2 * rows * width * HV * heads,
        rows * heads * 4 * 1024,
    )
    back_end = carry(collected, device_decay, -1)

    grad_columns = columns + ranks
    grad_shape = shaped((2, GROUPS // 2, LANES, grad_columns))
    mixer_back, input_grad, decay_out_grad, bias_grad, gain_one_part = call(
        functools.partial(mix_back_kernel, gather_homes()),
        (steps,),
        [
            back_row_spec,
            back_row_spec,
            by_head(HK, True),
            by_head(size, True),
            by_head(HK, True),
            by_head(HK, True),
            pl.BlockSpec((parts, heads, HV, HK), lambda i, *_: (steps - 1 - i, 0, 0, 0)),
            by_head(HV, True),
            by_head(HV, True),
            state_spec,
            fixed(query_weight),
            fixed(key_weight),
            fixed(rank_weight),
            fixed(decay_out_full),
            pl.BlockSpec((ROWS, ranks), lambda i, *_: (steps - 1 - i, 0)),
            gain_spec,
        ],
        [
            fixed(grad_shape),
            back_row_spec,
            pl.BlockSpec((heads, ranks, HK), lambda i, *_: (0, 0, 0)),
            bias_spec,
            gain_spec,
        ],
        [
            grad_shape,
            shaped((rows, width)),
            shaped((heads, ranks, HK)),
            shaped((heads, 1, HK)),
            shaped((1, width)),
        ],
        [
            pltpu.VMEM((heads, HV, HK), F32),
            pltpu.VMEM((ROWS, heads * size), BF16),
            pltpu.VMEM((ROWS, heads * size), BF16),
            pltpu.VMEM((ROWS, grad_columns), BF16),
        ],
        (
            info, tokens, back_middle, query, kv, cum, logits, states, back_mixed, back_out_gate,
            back_end, query_weight, key_weight, rank_weight, decay_out_full, rank, gain_one,
        ),
        1,
        2 * rows * width * columns * heads * 2,
        rows * heads * 4 * 2048,
    )
    own = info[-1]
    decay_out_own = lax.dynamic_index_in_dim(decay_out_grad, own, 0, keepdims=False)
    bias_own = lax.dynamic_index_in_dim(bias_grad, own, 0, keepdims=False)
    sums = jnp.concatenate(
        [
            gain_one_part.reshape(-1),
            gain_two_part.reshape(-1),
            head_gain_part.reshape(-1),
            bias_own.reshape(-1),
            decay_out_own.reshape(-1),
        ]
    )
    sums = total_over(sums)
    mixer_share = scatter_rows(mixer_back)
    gain_count = gains.shape[0]
    gains_grad = sums[:gain_count]
    bias_total = sums[gain_count : gain_count + HK]
    decay_out_total = sums[gain_count + HK :].reshape(ranks, HK)

    query_key_share = jnp.stack([mixer_share[:, :HK], mixer_share[:, size : size + HK]])
    value_gate_share = jnp.stack([mixer_share[:, size + HK : columns], mixer_share[:, HK:size]])
    decay_in_share = mixer_share[:, columns:]
    gate_up_share = jnp.stack([early_share[:units].T, early_share[units : 2 * units].T])
    down_share = early_share[2 * units : 3 * units]
    output_share = early_share[3 * units :]

    updated = adamw(
        query_key_weight,
        query_key_share,
        query_key_mean,
        query_key_square,
        RATE_MATRIX,
        WEIGHT_DECAY,
    )
    updated = updated + adamw(
        value_gate_weight,
        value_gate_share,
        value_gate_mean,
        value_gate_square,
        RATE_MATRIX,
        WEIGHT_DECAY,
    )
    updated = updated + adamw(
        decay_in_weight, decay_in_share, decay_in_mean, decay_in_square, RATE_MATRIX, WEIGHT_DECAY
    )
    updated = updated + adamw(
        decay_out_weight, decay_out_total, decay_out_mean, decay_out_square, RATE_RANK, WEIGHT_DECAY
    )
    updated = updated + adamw(
        decay_bias, bias_total, decay_bias_mean, decay_bias_square, RATE_BIAS, 0.0
    )
    updated = updated + adamw(
        output_weight, output_share, output_mean, output_square, RATE_MATRIX, WEIGHT_DECAY
    )
    updated = updated + adamw(
        gate_up_weight, gate_up_share, gate_up_mean, gate_up_square, RATE_MATRIX, WEIGHT_DECAY
    )
    updated = updated + adamw(
        down_weight, down_share, down_mean, down_square, RATE_MATRIX, WEIGHT_DECAY
    )
    updated = updated + adamw(gains, gains_grad, gains_mean, gains_square, RATE_GAIN, 0.0)
    return (layer_out, input_grad) + updated


def solution(mesh):
    tokens_at = P(("dp", "ctx"), None)
    split_at = P(None, ("dp", "ctx"), "tp")
    deep_at = P("tp", ("dp", "ctx"))
    rank_out_at = P(None, "tp")
    kinds = (split_at, split_at, tokens_at, rank_out_at, P("tp"), deep_at, split_at, deep_at, P())
    params = tuple(kind for kind in kinds for _ in range(3))
    return jax.shard_map(
        body,
        mesh=mesh,
        in_specs=(tokens_at, tokens_at, P("dp")) + params,
        out_specs=(tokens_at, tokens_at) + params,
        check_vma=False,
    )
```

```python
import functools

import jax
import jax.numpy as jnp
from jax import lax
from jax.experimental import pallas as pl
from jax.experimental.pallas import tpu as pltpu
from jax.sharding import PartitionSpec as P

HK = 128
HV = 256
BLOCK = 128
LANES = 128
GROUPS = 8
MID = 63
DECAY_ROWS = 32
ROWS = 256
FFN_ROWS = 512
FFN_CUTS = 8
STEP = 10

NORM_EPS = 1e-06
HEAD_EPS = 1e-05
GATE_SCALE = 16.0
BETA_ONE = 0.9
BETA_TWO = 0.95
ADAM_EPS = 1e-08
WEIGHT_DECAY = 0.1
RATE_MATRIX = 0.03
RATE_RANK = 0.1
RATE_BIAS = 1.5
RATE_GAIN = 0.3
VMEM_LIMIT = 60 * 1024 * 1024

F32 = jnp.float32
BF16 = jnp.bfloat16
NN = (((1,), (0,)), ((), ()))
NT = (((1,), (1,)), ((), ()))
TN = (((0,), (0,)), ((), ()))


def dot(left, right, dims=NN):
    return lax.dot_general(left, right, dims, preferred_element_type=F32)


def split_two(values):
    high = values.astype(BF16)
    return high, (values - high.astype(F32)).astype(BF16)


def dot_split(left, right, dims=NN):
    axis = 1 - dims[0][0][0]
    size = left[0].shape[axis]
    both = dot(jnp.concatenate(left, axis=axis), right[0], dims)
    return both[:size] + both[size:] + dot(left[0], right[1], dims)


def dot_exact(matrix, values):
    high = values.astype(BF16)
    rest = values - high.astype(F32)
    middle = rest.astype(BF16)
    low = (rest - middle.astype(F32)).astype(BF16)
    return dot(matrix, high) + dot(matrix, middle) + dot(matrix, low)


def lower_mask():
    rows = lax.broadcasted_iota(jnp.int32, (BLOCK, BLOCK), 0)
    columns = lax.broadcasted_iota(jnp.int32, (BLOCK, BLOCK), 1)
    return rows >= columns


def upper_mask():
    rows = lax.broadcasted_iota(jnp.int32, (BLOCK, BLOCK), 0)
    columns = lax.broadcasted_iota(jnp.int32, (BLOCK, BLOCK), 1)
    return rows <= columns


def as_ones(mask):
    return jnp.where(mask, 1.0, 0.0).astype(BF16)


def inverse_rms(values, epsilon):
    return lax.rsqrt(jnp.mean(values * values, axis=-1, keepdims=True) + epsilon)


def sigmoid(values):
    return 0.5 + 0.5 * jnp.tanh(0.5 * values)


def fill(info, first, second, pieces):
    heads = first.shape[1]
    for head in range(heads):
        slot = info[2 * GROUPS + head]
        for group in range(GROUPS):
            lanes = slice(group * LANES, (group + 1) * LANES)
            place = info[GROUPS + group]
            for source_index, source in enumerate((first, second)):

                @pl.when(info[group] == source_index)
                def _():
                    for target, start, count in pieces:
                        if target.shape[0] == count and head > 0:
                            continue
                        at = head * count
                        target[at : at + count, lanes] = source[
                            place, slot, start : start + count
                        ]


def project_kernel(
    info, tokens, gain, first, second, decay_out,
    normed_out, kv_out, rank_out, logits_out, cum_out, state_out, total_out, weight, rank_weight,
):
    heads = first.shape[1]
    size = HK + HV
    ranks = rank_out.shape[1]

    @pl.when(pl.program_id(0) == 0)
    def _():
        state_out[...] = jnp.zeros_like(state_out)
        total_out[...] = jnp.zeros_like(total_out)
        fill(info, first, second, ((weight, 0, size), (rank_weight, size, ranks)))

    inputs = tokens[...].astype(F32)
    normed = (inputs * inverse_rms(inputs, NORM_EPS) * gain[...]).astype(BF16)
    normed_out[...] = normed
    rank = dot(normed, rank_weight[...], NT)
    rank_out[...] = rank
    lower = as_ones(lower_mask())
    made = dot(normed, weight[...], NT)
    every = range(heads)
    keys = [made[:, head * size : head * size + HK] for head in every]
    values = [made[:, head * size + HK : (head + 1) * size] for head in every]
    logits = []
    for head in every:
        slot = info[2 * GROUPS + head]
        logits.append(
            lax.dot_general(
                rank, decay_out[slot, :ranks], NN, precision=lax.Precision.HIGHEST,
                preferred_element_type=F32,
            )
            + decay_out[slot, ranks : ranks + 1]
        )
    for head in every:
        kv_out[head, :, :HK] = keys[head]
        kv_out[head, :, HK:] = values[head]
        logits_out[head] = logits[head]
    log_decay = [
        (jnp.minimum(item, 0.0) - jnp.log1p(jnp.exp(-jnp.abs(item)))) / GATE_SCALE
        for item in logits
    ]
    for part in range(ROWS // BLOCK):
        span = slice(part * BLOCK, (part + 1) * BLOCK)
        cum = [dot_exact(lower, log_decay[head][span]) for head in every]
        total = [item[BLOCK - 1 :] for item in cum]
        carried = [
            split_two(keys[head][span] * jnp.exp(total[head] - cum[head])) for head in every
        ]
        value_parts = [split_two(values[head][span]) for head in every]
        added = [dot_split(value_parts[head], carried[head], TN) for head in every]
        for head in every:
            cum_out[head, span] = cum[head]
            state_out[head] = state_out[head] * jnp.exp(total[head]) + added[head]
            total_out[head] += total[head]


def mix_kernel(
    info, tokens, normed, kv, cum_in, start, first, second, head_gain, gain,
    query_out, gate_out, mixed_out, state_out, gated_out, middle_out, normed_out, weight, out_weight,
    state_ref, gated_ref,
):
    heads = start.shape[0]
    size = HK + HV

    @pl.when(pl.program_id(0) == 0)
    def _():
        state_ref[...] = start[...]
        fill(info, first, second, ((weight, 0, size), (out_weight, size, HV)))

    made = dot(normed[...], weight[...], NT)
    causal = lower_mask()
    every = range(heads)
    for part in range(ROWS // BLOCK):
        span = slice(part * BLOCK, (part + 1) * BLOCK)
        query = [made[span, head * size : head * size + HK] * HK ** (-0.5) for head in every]
        out_gate = [made[span, head * size + HK : (head + 1) * size] for head in every]
        keys = [kv[head, span, :HK] for head in every]
        cum = [cum_in[head, span] for head in every]
        center = [item[MID : MID + 1] for item in cum]
        total = [item[BLOCK - 1 :] for item in cum]
        query_mid = [split_two(query[head] * jnp.exp(cum[head] - center[head])) for head in every]
        key_mid = [split_two(keys[head] * jnp.exp(center[head] - cum[head])) for head in every]
        scores = [dot_split(query_mid[head], key_mid[head], NT) for head in every]
        since = [split_two(query[head] * jnp.exp(cum[head])) for head in every]
        states = [state_ref[head] for head in every]
        carried = [split_two(keys[head] * jnp.exp(total[head] - cum[head])) for head in every]
        values = [split_two(kv[head, span, HK:]) for head in every]
        outer = [dot_split(since[head], split_two(states[head]), NT) for head in every]
        added = [dot_split(values[head], carried[head], TN) for head in every]
        scores = [split_two(jnp.where(causal, item, 0.0)) for item in scores]
        mixed = [dot_split(scores[head], values[head]) + outer[head] for head in every]
        for head in every:
            query_out[head, span] = query[head]
            gate_out[head, span] = out_gate[head]
            state_out[part, head] = states[head]
            state_ref[head] = states[head] * jnp.exp(total[head]) + added[head]
            mixed_out[head, span] = mixed[head]
        for head in every:
            gated_ref[span, head * HV : (head + 1) * HV] = (
                mixed[head]
                * inverse_rms(mixed[head], HEAD_EPS)
                * head_gain[...]
                * (out_gate[head] * sigmoid(out_gate[head]))
            ).astype(BF16)

    for head in every:

        @pl.when(info[2 * GROUPS + heads] == head)
        def _():
            gated_out[...] = gated_ref[:, head * HV : (head + 1) * HV]

    middle = tokens[...].astype(F32) + dot(gated_ref[...], out_weight[...])
    middle_out[...] = middle
    normed_out[...] = (middle * inverse_rms(middle, NORM_EPS) * gain[...]).astype(BF16)


def ffn_kernel(
    weight_pieces, info, normed, back, middle, weight, gain,
    active_out, back_gate_out, back_up_out, layer_out, back_middle_out, back_attn_out, gain_out,
    ffn_ref, back_ref, active_ref, back_gate_ref, back_up_ref,
):
    step, piece = pl.program_id(0), pl.program_id(1)
    units = weight.shape[2] // 3

    @pl.when((step == 0) & (piece == 0))
    def _():
        gain_out[...] = jnp.zeros_like(gain_out)

    @pl.when(piece == 0)
    def _():
        ffn_ref[...] = jnp.zeros_like(ffn_ref)
        back_ref[...] = jnp.zeros_like(back_ref)

    def rows_of(start):
        return jnp.concatenate(
            [weight[group, 0, start : start + units] for group in range(GROUPS)], axis=1
        )

    gate_weight, up_weight, down_weight = rows_of(0), rows_of(units), rows_of(2 * units)
    half = normed.shape[0] // 2
    third = half // FFN_CUTS

    def made(part):
        span = slice(part * half, (part + 1) * half)
        yield dot(normed[span], gate_weight, NT)
        yield dot(normed[span], up_weight, NT)
        yield dot(back[span], down_weight, NT)

    def elementwise(part, values, cut):
        span = slice(cut * third, (cut + 1) * third)
        target = slice(part * half + cut * third, part * half + (cut + 1) * third)
        gate_values, upward, back_active = [item[span] for item in values]
        share = sigmoid(gate_values)
        silu = gate_values * share
        active_ref[target] = (silu * upward).astype(BF16)
        back_gate_ref[target] = (
            back_active * upward * (share * (1.0 + gate_values * (1.0 - share)))
        ).astype(BF16)
        back_up_ref[target] = (back_active * silu).astype(BF16)

    def added(part):
        span = slice(part * half, (part + 1) * half)
        ffn_ref[span] += dot(active_ref[span], down_weight)
        yield
        back_ref[span] += dot(back_gate_ref[span], gate_weight)
        yield
        back_ref[span] += dot(back_up_ref[span], up_weight)
        yield

    first = list(made(0))
    second = []
    for index, item in enumerate(made(1)):
        second.append(item)
        for cut in range(index * FFN_CUTS // 3, (index + 1) * FFN_CUTS // 3):
            elementwise(0, first, cut)
    for index, _ in enumerate(added(0)):
        for cut in range(index * FFN_CUTS // 3, (index + 1) * FFN_CUTS // 3):
            elementwise(1, second, cut)
    for _ in added(1):
        pass

    @pl.when(piece == info[2 * GROUPS + weight_pieces])
    def _():
        active_out[...] = active_ref[...]
        back_gate_out[...] = back_gate_ref[...]
        back_up_out[...] = back_up_ref[...]

    @pl.when(piece == pl.num_programs(1) - 1)
    def _():
        mid = middle[...]
        layer_out[...] = (mid + ffn_ref[...]).astype(BF16)
        inverse = inverse_rms(mid, NORM_EPS)
        unit = mid * inverse
        total = back_ref[...]
        weighted = total * gain[...]
        back_middle = back[...].astype(F32) + inverse * (
            weighted - unit * jnp.mean(weighted * unit, axis=-1, keepdims=True)
        )
        back_middle_out[...] = back_middle
        back_attn_out[...] = back_middle.astype(BF16)
        gain_out[...] += jnp.sum(total * unit, axis=0, keepdims=True)


def gate_back_kernel(
    back_attn, out_weight, mixed_in, gate, query_in, cum_in, head_gain,
    back_mixed_out, back_gate_out, gain_out, state_out,
):
    heads = gate.shape[0]

    @pl.when(pl.program_id(0) == 0)
    def _():
        gain_out[...] = jnp.zeros_like(gain_out)
        state_out[...] = jnp.zeros_like(state_out)

    every = range(heads)
    back_gated = [
        dot(back_attn[...], out_weight[head * HV : (head + 1) * HV], NT) for head in every
    ]
    scaled = [query_in[head] * jnp.exp(cum_in[head]) for head in every]
    back_mixed = []
    for head in every:
        mixed = mixed_in[head]
        out_gate = gate[head]
        inverse = inverse_rms(mixed, HEAD_EPS)
        unit = mixed * inverse
        share = sigmoid(out_gate)
        silu = out_gate * share
        slope = share * (1.0 + out_gate * (1.0 - share))
        shaped_back = back_gated[head] * unit
        back_gate_out[head] = (shaped_back * head_gain[...] * slope).astype(BF16)
        gain_out[...] += jnp.sum(shaped_back * silu, axis=0, keepdims=True)
        weighted = back_gated[head] * head_gain[...] * silu
        item = inverse * (weighted - unit * jnp.mean(weighted * unit, axis=-1, keepdims=True))
        back_mixed_out[head] = item
        back_mixed.append(item)
    for part in reversed(range(ROWS // BLOCK)):
        span = slice(part * BLOCK, (part + 1) * BLOCK)
        added = [
            dot_split(split_two(back_mixed[head][span]), split_two(scaled[head][span]), TN)
            for head in every
        ]
        for head in every:
            last = cum_in[head, (part + 1) * BLOCK - 1 : (part + 1) * BLOCK]
            state_out[head] = state_out[head] * jnp.exp(last) + added[head]


def mix_back_kernel(
    homes, info, tokens, back_middle, query_in, kv, cum_in, logits_in, states, back_mixed, back_gate,
    back_end, query_weight, key_weight, rank_weight, decay_out, rank, gain,
    kept_out, sent_out, rank_grad_out, input_out, decay_grad_out, bias_out, gain_out,
    state_ref, query_ref, key_ref, grad_ref, rank_ref, sum_ref,
):
    heads = back_end.shape[0]
    size = HK + HV
    ranks = rank.shape[1]

    @pl.when(pl.program_id(0) == 0)
    def _():
        state_ref[...] = back_end[...]
        sum_ref[...] = jnp.zeros_like(sum_ref)
        rank_grad_out[...] = jnp.zeros_like(rank_grad_out)
        decay_grad_out[...] = jnp.zeros_like(decay_grad_out)
        bias_out[...] = jnp.zeros_like(bias_out)
        gain_out[...] = jnp.zeros_like(gain_out)

    causal = lower_mask()
    upper = as_ones(upper_mask())
    every = range(heads)
    for part in reversed(range(ROWS // BLOCK)):
        span = slice(part * BLOCK, (part + 1) * BLOCK)
        query = [query_in[head, span] for head in every]
        keys = [kv[head, span, :HK] for head in every]
        cum = [cum_in[head, span] for head in every]
        center = [item[MID : MID + 1] for item in cum]
        total = [item[BLOCK - 1 :] for item in cum]
        grow = [jnp.exp(cum[head] - center[head]) for head in every]
        shrink = [jnp.exp(center[head] - cum[head]) for head in every]
        query_mid = [split_two(query[head] * grow[head]) for head in every]
        key_mid = [split_two(keys[head] * shrink[head]) for head in every]
        values = [split_two(kv[head, span, HK:]) for head in every]
        back = [split_two(back_mixed[head, span]) for head in every]
        scores = [dot_split(query_mid[head], key_mid[head], NT) for head in every]
        back_scores = [dot_split(back[head], values[head], NT) for head in every]
        since = [jnp.exp(cum[head]) for head in every]
        until = [jnp.exp(total[head] - cum[head]) for head in every]
        carried = [keys[head] * until[head] for head in every]
        back_state = [state_ref[head] for head in every]
        back_state_parts = [split_two(item) for item in back_state]
        back_carried = [dot_split(values[head], back_state_parts[head]) for head in every]
        back_since = [dot_split(back[head], split_two(states[part, head])) for head in every]
        added = [
            dot_split(back[head], split_two(query[head] * since[head]), TN) for head in every
        ]
        outer = [
            dot_split(split_two(carried[head]), back_state_parts[head], NT) for head in every
        ]
        scores = [split_two(jnp.where(causal, item, 0.0)) for item in scores]
        back_scores = [split_two(jnp.where(causal, item, 0.0)) for item in back_scores]
        back_query = [
            dot_split(back_scores[head], key_mid[head]) * grow[head]
            + back_since[head] * since[head]
            for head in every
        ]
        back_keys = [
            dot_split(back_scores[head], query_mid[head], TN) * shrink[head]
            + back_carried[head] * until[head]
            for head in every
        ]
        back_values = [dot_split(scores[head], back[head], TN) + outer[head] for head in every]
        back_total = []
        for head in every:
            decayed = back_state[head] * jnp.exp(total[head])
            back_total.append(
                jnp.sum(back_carried[head] * carried[head], axis=0, keepdims=True)
                + jnp.sum(decayed * states[part, head], axis=0, keepdims=True)
            )
            state_ref[head] = decayed + added[head]
        back_logits = [
            (
                dot_exact(upper, query[head] * back_query[head] - keys[head] * back_keys[head])
                + back_total[head]
            )
            * sigmoid(-logits_in[head, span])
            / GATE_SCALE
            for head in every
        ]
        rank_parts = split_two(rank[span])
        rank_back = jnp.zeros((BLOCK, ranks), F32)
        for head in every:
            slot = info[2 * GROUPS + head]
            rank_back += lax.dot_general(
                back_logits[head], decay_out[slot, :ranks], NT, precision=lax.Precision.HIGHEST,
                preferred_element_type=F32,
            )
            bias_out[head] += jnp.sum(back_logits[head], axis=0, keepdims=True)
            decay_grad_out[head] += dot_split(rank_parts, split_two(back_logits[head]), TN)
            at = head * size
            query_ref[span, at : at + HK] = (back_query[head] * HK ** (-0.5)).astype(BF16)
            query_ref[span, at + HK : at + size] = back_gate[head, span]
            key_ref[span, at : at + HK] = back_keys[head].astype(BF16)
            key_ref[span, at + HK : at + size] = back_values[head].astype(BF16)
        rank_ref[span] = rank_back.astype(BF16)

    for head in every:

        @pl.when(info[2 * GROUPS + heads] == head)
        def _():
            grad_ref[:, :size] = query_ref[:, head * size : (head + 1) * size]
            grad_ref[:, size:] = key_ref[:, head * size : (head + 1) * size]

    back_normed = (
        dot(rank_ref[...], rank_weight[...])
        + dot(query_ref[...], query_weight[...])
        + dot(key_ref[...], key_weight[...])
    )
    inputs = tokens[...].astype(F32)
    inverse = inverse_rms(inputs, NORM_EPS)
    unit = inputs * inverse
    normed = (unit * gain[...]).astype(BF16)
    sum_ref[...] += dot(normed, grad_ref[...], TN)
    rank_grad_out[...] += dot(rank_ref[...], normed, TN)
    weighted = back_normed * gain[...]
    input_out[...] = back_middle[...] + inverse * (
        weighted - unit * jnp.mean(weighted * unit, axis=-1, keepdims=True)
    )
    gain_out[...] += jnp.sum(back_normed * unit, axis=0, keepdims=True)

    @pl.when(pl.program_id(0) == pl.num_programs(0) - 1)
    def _():
        for group in range(GROUPS):
            found = slice(group * LANES, (group + 1) * LANES)
            for index, target in enumerate((kept_out, sent_out)):

                @pl.when(info[group] == index)
                def _():
                    target[homes[group]] = sum_ref[found]


def shaped(shape, kind=F32):
    return jax.ShapeDtypeStruct(shape, kind)


def call(kernel, grid, in_specs, out_specs, out_shape, scratch, operands, prefetch, flops, moved):
    return pl.pallas_call(
        kernel,
        grid_spec=pltpu.PrefetchScalarGridSpec(
            num_scalar_prefetch=prefetch,
            grid=grid,
            in_specs=in_specs,
            out_specs=out_specs,
            scratch_shapes=scratch,
        ),
        out_shape=out_shape,
        compiler_params=pltpu.CompilerParams(
            vmem_limit_bytes=VMEM_LIMIT, dimension_semantics=("arbitrary",) * len(grid)
        ),
        cost_estimate=pl.CostEstimate(flops=flops, bytes_accessed=moved, transcendentals=0),
    )(*operands)


def from_behind(value, axis, steps):
    count = lax.axis_size(axis)
    first, last = (max(0, -steps), min(count, count - steps))
    return lax.ppermute(value, axis, [(source, source + steps) for source in range(first, last)])


def carry(local, decay, steps):
    incoming = jnp.zeros_like(local)
    for _ in range(lax.axis_size("ctx") - 1):
        incoming = from_behind(decay * incoming + local, "ctx", steps)
    return incoming


def staged():
    return lax.axis_size("dp") == 4 and lax.axis_size("ctx") == 2


def swap(value, axis, distance):
    count = lax.axis_size(axis)
    return lax.ppermute(value, axis, [(source, source ^ distance) for source in range(count)])


def shift(value, axis, distance):
    count = lax.axis_size(axis)
    return lax.ppermute(
        value, axis, [(source, (source + distance) % count) for source in range(count)]
    )


def gather_plain(pack):
    rows = pack.shape[0]
    whole = lax.all_gather(lax.all_gather(pack, "tp"), ("dp", "ctx"), axis=2, tiled=True)
    return whole.reshape(whole.shape[0], rows, GROUPS, LANES).transpose(2, 0, 1, 3)


def gather_line(pack):
    count = lax.axis_size("tp")
    return jnp.stack([pack] + [shift(pack, "tp", distance) for distance in range(1, count)])


def gather_square(line):
    return [line] + [swap(line, "dp", distance) for distance in range(1, 4)]


def gather_slots(key_pack, query_pack):
    key_line = gather_line(key_pack)
    query_pack, key_line = lax.optimization_barrier((query_pack, key_line))
    key_first = jnp.stack(gather_square(key_line))
    query_line = gather_line(query_pack)
    query_line, key_first = lax.optimization_barrier((query_line, key_first))
    return key_first, swap(key_first, "ctx", 1), gather_square(query_line)


def gather_pair(pack):
    whole = gather_plain(pack)
    half = GROUPS // 2
    return whole[:half], whole[half:]


def gather_homes():
    if staged():
        return [group // 2 for group in range(GROUPS)]
    return [group % (GROUPS // 2) for group in range(GROUPS)]


def gather_info():
    count = lax.axis_size("tp")
    own = lax.axis_index("tp")
    group = jnp.arange(GROUPS, dtype=jnp.int32)
    heads = jnp.arange(count, dtype=jnp.int32)
    if staged():
        which = (group % 2) ^ lax.axis_index("ctx")
        place = (group // 2) ^ lax.axis_index("dp")
        slot = lax.rem(own - heads + count, count)
    else:
        which, place, slot = group // (GROUPS // 2), group % (GROUPS // 2), heads
    return jnp.concatenate([which, place, slot, own.reshape(1)]).astype(jnp.int32)


def gather_whole(pack):
    if staged():
        rows, share = pack.shape
        whole = lax.all_gather(pack, ("dp", "ctx", "tp"))
        return whole.reshape(-1, lax.axis_size("tp"), rows, share)
    return gather_plain(pack)


def scatter_rows(kept, sent, early):
    columns = kept.shape[-1]
    if not staged():
        whole = jnp.concatenate([kept, sent]).reshape(-1, columns)
        return lax.psum_scatter(whole, ("dp", "ctx"), scatter_dimension=0, tiled=True), early
    device = lax.axis_index("dp")
    row, column = device // 2, device % 2

    def pick(array, axis, index):
        return lax.dynamic_index_in_dim(array, index, axis, keepdims=False)

    value = kept + swap(sent, "ctx", 1)
    value, early = lax.optimization_barrier((value, early))
    value = value.reshape(2, 2, LANES, columns)
    half = LANES // 2
    upper, lower = value[:, :, :half], value[:, :, half:]
    upper = pick(upper, 1, column) + swap(pick(upper, 1, 1 - column), "dp", 1)
    lower = pick(lower, 0, row) + swap(pick(lower, 0, 1 - row), "dp", 2)
    upper = pick(upper, 0, row) + swap(pick(upper, 0, 1 - row), "dp", 2)
    lower = pick(lower, 0, column) + swap(pick(lower, 0, 1 - column), "dp", 1)
    return jnp.concatenate([upper, lower]), early


def total_over(value):
    if not staged():
        return lax.psum(value, ("dp", "ctx"))
    for axis, distance in (("ctx", 1), ("dp", 1), ("dp", 2)):
        value = value + swap(value, axis, distance)
    return value


def adamw(weight_now, grad_now, mean_now, square_now, rate_value, decay_value):
    mean_new = BETA_ONE * mean_now + (1.0 - BETA_ONE) * grad_now
    square_new = BETA_TWO * square_now + (1.0 - BETA_TWO) * grad_now * grad_now
    mean_hat = mean_new / (1.0 - BETA_ONE**STEP)
    square_hat = square_new / (1.0 - BETA_TWO**STEP)
    weight_new = weight_now - rate_value * (
        mean_hat / (jnp.sqrt(square_hat) + ADAM_EPS) + decay_value * weight_now
    )
    return (mean_new, square_new, weight_new)


def three_parts(value):
    high = lax.reduce_precision(value, 8, 7)
    rest = value - high
    middle = lax.reduce_precision(rest, 8, 7)
    low = lax.reduce_precision(rest - middle, 8, 7)
    return [part.astype(BF16) for part in (high, middle, low)]


def body(
    tokens,
    cotangent,
    lengths,
    query_key_weight,
    query_key_mean,
    query_key_square,
    value_gate_weight,
    value_gate_mean,
    value_gate_square,
    decay_in_weight,
    decay_in_mean,
    decay_in_square,
    decay_out_weight,
    decay_out_mean,
    decay_out_square,
    decay_bias,
    decay_bias_mean,
    decay_bias_square,
    output_weight,
    output_mean,
    output_square,
    gate_up_weight,
    gate_up_mean,
    gate_up_square,
    down_weight,
    down_mean,
    down_square,
    gains,
    gains_mean,
    gains_square,
):
    rows, width = tokens.shape
    heads = lax.axis_size("tp")
    ranks = decay_in_weight.shape[1]
    units = down_weight.shape[0]
    steps = rows // ROWS
    info = gather_info()
    gain_one = gains[:width].reshape(1, width)
    gain_two = gains[width : 2 * width].reshape(1, width)
    gain_head = gains[2 * width :].reshape(1, HV)
    size = HK + HV

    small = jnp.concatenate(
        [
            decay_out_weight,
            decay_bias.reshape(1, HK),
            jnp.zeros((DECAY_ROWS - ranks - 1, HK), F32),
        ]
    )
    key_parts = [
        query_key_weight[1].T.astype(BF16),
        value_gate_weight[0].T.astype(BF16),
        decay_in_weight.T.astype(BF16),
    ]
    query_pack = jnp.concatenate(
        [query_key_weight[0].T, value_gate_weight[1].T, output_weight]
    ).astype(BF16)
    if staged():
        key_first, key_second, query_square = gather_slots(
            jnp.concatenate(key_parts + three_parts(small)), query_pack
        )
        sent = key_first[0, :, size + ranks :].astype(F32).reshape(heads, 3, DECAY_ROWS, HK)
        decay_out_full = sent[:, 0] + sent[:, 1] + sent[:, 2]
    else:
        key_first, key_second = gather_pair(jnp.concatenate(key_parts))
        query_first, query_second = gather_pair(query_pack)
        decay_out_full = lax.all_gather(small, "tp")
    ffn = gather_whole(
        jnp.concatenate([gate_up_weight[0].T, gate_up_weight[1].T, down_weight]).astype(BF16)
    )

    position = lax.axis_index("ctx") * rows + jnp.arange(rows, dtype=jnp.int32)
    back_ffn = jnp.where((position < lengths[0])[:, None], cotangent, jnp.zeros_like(cotangent))

    columns = 2 * size
    row_spec = pl.BlockSpec((ROWS, width), lambda i, *_: (i, 0))
    gain_spec = pl.BlockSpec((1, width), lambda i, *_: (0, 0))
    head_gain_spec = pl.BlockSpec((1, HV), lambda i, *_: (0, 0))
    state_spec = pl.BlockSpec((heads, HV, HK), lambda i, *_: (0, 0, 0))
    bias_spec = pl.BlockSpec((heads, 1, HK), lambda i, *_: (0, 0, 0))

    def fixed(array):
        return pl.BlockSpec(
            array.shape, lambda i, *_: (0,) * len(array.shape), pipeline_mode=pl.Buffered(1)
        )

    def by_head(length, reverse=False):
        if reverse:
            return pl.BlockSpec((heads, ROWS, length), lambda i, *_: (0, steps - 1 - i, 0))
        return pl.BlockSpec((heads, ROWS, length), lambda i, *_: (0, i, 0))

    weight_shape = shaped((heads * size, width), BF16)
    rank_shape = shaped((ranks, width), BF16)
    out_weight_shape = shaped((heads * HV, width), BF16)
    parts = ROWS // BLOCK
    normed, kv, rank, logits, cum, local_state, local_total, key_weight, rank_weight = call(
        project_kernel,
        (steps,),
        [row_spec, gain_spec, fixed(key_first), fixed(key_second), fixed(decay_out_full)],
        [
            row_spec,
            by_head(size),
            pl.BlockSpec((ROWS, ranks), lambda i, *_: (i, 0)),
            by_head(HK),
            by_head(HK),
            state_spec,
            bias_spec,
            fixed(weight_shape),
            fixed(rank_shape),
        ],
        [
            shaped((rows, width), BF16),
            shaped((heads, rows, size)),
            shaped((rows, ranks)),
            shaped((heads, rows, HK)),
            shaped((heads, rows, HK)),
            shaped((heads, HV, HK)),
            shaped((heads, 1, HK)),
            weight_shape,
            rank_shape,
        ],
        [],
        (info, tokens, gain_one, key_first, key_second, decay_out_full),
        1,
        2 * rows * width * size * heads,
        rows * heads * 4 * 1024,
    )
    if staged():
        query_square, local_state = lax.optimization_barrier((query_square, local_state))
        query_first = jnp.stack(query_square)
        query_second = swap(query_first, "ctx", 1)
    device_decay = jnp.exp(local_total)
    start_state = carry(local_state, device_decay, 1)

    query, out_gate, mixed, states, gated_own, middle, normed_two, query_weight, out_weight = call(
        mix_kernel,
        (steps,),
        [
            row_spec,
            row_spec,
            by_head(size),
            by_head(HK),
            state_spec,
            fixed(query_first),
            fixed(query_second),
            head_gain_spec,
            gain_spec,
        ],
        [
            by_head(HK),
            by_head(HV),
            by_head(HV),
            pl.BlockSpec((parts, heads, HV, HK), lambda i, *_: (i, 0, 0, 0)),
            pl.BlockSpec((ROWS, HV), lambda i, *_: (i, 0)),
            row_spec,
            row_spec,
            fixed(weight_shape),
            fixed(out_weight_shape),
        ],
        [
            shaped((heads, rows, HK)),
            shaped((heads, rows, HV)),
            shaped((heads, rows, HV)),
            shaped((steps * parts, heads, HV, HK)),
            shaped((rows, HV), BF16),
            shaped((rows, width)),
            shaped((rows, width), BF16),
            weight_shape,
            out_weight_shape,
        ],
        [pltpu.VMEM((heads, HV, HK), F32), pltpu.VMEM((ROWS, heads * HV), BF16)],
        (
            info, tokens, normed, kv, cum, start_state, query_first, query_second,
            gain_head, gain_two,
        ),
        1,
        2 * rows * width * (size + 2 * HV) * heads,
        rows * heads * 4 * 1024,
    )

    wide_spec = pl.BlockSpec((FFN_ROWS, width), lambda i, j, *_: (i, 0))
    own_spec = pl.BlockSpec((FFN_ROWS, units), lambda i, j, *_: (i, 0))
    wide_gain_spec = pl.BlockSpec((1, width), lambda i, j, *_: (0, 0))
    active, back_gate, back_up, layer_out, back_middle, back_attn, gain_two_part = call(
        functools.partial(ffn_kernel, heads),
        (rows // FFN_ROWS, heads),
        [
            wide_spec,
            wide_spec,
            wide_spec,
            pl.BlockSpec((GROUPS, 1, 3 * units, LANES), lambda i, j, *_: (0, j, 0, 0)),
            wide_gain_spec,
        ],
        [own_spec, own_spec, own_spec, wide_spec, wide_spec, wide_spec, wide_gain_spec],
        [
            shaped((rows, units), BF16),
            shaped((rows, units), BF16),
            shaped((rows, units), BF16),
            shaped((rows, width), BF16),
            shaped((rows, width)),
            shaped((rows, width), BF16),
            shaped((1, width)),
        ],
        [
            pltpu.VMEM((FFN_ROWS, width), F32),
            pltpu.VMEM((FFN_ROWS, width), F32),
            pltpu.VMEM((FFN_ROWS, units), BF16),
            pltpu.VMEM((FFN_ROWS, units), BF16),
            pltpu.VMEM((FFN_ROWS, units), BF16),
        ],
        (info, normed_two, back_ffn, middle, ffn, gain_two),
        1,
        12 * rows * width * units * heads,
        rows * width * 24,
    )
    early_grad = jnp.concatenate(
        [
            dot(back_gate, normed_two, TN),
            dot(back_up, normed_two, TN),
            dot(active, back_ffn, TN),
            dot(gated_own, back_attn, TN),
        ]
    )
    early_grad, back_attn = lax.optimization_barrier((early_grad, back_attn))
    early_share = lax.psum_scatter(early_grad, ("dp", "ctx"), scatter_dimension=1, tiled=True)

    back_row_spec = pl.BlockSpec((ROWS, width), lambda i, *_: (steps - 1 - i, 0))
    back_mixed, back_out_gate, head_gain_part, collected = call(
        gate_back_kernel,
        (steps,),
        [
            back_row_spec,
            fixed(out_weight),
            by_head(HV, True),
            by_head(HV, True),
            by_head(HK, True),
            by_head(HK, True),
            head_gain_spec,
        ],
        [by_head(HV, True), by_head(HV, True), head_gain_spec, state_spec],
        [
            shaped((heads, rows, HV)),
            shaped((heads, rows, HV), BF16),
            shaped((1, HV)),
            shaped((heads, HV, HK)),
        ],
        [],
        (back_attn, out_weight, mixed, out_gate, query, cum, gain_head),
        0,
        2 * rows * width * HV * heads,
        rows * heads * 4 * 1024,
    )
    back_end = carry(collected, device_decay, -1)

    grad_shape = shaped((GROUPS // 2, LANES, columns))
    rank_grad_shape = shaped((ranks, width))
    kept, sent_away, rank_grad, input_grad, decay_out_grad, bias_grad, gain_one_part = call(
        functools.partial(mix_back_kernel, gather_homes()),
        (steps,),
        [
            back_row_spec,
            back_row_spec,
            by_head(HK, True),
            by_head(size, True),
            by_head(HK, True),
            by_head(HK, True),
            pl.BlockSpec((parts, heads, HV, HK), lambda i, *_: (steps - 1 - i, 0, 0, 0)),
            by_head(HV, True),
            by_head(HV, True),
            state_spec,
            fixed(query_weight),
            fixed(key_weight),
            fixed(rank_weight),
            fixed(decay_out_full),
            pl.BlockSpec((ROWS, ranks), lambda i, *_: (steps - 1 - i, 0)),
            gain_spec,
        ],
        [
            fixed(grad_shape),
            fixed(grad_shape),
            fixed(rank_grad_shape),
            back_row_spec,
            pl.BlockSpec((heads, ranks, HK), lambda i, *_: (0, 0, 0)),
            bias_spec,
            gain_spec,
        ],
        [
            grad_shape,
            grad_shape,
            rank_grad_shape,
            shaped((rows, width)),
            shaped((heads, ranks, HK)),
            shaped((heads, 1, HK)),
            shaped((1, width)),
        ],
        [
            pltpu.VMEM((heads, HV, HK), F32),
            pltpu.VMEM((ROWS, heads * size), BF16),
            pltpu.VMEM((ROWS, heads * size), BF16),
            pltpu.VMEM((ROWS, columns), BF16),
            pltpu.VMEM((ROWS, ranks), BF16),
            pltpu.VMEM((width, columns), F32),
        ],
        (
            info, tokens, back_middle, query, kv, cum, logits, states, back_mixed, back_out_gate,
            back_end, query_weight, key_weight, rank_weight, decay_out_full, rank, gain_one,
        ),
        1,
        2 * rows * width * columns * heads * 2,
        rows * heads * 4 * 2048,
    )
    mixer_share, early_share = scatter_rows(kept, sent_away, early_share)
    own = info[-1]
    decay_out_own = lax.dynamic_index_in_dim(decay_out_grad, own, 0, keepdims=False)
    bias_own = lax.dynamic_index_in_dim(bias_grad, own, 0, keepdims=False)
    sums = total_over(
        jnp.concatenate(
            [
                gain_one_part.reshape(-1),
                gain_two_part.reshape(-1),
                head_gain_part.reshape(-1),
                bias_own.reshape(-1),
                decay_out_own.reshape(-1),
                rank_grad.reshape(-1),
            ]
        )
    )
    gain_count = gains.shape[0]
    decay_start = gain_count + HK
    rank_start = decay_start + ranks * HK
    gains_grad = sums[:gain_count]
    bias_total = sums[gain_count:decay_start]
    decay_out_total = sums[decay_start:rank_start].reshape(ranks, HK)
    share = decay_in_weight.shape[0]
    place = (lax.axis_index("dp") * lax.axis_size("ctx") + lax.axis_index("ctx")) * share
    decay_in_share = lax.dynamic_slice_in_dim(
        sums[rank_start:].reshape(ranks, width), place, share, axis=1
    ).T

    query_key_share = jnp.stack([mixer_share[:, :HK], mixer_share[:, size : size + HK]])
    value_gate_share = jnp.stack([mixer_share[:, size + HK : columns], mixer_share[:, HK:size]])
    gate_up_share = jnp.stack([early_share[:units].T, early_share[units : 2 * units].T])
    down_share = early_share[2 * units : 3 * units]
    output_share = early_share[3 * units :]

    updated = adamw(
        query_key_weight,
        query_key_share,
        query_key_mean,
        query_key_square,
        RATE_MATRIX,
        WEIGHT_DECAY,
    )
    updated = updated + adamw(
        value_gate_weight,
        value_gate_share,
        value_gate_mean,
        value_gate_square,
        RATE_MATRIX,
        WEIGHT_DECAY,
    )
    updated = updated + adamw(
        decay_in_weight, decay_in_share, decay_in_mean, decay_in_square, RATE_MATRIX, WEIGHT_DECAY
    )
    updated = updated + adamw(
        decay_out_weight, decay_out_total, decay_out_mean, decay_out_square, RATE_RANK, WEIGHT_DECAY
    )
    updated = updated + adamw(
        decay_bias, bias_total, decay_bias_mean, decay_bias_square, RATE_BIAS, 0.0
    )
    updated = updated + adamw(
        output_weight, output_share, output_mean, output_square, RATE_MATRIX, WEIGHT_DECAY
    )
    updated = updated + adamw(
        gate_up_weight, gate_up_share, gate_up_mean, gate_up_square, RATE_MATRIX, WEIGHT_DECAY
    )
    updated = updated + adamw(
        down_weight, down_share, down_mean, down_square, RATE_MATRIX, WEIGHT_DECAY
    )
    updated = updated + adamw(gains, gains_grad, gains_mean, gains_square, RATE_GAIN, 0.0)
    return (layer_out, input_grad) + updated


def solution(mesh):
    tokens_at = P(("dp", "ctx"), None)
    split_at = P(None, ("dp", "ctx"), "tp")
    deep_at = P("tp", ("dp", "ctx"))
    rank_out_at = P(None, "tp")
    kinds = (split_at, split_at, tokens_at, rank_out_at, P("tp"), deep_at, split_at, deep_at, P())
    params = tuple(kind for kind in kinds for _ in range(3))
    return jax.shard_map(
        body,
        mesh=mesh,
        in_specs=(tokens_at, tokens_at, P("dp")) + params,
        out_specs=(tokens_at, tokens_at) + params,
        check_vma=False,
    )
```

```python
import functools

import jax
import jax.numpy as jnp
from jax import lax
from jax.experimental import pallas as pl
from jax.experimental.pallas import tpu as pltpu
from jax.sharding import PartitionSpec as P

HK = 128
HV = 256
BLOCK = 128
LANES = 128
GROUPS = 8
MID = 63
DECAY_ROWS = 32
ROWS = 256
FFN_ROWS = 512
STEP = 10

NORM_EPS = 1e-06
HEAD_EPS = 1e-05
GATE_SCALE = 16.0
BETA_ONE = 0.9
BETA_TWO = 0.95
ADAM_EPS = 1e-08
WEIGHT_DECAY = 0.1
RATE_MATRIX = 0.03
RATE_RANK = 0.1
RATE_BIAS = 1.5
RATE_GAIN = 0.3
VMEM_LIMIT = 62 * 1024 * 1024

F32 = jnp.float32
BF16 = jnp.bfloat16
NN = (((1,), (0,)), ((), ()))
NT = (((1,), (1,)), ((), ()))
TN = (((0,), (0,)), ((), ()))


def dot(left, right, dims=NN):
    return lax.dot_general(left, right, dims, preferred_element_type=F32)


def split_two(values):
    high = values.astype(BF16)
    return high, (values - high.astype(F32)).astype(BF16)


def dot_split(left, right, dims=NN):
    axis = 1 - dims[0][0][0]
    size = left[0].shape[axis]
    both = dot(jnp.concatenate(left, axis=axis), right[0], dims)
    return both[:size] + both[size:] + dot(left[0], right[1], dims)


def dot_exact(matrix, values):
    high = values.astype(BF16)
    rest = values - high.astype(F32)
    middle = rest.astype(BF16)
    low = (rest - middle.astype(F32)).astype(BF16)
    return dot(matrix, high) + dot(matrix, middle) + dot(matrix, low)


def lower_mask():
    rows = lax.broadcasted_iota(jnp.int32, (BLOCK, BLOCK), 0)
    columns = lax.broadcasted_iota(jnp.int32, (BLOCK, BLOCK), 1)
    return rows >= columns


def upper_mask():
    rows = lax.broadcasted_iota(jnp.int32, (BLOCK, BLOCK), 0)
    columns = lax.broadcasted_iota(jnp.int32, (BLOCK, BLOCK), 1)
    return rows <= columns


def as_ones(mask):
    return jnp.where(mask, 1.0, 0.0).astype(BF16)


def inverse_rms(values, epsilon):
    return lax.rsqrt(jnp.mean(values * values, axis=-1, keepdims=True) + epsilon)


def sigmoid(values):
    return 0.5 + 0.5 * jnp.tanh(0.5 * values)


def fill(info, first, second, pieces):
    heads = first.shape[1]
    for head in range(heads):
        slot = info[2 * GROUPS + head]
        for group in range(GROUPS):
            lanes = slice(group * LANES, (group + 1) * LANES)
            place = info[GROUPS + group]
            for source_index, source in enumerate((first, second)):

                @pl.when(info[group] == source_index)
                def _():
                    for target, start, count in pieces:
                        if target.shape[0] == count and head > 0:
                            continue
                        at = head * count
                        target[at : at + count, lanes] = source[
                            place, slot, start : start + count
                        ]


def project_kernel(
    info, tokens, gain, first, second, decay_out,
    normed_out, kv_out, rank_out, logits_out, cum_out, state_out, total_out, weight, rank_weight,
):
    heads = first.shape[1]
    size = HK + HV
    ranks = rank_out.shape[1]

    @pl.when(pl.program_id(0) == 0)
    def _():
        state_out[...] = jnp.zeros_like(state_out)
        total_out[...] = jnp.zeros_like(total_out)
        fill(info, first, second, ((weight, 0, size), (rank_weight, size, ranks)))

    inputs = tokens[...].astype(F32)
    normed = (inputs * inverse_rms(inputs, NORM_EPS) * gain[...]).astype(BF16)
    normed_out[...] = normed
    rank = dot(normed, rank_weight[...], NT)
    rank_out[...] = rank
    lower = as_ones(lower_mask())
    made = dot(normed, weight[...], NT)
    every = range(heads)
    keys = [made[:, head * size : head * size + HK] for head in every]
    values = [made[:, head * size + HK : (head + 1) * size] for head in every]
    logits = []
    for head in every:
        slot = info[2 * GROUPS + head]
        logits.append(
            lax.dot_general(
                rank, decay_out[slot, :ranks], NN, precision=lax.Precision.HIGHEST,
                preferred_element_type=F32,
            )
            + decay_out[slot, ranks : ranks + 1]
        )
    for head in every:
        kv_out[head, :, :HK] = keys[head]
        kv_out[head, :, HK:] = values[head]
        logits_out[head] = logits[head]
    log_decay = [
        (jnp.minimum(item, 0.0) - jnp.log1p(jnp.exp(-jnp.abs(item)))) / GATE_SCALE
        for item in logits
    ]
    for part in range(ROWS // BLOCK):
        span = slice(part * BLOCK, (part + 1) * BLOCK)
        cum = [dot_exact(lower, log_decay[head][span]) for head in every]
        total = [item[BLOCK - 1 :] for item in cum]
        carried = [
            split_two(keys[head][span] * jnp.exp(total[head] - cum[head])) for head in every
        ]
        value_parts = [split_two(values[head][span]) for head in every]
        added = [dot_split(value_parts[head], carried[head], TN) for head in every]
        for head in every:
            cum_out[head, span] = cum[head]
            state_out[head] = state_out[head] * jnp.exp(total[head]) + added[head]
            total_out[head] += total[head]


def mix_kernel(
    info, tokens, normed, kv, cum_in, start, first, second, head_gain, gain,
    query_out, gate_out, mixed_out, state_out, gated_out, middle_out, normed_out, weight, out_weight,
    state_ref, gated_ref,
):
    heads = start.shape[0]
    size = HK + HV

    @pl.when(pl.program_id(0) == 0)
    def _():
        state_ref[...] = start[...]
        fill(info, first, second, ((weight, 0, size), (out_weight, size, HV)))

    made = dot(normed[...], weight[...], NT)
    causal = lower_mask()
    every = range(heads)
    for part in range(ROWS // BLOCK):
        span = slice(part * BLOCK, (part + 1) * BLOCK)
        query = [made[span, head * size : head * size + HK] * HK ** (-0.5) for head in every]
        out_gate = [made[span, head * size + HK : (head + 1) * size] for head in every]
        keys = [kv[head, span, :HK] for head in every]
        cum = [cum_in[head, span] for head in every]
        center = [item[MID : MID + 1] for item in cum]
        total = [item[BLOCK - 1 :] for item in cum]
        query_mid = [split_two(query[head] * jnp.exp(cum[head] - center[head])) for head in every]
        key_mid = [split_two(keys[head] * jnp.exp(center[head] - cum[head])) for head in every]
        scores = [dot_split(query_mid[head], key_mid[head], NT) for head in every]
        since = [split_two(query[head] * jnp.exp(cum[head])) for head in every]
        states = [state_ref[head] for head in every]
        carried = [split_two(keys[head] * jnp.exp(total[head] - cum[head])) for head in every]
        values = [split_two(kv[head, span, HK:]) for head in every]
        outer = [dot_split(since[head], split_two(states[head]), NT) for head in every]
        added = [dot_split(values[head], carried[head], TN) for head in every]
        scores = [split_two(jnp.where(causal, item, 0.0)) for item in scores]
        mixed = [dot_split(scores[head], values[head]) + outer[head] for head in every]
        for head in every:
            query_out[head, span] = query[head]
            gate_out[head, span] = out_gate[head]
            state_out[part, head] = states[head]
            state_ref[head] = states[head] * jnp.exp(total[head]) + added[head]
            mixed_out[head, span] = mixed[head]
        for head in every:
            gated_ref[span, head * HV : (head + 1) * HV] = (
                mixed[head]
                * inverse_rms(mixed[head], HEAD_EPS)
                * head_gain[...]
                * (out_gate[head] * sigmoid(out_gate[head]))
            ).astype(BF16)

    for head in every:

        @pl.when(info[2 * GROUPS + heads] == head)
        def _():
            gated_out[...] = gated_ref[:, head * HV : (head + 1) * HV]

    middle = tokens[...].astype(F32) + dot(gated_ref[...], out_weight[...])
    middle_out[...] = middle
    normed_out[...] = (middle * inverse_rms(middle, NORM_EPS) * gain[...]).astype(BF16)


def ffn_kernel(
    info, normed, back, middle, weight, gain,
    active_out, back_gate_out, back_up_out, layer_out, back_middle_out, back_attn_out, gain_out,
    ffn_ref, back_ref, turned_ref, active_ref, back_gate_ref, back_up_ref,
):
    piece, step = pl.program_id(0), pl.program_id(1)
    pieces = pl.num_programs(0)
    units = weight.shape[2] // 3
    count = normed.shape[0]
    rows = pl.ds(pl.multiple_of(step * count, count), count)

    @pl.when((step == 0) & (piece == 0))
    def _():
        gain_out[...] = jnp.zeros_like(gain_out)
        ffn_ref[...] = jnp.zeros_like(ffn_ref)
        back_ref[...] = jnp.zeros_like(back_ref)

    @pl.when(step == 0)
    def _():
        for kind in range(3):
            for group in range(GROUPS):
                turned_ref[kind, group * LANES : (group + 1) * LANES] = weight[
                    group, 0, kind * units : (kind + 1) * units
                ].T

    def rows_of(start):
        return jnp.concatenate(
            [weight[group, 0, start : start + units] for group in range(GROUPS)], axis=1
        )

    gate_values = dot(normed[...], turned_ref[0])
    upward = dot(normed[...], turned_ref[1])
    back_active = dot(back[...], turned_ref[2])
    share = sigmoid(gate_values)
    silu = gate_values * share
    active_ref[...] = (silu * upward).astype(BF16)
    back_gate_ref[...] = (
        back_active * upward * (share * (1.0 + gate_values * (1.0 - share)))
    ).astype(BF16)
    back_up_ref[...] = (back_active * silu).astype(BF16)
    ffn_ref[rows] += dot(active_ref[...], rows_of(2 * units))
    back_ref[rows] += dot(back_gate_ref[...], rows_of(0)) + dot(back_up_ref[...], rows_of(units))

    @pl.when(piece == info[2 * GROUPS + pieces])
    def _():
        active_out[...] = active_ref[...]
        back_gate_out[...] = back_gate_ref[...]
        back_up_out[...] = back_up_ref[...]

    @pl.when(piece == pieces - 1)
    def _():
        mid = middle[...]
        layer_out[...] = (mid + ffn_ref[rows]).astype(BF16)
        inverse = inverse_rms(mid, NORM_EPS)
        unit = mid * inverse
        total = back_ref[rows]
        weighted = total * gain[...]
        back_middle = back[...].astype(F32) + inverse * (
            weighted - unit * jnp.mean(weighted * unit, axis=-1, keepdims=True)
        )
        back_middle_out[...] = back_middle
        back_attn_out[...] = back_middle.astype(BF16)
        gain_out[...] += jnp.sum(total * unit, axis=0, keepdims=True)


def gate_back_kernel(
    back_attn, out_weight, mixed_in, gate, query_in, cum_in, head_gain,
    back_mixed_out, back_gate_out, gain_out, state_out,
):
    heads = gate.shape[0]

    @pl.when(pl.program_id(0) == 0)
    def _():
        gain_out[...] = jnp.zeros_like(gain_out)
        state_out[...] = jnp.zeros_like(state_out)

    every = range(heads)
    back_gated = [
        dot(back_attn[...], out_weight[head * HV : (head + 1) * HV], NT) for head in every
    ]
    scaled = [query_in[head] * jnp.exp(cum_in[head]) for head in every]
    back_mixed = []
    for head in every:
        mixed = mixed_in[head]
        out_gate = gate[head]
        inverse = inverse_rms(mixed, HEAD_EPS)
        unit = mixed * inverse
        share = sigmoid(out_gate)
        silu = out_gate * share
        slope = share * (1.0 + out_gate * (1.0 - share))
        shaped_back = back_gated[head] * unit
        back_gate_out[head] = (shaped_back * head_gain[...] * slope).astype(BF16)
        gain_out[...] += jnp.sum(shaped_back * silu, axis=0, keepdims=True)
        weighted = back_gated[head] * head_gain[...] * silu
        item = inverse * (weighted - unit * jnp.mean(weighted * unit, axis=-1, keepdims=True))
        back_mixed_out[head] = item
        back_mixed.append(item)
    for part in reversed(range(ROWS // BLOCK)):
        span = slice(part * BLOCK, (part + 1) * BLOCK)
        added = [
            dot_split(split_two(back_mixed[head][span]), split_two(scaled[head][span]), TN)
            for head in every
        ]
        for head in every:
            last = cum_in[head, (part + 1) * BLOCK - 1 : (part + 1) * BLOCK]
            state_out[head] = state_out[head] * jnp.exp(last) + added[head]


def mix_back_kernel(
    homes, info, tokens, back_middle, query_in, kv, cum_in, logits_in, states, back_mixed, back_gate,
    back_end, query_weight, key_weight, rank_weight, decay_out, rank, gain,
    kept_out, sent_out, rank_grad_out, input_out, decay_grad_out, bias_out, gain_out,
    state_ref, query_ref, key_ref, grad_ref, rank_ref, sum_ref,
):
    heads = back_end.shape[0]
    size = HK + HV
    ranks = rank.shape[1]

    @pl.when(pl.program_id(0) == 0)
    def _():
        state_ref[...] = back_end[...]
        sum_ref[...] = jnp.zeros_like(sum_ref)
        rank_grad_out[...] = jnp.zeros_like(rank_grad_out)
        decay_grad_out[...] = jnp.zeros_like(decay_grad_out)
        bias_out[...] = jnp.zeros_like(bias_out)
        gain_out[...] = jnp.zeros_like(gain_out)

    causal = lower_mask()
    upper = as_ones(upper_mask())
    every = range(heads)
    for part in reversed(range(ROWS // BLOCK)):
        span = slice(part * BLOCK, (part + 1) * BLOCK)
        query = [query_in[head, span] for head in every]
        keys = [kv[head, span, :HK] for head in every]
        cum = [cum_in[head, span] for head in every]
        center = [item[MID : MID + 1] for item in cum]
        total = [item[BLOCK - 1 :] for item in cum]
        grow = [jnp.exp(cum[head] - center[head]) for head in every]
        shrink = [jnp.exp(center[head] - cum[head]) for head in every]
        query_mid = [split_two(query[head] * grow[head]) for head in every]
        key_mid = [split_two(keys[head] * shrink[head]) for head in every]
        values = [split_two(kv[head, span, HK:]) for head in every]
        back = [split_two(back_mixed[head, span]) for head in every]
        scores = [dot_split(query_mid[head], key_mid[head], NT) for head in every]
        back_scores = [dot_split(back[head], values[head], NT) for head in every]
        since = [jnp.exp(cum[head]) for head in every]
        until = [jnp.exp(total[head] - cum[head]) for head in every]
        carried = [keys[head] * until[head] for head in every]
        back_state = [state_ref[head] for head in every]
        back_state_parts = [split_two(item) for item in back_state]
        back_carried = [dot_split(values[head], back_state_parts[head]) for head in every]
        back_since = [dot_split(back[head], split_two(states[part, head])) for head in every]
        added = [
            dot_split(back[head], split_two(query[head] * since[head]), TN) for head in every
        ]
        outer = [
            dot_split(split_two(carried[head]), back_state_parts[head], NT) for head in every
        ]
        scores = [split_two(jnp.where(causal, item, 0.0)) for item in scores]
        back_scores = [split_two(jnp.where(causal, item, 0.0)) for item in back_scores]
        back_query = [
            dot_split(back_scores[head], key_mid[head]) * grow[head]
            + back_since[head] * since[head]
            for head in every
        ]
        back_keys = [
            dot_split(back_scores[head], query_mid[head], TN) * shrink[head]
            + back_carried[head] * until[head]
            for head in every
        ]
        back_values = [dot_split(scores[head], back[head], TN) + outer[head] for head in every]
        back_total = []
        for head in every:
            decayed = back_state[head] * jnp.exp(total[head])
            back_total.append(
                jnp.sum(back_carried[head] * carried[head], axis=0, keepdims=True)
                + jnp.sum(decayed * states[part, head], axis=0, keepdims=True)
            )
            state_ref[head] = decayed + added[head]
        back_logits = [
            (
                dot_exact(upper, query[head] * back_query[head] - keys[head] * back_keys[head])
                + back_total[head]
            )
            * sigmoid(-logits_in[head, span])
            / GATE_SCALE
            for head in every
        ]
        rank_parts = split_two(rank[span])
        rank_back = jnp.zeros((BLOCK, ranks), F32)
        for head in every:
            slot = info[2 * GROUPS + head]
            rank_back += lax.dot_general(
                back_logits[head], decay_out[slot, :ranks], NT, precision=lax.Precision.HIGHEST,
                preferred_element_type=F32,
            )
            bias_out[head] += jnp.sum(back_logits[head], axis=0, keepdims=True)
            decay_grad_out[head] += dot_split(rank_parts, split_two(back_logits[head]), TN)
            at = head * size
            query_ref[span, at : at + HK] = (back_query[head] * HK ** (-0.5)).astype(BF16)
            query_ref[span, at + HK : at + size] = back_gate[head, span]
            key_ref[span, at : at + HK] = back_keys[head].astype(BF16)
            key_ref[span, at + HK : at + size] = back_values[head].astype(BF16)
        rank_ref[span] = rank_back.astype(BF16)

    for head in every:

        @pl.when(info[2 * GROUPS + heads] == head)
        def _():
            grad_ref[:, :size] = query_ref[:, head * size : (head + 1) * size]
            grad_ref[:, size:] = key_ref[:, head * size : (head + 1) * size]

    back_normed = (
        dot(rank_ref[...], rank_weight[...])
        + dot(query_ref[...], query_weight[...])
        + dot(key_ref[...], key_weight[...])
    )
    inputs = tokens[...].astype(F32)
    inverse = inverse_rms(inputs, NORM_EPS)
    unit = inputs * inverse
    normed = (unit * gain[...]).astype(BF16)
    sum_ref[...] += dot(normed, grad_ref[...], TN)
    rank_grad_out[...] += dot(rank_ref[...], normed, TN)
    weighted = back_normed * gain[...]
    input_out[...] = back_middle[...] + inverse * (
        weighted - unit * jnp.mean(weighted * unit, axis=-1, keepdims=True)
    )
    gain_out[...] += jnp.sum(back_normed * unit, axis=0, keepdims=True)

    @pl.when(pl.program_id(0) == pl.num_programs(0) - 1)
    def _():
        for group in range(GROUPS):
            found = slice(group * LANES, (group + 1) * LANES)
            for index, target in enumerate((kept_out, sent_out)):

                @pl.when(info[group] == index)
                def _():
                    target[homes[group]] = sum_ref[found]


def shaped(shape, kind=F32):
    return jax.ShapeDtypeStruct(shape, kind)


def call(kernel, grid, in_specs, out_specs, out_shape, scratch, operands, prefetch, flops, moved):
    return pl.pallas_call(
        kernel,
        grid_spec=pltpu.PrefetchScalarGridSpec(
            num_scalar_prefetch=prefetch,
            grid=grid,
            in_specs=in_specs,
            out_specs=out_specs,
            scratch_shapes=scratch,
        ),
        out_shape=out_shape,
        compiler_params=pltpu.CompilerParams(
            vmem_limit_bytes=VMEM_LIMIT, dimension_semantics=("arbitrary",) * len(grid)
        ),
        cost_estimate=pl.CostEstimate(flops=flops, bytes_accessed=moved, transcendentals=0),
    )(*operands)


def from_behind(value, axis, steps):
    count = lax.axis_size(axis)
    first, last = (max(0, -steps), min(count, count - steps))
    return lax.ppermute(value, axis, [(source, source + steps) for source in range(first, last)])


def carry(local, decay, steps):
    incoming = jnp.zeros_like(local)
    for _ in range(lax.axis_size("ctx") - 1):
        incoming = from_behind(decay * incoming + local, "ctx", steps)
    return incoming


def staged():
    return lax.axis_size("dp") == 4 and lax.axis_size("ctx") == 2


def swap(value, axis, distance):
    count = lax.axis_size(axis)
    return lax.ppermute(value, axis, [(source, source ^ distance) for source in range(count)])


def shift(value, axis, distance):
    count = lax.axis_size(axis)
    return lax.ppermute(
        value, axis, [(source, (source + distance) % count) for source in range(count)]
    )


def gather_plain(pack):
    rows = pack.shape[0]
    whole = lax.all_gather(lax.all_gather(pack, "tp"), ("dp", "ctx"), axis=2, tiled=True)
    return whole.reshape(whole.shape[0], rows, GROUPS, LANES).transpose(2, 0, 1, 3)


def gather_line(pack):
    count = lax.axis_size("tp")
    return jnp.stack([pack] + [shift(pack, "tp", distance) for distance in range(1, count)])


def gather_square(line):
    return [line] + [swap(line, "dp", distance) for distance in range(1, 4)]


def gather_slots(key_pack, query_pack):
    key_line = gather_line(key_pack)
    query_pack, key_line = lax.optimization_barrier((query_pack, key_line))
    key_first = jnp.stack(gather_square(key_line))
    query_line = gather_line(query_pack)
    query_line, key_first = lax.optimization_barrier((query_line, key_first))
    return key_first, swap(key_first, "ctx", 1), gather_square(query_line)


def gather_pair(pack):
    whole = gather_plain(pack)
    half = GROUPS // 2
    return whole[:half], whole[half:]


def gather_homes():
    if staged():
        return [group // 2 for group in range(GROUPS)]
    return [group % (GROUPS // 2) for group in range(GROUPS)]


def gather_info():
    count = lax.axis_size("tp")
    own = lax.axis_index("tp")
    group = jnp.arange(GROUPS, dtype=jnp.int32)
    heads = jnp.arange(count, dtype=jnp.int32)
    if staged():
        which = (group % 2) ^ lax.axis_index("ctx")
        place = (group // 2) ^ lax.axis_index("dp")
        slot = lax.rem(own - heads + count, count)
    else:
        which, place, slot = group // (GROUPS // 2), group % (GROUPS // 2), heads
    return jnp.concatenate([which, place, slot, own.reshape(1)]).astype(jnp.int32)


def gather_whole(pack):
    if staged():
        rows, share = pack.shape
        whole = lax.all_gather(pack, ("dp", "ctx", "tp"))
        return whole.reshape(-1, lax.axis_size("tp"), rows, share)
    return gather_plain(pack)


def finish_sums(kept, sent, sums, early):
    columns = kept.shape[-1]
    if not staged():
        whole = jnp.concatenate([kept, sent]).reshape(-1, columns)
        share = lax.psum_scatter(whole, ("dp", "ctx"), scatter_dimension=0, tiled=True)
        return share, lax.psum(sums, ("dp", "ctx")), early
    device = lax.axis_index("dp")
    row, column = device // 2, device % 2

    def pick(array, axis, index):
        return lax.dynamic_index_in_dim(array, index, axis, keepdims=False)

    value = kept + swap(sent, "ctx", 1)
    sums = sums + swap(sums, "ctx", 1)
    value, sums, early = lax.optimization_barrier((value, sums, early))
    value = value.reshape(2, 2, LANES, columns)
    half = LANES // 2
    upper, lower = value[:, :, :half], value[:, :, half:]
    upper = pick(upper, 1, column) + swap(pick(upper, 1, 1 - column), "dp", 1)
    lower = pick(lower, 0, row) + swap(pick(lower, 0, 1 - row), "dp", 2)
    sums = sums + swap(sums, "dp", 1)
    upper, lower, sums = lax.optimization_barrier((upper, lower, sums))
    upper = pick(upper, 0, row) + swap(pick(upper, 0, 1 - row), "dp", 2)
    lower = pick(lower, 0, column) + swap(pick(lower, 0, 1 - column), "dp", 1)
    sums = sums + swap(sums, "dp", 2)
    return jnp.concatenate([upper, lower]), sums, early


def adamw(weight_now, grad_now, mean_now, square_now, rate_value, decay_value):
    mean_new = BETA_ONE * mean_now + (1.0 - BETA_ONE) * grad_now
    square_new = BETA_TWO * square_now + (1.0 - BETA_TWO) * grad_now * grad_now
    mean_hat = mean_new / (1.0 - BETA_ONE**STEP)
    square_hat = square_new / (1.0 - BETA_TWO**STEP)
    weight_new = weight_now - rate_value * (
        mean_hat / (jnp.sqrt(square_hat) + ADAM_EPS) + decay_value * weight_now
    )
    return (mean_new, square_new, weight_new)


def three_parts(value):
    high = lax.reduce_precision(value, 8, 7)
    rest = value - high
    middle = lax.reduce_precision(rest, 8, 7)
    low = lax.reduce_precision(rest - middle, 8, 7)
    return [part.astype(BF16) for part in (high, middle, low)]


def body(
    tokens,
    cotangent,
    lengths,
    query_key_weight,
    query_key_mean,
    query_key_square,
    value_gate_weight,
    value_gate_mean,
    value_gate_square,
    decay_in_weight,
    decay_in_mean,
    decay_in_square,
    decay_out_weight,
    decay_out_mean,
    decay_out_square,
    decay_bias,
    decay_bias_mean,
    decay_bias_square,
    output_weight,
    output_mean,
    output_square,
    gate_up_weight,
    gate_up_mean,
    gate_up_square,
    down_weight,
    down_mean,
    down_square,
    gains,
    gains_mean,
    gains_square,
):
    rows, width = tokens.shape
    heads = lax.axis_size("tp")
    ranks = decay_in_weight.shape[1]
    units = down_weight.shape[0]
    steps = rows // ROWS
    info = gather_info()
    gain_one = gains[:width].reshape(1, width)
    gain_two = gains[width : 2 * width].reshape(1, width)
    gain_head = gains[2 * width :].reshape(1, HV)
    size = HK + HV

    small = jnp.concatenate(
        [
            decay_out_weight,
            decay_bias.reshape(1, HK),
            jnp.zeros((DECAY_ROWS - ranks - 1, HK), F32),
        ]
    )
    key_parts = [
        query_key_weight[1].T.astype(BF16),
        value_gate_weight[0].T.astype(BF16),
        decay_in_weight.T.astype(BF16),
    ]
    query_pack = jnp.concatenate(
        [query_key_weight[0].T, value_gate_weight[1].T, output_weight]
    ).astype(BF16)
    if staged():
        key_first, key_second, query_square = gather_slots(
            jnp.concatenate(key_parts + three_parts(small)), query_pack
        )
        sent = key_first[0, :, size + ranks :].astype(F32).reshape(heads, 3, DECAY_ROWS, HK)
        decay_out_full = sent[:, 0] + sent[:, 1] + sent[:, 2]
    else:
        key_first, key_second = gather_pair(jnp.concatenate(key_parts))
        query_first, query_second = gather_pair(query_pack)
        decay_out_full = lax.all_gather(small, "tp")
    ffn = gather_whole(
        jnp.concatenate([gate_up_weight[0].T, gate_up_weight[1].T, down_weight]).astype(BF16)
    )

    position = lax.axis_index("ctx") * rows + jnp.arange(rows, dtype=jnp.int32)
    back_ffn = jnp.where((position < lengths[0])[:, None], cotangent, jnp.zeros_like(cotangent))

    columns = 2 * size
    row_spec = pl.BlockSpec((ROWS, width), lambda i, *_: (i, 0))
    gain_spec = pl.BlockSpec((1, width), lambda i, *_: (0, 0))
    head_gain_spec = pl.BlockSpec((1, HV), lambda i, *_: (0, 0))
    state_spec = pl.BlockSpec((heads, HV, HK), lambda i, *_: (0, 0, 0))
    bias_spec = pl.BlockSpec((heads, 1, HK), lambda i, *_: (0, 0, 0))

    def fixed(array):
        return pl.BlockSpec(
            array.shape, lambda i, *_: (0,) * len(array.shape), pipeline_mode=pl.Buffered(1)
        )

    def by_head(length, reverse=False):
        if reverse:
            return pl.BlockSpec((heads, ROWS, length), lambda i, *_: (0, steps - 1 - i, 0))
        return pl.BlockSpec((heads, ROWS, length), lambda i, *_: (0, i, 0))

    weight_shape = shaped((heads * size, width), BF16)
    rank_shape = shaped((ranks, width), BF16)
    out_weight_shape = shaped((heads * HV, width), BF16)
    parts = ROWS // BLOCK
    normed, kv, rank, logits, cum, local_state, local_total, key_weight, rank_weight = call(
        project_kernel,
        (steps,),
        [row_spec, gain_spec, fixed(key_first), fixed(key_second), fixed(decay_out_full)],
        [
            row_spec,
            by_head(size),
            pl.BlockSpec((ROWS, ranks), lambda i, *_: (i, 0)),
            by_head(HK),
            by_head(HK),
            state_spec,
            bias_spec,
            fixed(weight_shape),
            fixed(rank_shape),
        ],
        [
            shaped((rows, width), BF16),
            shaped((heads, rows, size)),
            shaped((rows, ranks)),
            shaped((heads, rows, HK)),
            shaped((heads, rows, HK)),
            shaped((heads, HV, HK)),
            shaped((heads, 1, HK)),
            weight_shape,
            rank_shape,
        ],
        [],
        (info, tokens, gain_one, key_first, key_second, decay_out_full),
        1,
        2 * rows * width * size * heads,
        rows * heads * 4 * 1024,
    )
    if staged():
        query_square, local_state = lax.optimization_barrier((query_square, local_state))
        query_first = jnp.stack(query_square)
        query_second = swap(query_first, "ctx", 1)
    device_decay = jnp.exp(local_total)
    start_state = carry(local_state, device_decay, 1)

    query, out_gate, mixed, states, gated_own, middle, normed_two, query_weight, out_weight = call(
        mix_kernel,
        (steps,),
        [
            row_spec,
            row_spec,
            by_head(size),
            by_head(HK),
            state_spec,
            fixed(query_first),
            fixed(query_second),
            head_gain_spec,
            gain_spec,
        ],
        [
            by_head(HK),
            by_head(HV),
            by_head(HV),
            pl.BlockSpec((parts, heads, HV, HK), lambda i, *_: (i, 0, 0, 0)),
            pl.BlockSpec((ROWS, HV), lambda i, *_: (i, 0)),
            row_spec,
            row_spec,
            fixed(weight_shape),
            fixed(out_weight_shape),
        ],
        [
            shaped((heads, rows, HK)),
            shaped((heads, rows, HV)),
            shaped((heads, rows, HV)),
            shaped((steps * parts, heads, HV, HK)),
            shaped((rows, HV), BF16),
            shaped((rows, width)),
            shaped((rows, width), BF16),
            weight_shape,
            out_weight_shape,
        ],
        [pltpu.VMEM((heads, HV, HK), F32), pltpu.VMEM((ROWS, heads * HV), BF16)],
        (
            info, tokens, normed, kv, cum, start_state, query_first, query_second,
            gain_head, gain_two,
        ),
        1,
        2 * rows * width * (size + 2 * HV) * heads,
        rows * heads * 4 * 1024,
    )

    tiles = rows // FFN_ROWS

    def last_only(j, i, info):
        return (jnp.where(j == heads - 1, i, 0), 0)

    def own_only(j, i, info):
        own = info[2 * GROUPS + heads]
        return (jnp.where(j < own, 0, jnp.where(j > own, tiles - 1, i)), 0)

    tile_spec = pl.BlockSpec((FFN_ROWS, width), lambda j, i, *_: (i, 0))
    last_spec = pl.BlockSpec((FFN_ROWS, width), last_only, pipeline_mode=pl.Buffered(1))
    own_spec = pl.BlockSpec((FFN_ROWS, units), own_only, pipeline_mode=pl.Buffered(1))
    tile_gain_spec = pl.BlockSpec((1, width), lambda j, i, *_: (0, 0))
    active, back_gate, back_up, layer_out, back_middle, back_attn, gain_two_part = call(
        ffn_kernel,
        (heads, tiles),
        [
            tile_spec,
            tile_spec,
            last_spec,
            pl.BlockSpec((GROUPS, 1, 3 * units, LANES), lambda j, i, *_: (0, j, 0, 0)),
            tile_gain_spec,
        ],
        [own_spec, own_spec, own_spec, last_spec, last_spec, last_spec, tile_gain_spec],
        [
            shaped((rows, units), BF16),
            shaped((rows, units), BF16),
            shaped((rows, units), BF16),
            shaped((rows, width), BF16),
            shaped((rows, width)),
            shaped((rows, width), BF16),
            shaped((1, width)),
        ],
        [
            pltpu.VMEM((rows, width), F32),
            pltpu.VMEM((rows, width), F32),
            pltpu.VMEM((3, width, units), BF16),
            pltpu.VMEM((FFN_ROWS, units), BF16),
            pltpu.VMEM((FFN_ROWS, units), BF16),
            pltpu.VMEM((FFN_ROWS, units), BF16),
        ],
        (info, normed_two, back_ffn, middle, ffn, gain_two),
        1,
        12 * rows * width * units * heads,
        rows * width * 24,
    )
    early_grad = jnp.concatenate(
        [
            dot(back_gate, normed_two, TN),
            dot(back_up, normed_two, TN),
            dot(active, back_ffn, TN),
            dot(gated_own, back_attn, TN),
        ]
    )
    early_grad, back_attn = lax.optimization_barrier((early_grad, back_attn))
    early_share = lax.psum_scatter(early_grad, ("dp", "ctx"), scatter_dimension=1, tiled=True)

    back_row_spec = pl.BlockSpec((ROWS, width), lambda i, *_: (steps - 1 - i, 0))
    back_mixed, back_out_gate, head_gain_part, collected = call(
        gate_back_kernel,
        (steps,),
        [
            back_row_spec,
            fixed(out_weight),
            by_head(HV, True),
            by_head(HV, True),
            by_head(HK, True),
            by_head(HK, True),
            head_gain_spec,
        ],
        [by_head(HV, True), by_head(HV, True), head_gain_spec, state_spec],
        [
            shaped((heads, rows, HV)),
            shaped((heads, rows, HV), BF16),
            shaped((1, HV)),
            shaped((heads, HV, HK)),
        ],
        [],
        (back_attn, out_weight, mixed, out_gate, query, cum, gain_head),
        0,
        2 * rows * width * HV * heads,
        rows * heads * 4 * 1024,
    )
    back_end = carry(collected, device_decay, -1)

    grad_shape = shaped((GROUPS // 2, LANES, columns))
    rank_grad_shape = shaped((ranks, width))
    kept, sent_away, rank_grad, input_grad, decay_out_grad, bias_grad, gain_one_part = call(
        functools.partial(mix_back_kernel, gather_homes()),
        (steps,),
        [
            back_row_spec,
            back_row_spec,
            by_head(HK, True),
            by_head(size, True),
            by_head(HK, True),
            by_head(HK, True),
            pl.BlockSpec((parts, heads, HV, HK), lambda i, *_: (steps - 1 - i, 0, 0, 0)),
            by_head(HV, True),
            by_head(HV, True),
            state_spec,
            fixed(query_weight),
            fixed(key_weight),
            fixed(rank_weight),
            fixed(decay_out_full),
            pl.BlockSpec((ROWS, ranks), lambda i, *_: (steps - 1 - i, 0)),
            gain_spec,
        ],
        [
            fixed(grad_shape),
            fixed(grad_shape),
            fixed(rank_grad_shape),
            back_row_spec,
            pl.BlockSpec((heads, ranks, HK), lambda i, *_: (0, 0, 0)),
            bias_spec,
            gain_spec,
        ],
        [
            grad_shape,
            grad_shape,
            rank_grad_shape,
            shaped((rows, width)),
            shaped((heads, ranks, HK)),
            shaped((heads, 1, HK)),
            shaped((1, width)),
        ],
        [
            pltpu.VMEM((heads, HV, HK), F32),
            pltpu.VMEM((ROWS, heads * size), BF16),
            pltpu.VMEM((ROWS, heads * size), BF16),
            pltpu.VMEM((ROWS, columns), BF16),
            pltpu.VMEM((ROWS, ranks), BF16),
            pltpu.VMEM((width, columns), F32),
        ],
        (
            info, tokens, back_middle, query, kv, cum, logits, states, back_mixed, back_out_gate,
            back_end, query_weight, key_weight, rank_weight, decay_out_full, rank, gain_one,
        ),
        1,
        2 * rows * width * columns * heads * 2,
        rows * heads * 4 * 2048,
    )
    own = info[-1]
    decay_out_own = lax.dynamic_index_in_dim(decay_out_grad, own, 0, keepdims=False)
    bias_own = lax.dynamic_index_in_dim(bias_grad, own, 0, keepdims=False)
    sums = jnp.concatenate(
        [
            gain_one_part.reshape(-1),
            gain_two_part.reshape(-1),
            head_gain_part.reshape(-1),
            bias_own.reshape(-1),
            decay_out_own.reshape(-1),
            rank_grad.reshape(-1),
        ]
    )
    mixer_share, sums, early_share = finish_sums(kept, sent_away, sums, early_share)
    gain_count = gains.shape[0]
    decay_start = gain_count + HK
    rank_start = decay_start + ranks * HK
    gains_grad = sums[:gain_count]
    bias_total = sums[gain_count:decay_start]
    decay_out_total = sums[decay_start:rank_start].reshape(ranks, HK)
    share = decay_in_weight.shape[0]
    place = (lax.axis_index("dp") * lax.axis_size("ctx") + lax.axis_index("ctx")) * share
    decay_in_share = lax.dynamic_slice_in_dim(
        sums[rank_start:].reshape(ranks, width), place, share, axis=1
    ).T

    query_key_share = jnp.stack([mixer_share[:, :HK], mixer_share[:, size : size + HK]])
    value_gate_share = jnp.stack([mixer_share[:, size + HK : columns], mixer_share[:, HK:size]])
    gate_up_share = jnp.stack([early_share[:units].T, early_share[units : 2 * units].T])
    down_share = early_share[2 * units : 3 * units]
    output_share = early_share[3 * units :]

    updated = adamw(
        query_key_weight,
        query_key_share,
        query_key_mean,
        query_key_square,
        RATE_MATRIX,
        WEIGHT_DECAY,
    )
    updated = updated + adamw(
        value_gate_weight,
        value_gate_share,
        value_gate_mean,
        value_gate_square,
        RATE_MATRIX,
        WEIGHT_DECAY,
    )
    updated = updated + adamw(
        decay_in_weight, decay_in_share, decay_in_mean, decay_in_square, RATE_MATRIX, WEIGHT_DECAY
    )
    updated = updated + adamw(
        decay_out_weight, decay_out_total, decay_out_mean, decay_out_square, RATE_RANK, WEIGHT_DECAY
    )
    updated = updated + adamw(
        decay_bias, bias_total, decay_bias_mean, decay_bias_square, RATE_BIAS, 0.0
    )
    updated = updated + adamw(
        output_weight, output_share, output_mean, output_square, RATE_MATRIX, WEIGHT_DECAY
    )
    updated = updated + adamw(
        gate_up_weight, gate_up_share, gate_up_mean, gate_up_square, RATE_MATRIX, WEIGHT_DECAY
    )
    updated = updated + adamw(
        down_weight, down_share, down_mean, down_square, RATE_MATRIX, WEIGHT_DECAY
    )
    updated = updated + adamw(gains, gains_grad, gains_mean, gains_square, RATE_GAIN, 0.0)
    return (layer_out, input_grad) + updated


def solution(mesh):
    tokens_at = P(("dp", "ctx"), None)
    split_at = P(None, ("dp", "ctx"), "tp")
    deep_at = P("tp", ("dp", "ctx"))
    rank_out_at = P(None, "tp")
    kinds = (split_at, split_at, tokens_at, rank_out_at, P("tp"), deep_at, split_at, deep_at, P())
    params = tuple(kind for kind in kinds for _ in range(3))
    return jax.shard_map(
        body,
        mesh=mesh,
        in_specs=(tokens_at, tokens_at, P("dp")) + params,
        out_specs=(tokens_at, tokens_at) + params,
        check_vma=False,
    )
```

```python
import functools

import jax
import jax.numpy as jnp
from jax import lax
from jax.experimental import pallas as pl
from jax.experimental.pallas import tpu as pltpu
from jax.sharding import PartitionSpec as P

HK = 128
HV = 256
BLOCK = 128
LANES = 128
GROUPS = 8
MID = 63
DECAY_ROWS = 32
ROWS = 256
FFN_CUT = 256
STEP = 10

NORM_EPS = 1e-06
HEAD_EPS = 1e-05
GATE_SCALE = 16.0
BETA_ONE = 0.9
BETA_TWO = 0.95
ADAM_EPS = 1e-08
WEIGHT_DECAY = 0.1
RATE_MATRIX = 0.03
RATE_RANK = 0.1
RATE_BIAS = 1.5
RATE_GAIN = 0.3
VMEM_LIMIT = 62 * 1024 * 1024

F32 = jnp.float32
BF16 = jnp.bfloat16
NN = (((1,), (0,)), ((), ()))
NT = (((1,), (1,)), ((), ()))
TN = (((0,), (0,)), ((), ()))


def dot(left, right, dims=NN):
    return lax.dot_general(left, right, dims, preferred_element_type=F32)


def split_two(values):
    high = values.astype(BF16)
    return high, (values - high.astype(F32)).astype(BF16)


def dot_split(left, right, dims=NN):
    axis = 1 - dims[0][0][0]
    size = left[0].shape[axis]
    both = dot(jnp.concatenate(left, axis=axis), right[0], dims)
    return both[:size] + both[size:] + dot(left[0], right[1], dims)


def dot_sum(matrix, values):
    high, low = split_two(values)
    both = dot(matrix, jnp.concatenate([high, low], axis=1))
    return both[:, : values.shape[1]] + both[:, values.shape[1] :]


def dot_two(left, right, dims=NN):
    axis = 1 - dims[0][0][0]
    size = left[0].shape[axis]
    both = dot(jnp.concatenate(left, axis=axis), right, dims)
    return both[:size] + both[size:]


def heads_side_by_side(info, decay_out, start, stop):
    heads = decay_out.shape[0]
    return jnp.concatenate(
        [decay_out[info[2 * GROUPS + head], start:stop] for head in range(heads)], axis=1
    )


def lower_mask():
    rows = lax.broadcasted_iota(jnp.int32, (BLOCK, BLOCK), 0)
    columns = lax.broadcasted_iota(jnp.int32, (BLOCK, BLOCK), 1)
    return rows >= columns


def upper_mask():
    rows = lax.broadcasted_iota(jnp.int32, (BLOCK, BLOCK), 0)
    columns = lax.broadcasted_iota(jnp.int32, (BLOCK, BLOCK), 1)
    return rows <= columns


def as_ones(mask):
    return jnp.where(mask, 1.0, 0.0).astype(BF16)


def inverse_rms(values, epsilon):
    return lax.rsqrt(jnp.mean(values * values, axis=-1, keepdims=True) + epsilon)


def sigmoid(values):
    return 0.5 + 0.5 * jnp.tanh(0.5 * values)


def fill(info, first, second, pieces):
    heads = first.shape[1]
    for head in range(heads):
        slot = info[2 * GROUPS + head]
        for group in range(GROUPS):
            lanes = slice(group * LANES, (group + 1) * LANES)
            place = info[GROUPS + group]
            for source_index, source in enumerate((first, second)):

                @pl.when(info[group] == source_index)
                def _():
                    for target, start, count in pieces:
                        if target.shape[0] == count and head > 0:
                            continue
                        at = head * count
                        target[at : at + count, lanes] = source[
                            place, slot, start : start + count
                        ]


def project_kernel(
    info, tokens, gain, first, second, decay_out,
    normed_out, kv_out, rank_out, logits_out, cum_out, state_out, total_out, weight, rank_weight,
):
    heads = first.shape[1]
    size = HK + HV
    ranks = rank_out.shape[1]

    @pl.when(pl.program_id(0) == 0)
    def _():
        state_out[...] = jnp.zeros_like(state_out)
        total_out[...] = jnp.zeros_like(total_out)
        fill(info, first, second, ((weight, 0, size), (rank_weight, size, ranks)))

    inputs = tokens[...].astype(F32)
    normed = (inputs * inverse_rms(inputs, NORM_EPS) * gain[...]).astype(BF16)
    normed_out[...] = normed
    rank = dot(normed, rank_weight[...], NT)
    rank_out[...] = rank
    lower = as_ones(lower_mask())
    made = dot(normed, weight[...], NT)
    every = range(heads)
    keys = [made[:, head * size : head * size + HK] for head in every]
    values = [made[:, head * size + HK : (head + 1) * size] for head in every]
    all_logits = lax.dot_general(
        rank, heads_side_by_side(info, decay_out, 0, ranks), NN,
        precision=lax.Precision.HIGHEST, preferred_element_type=F32,
    ) + heads_side_by_side(info, decay_out, ranks, ranks + 1)
    logits = [all_logits[:, head * HK : (head + 1) * HK] for head in every]
    for head in every:
        kv_out[head, :, :HK] = keys[head]
        kv_out[head, :, HK:] = values[head]
        logits_out[head] = logits[head]
    log_decay = [
        (jnp.minimum(item, 0.0) - jnp.log1p(jnp.exp(-jnp.abs(item)))) / GATE_SCALE
        for item in logits
    ]
    for part in range(ROWS // BLOCK):
        span = slice(part * BLOCK, (part + 1) * BLOCK)
        cum = [dot_sum(lower, log_decay[head][span]) for head in every]
        total = [item[BLOCK - 1 :] for item in cum]
        carried = [
            split_two(keys[head][span] * jnp.exp(total[head] - cum[head])) for head in every
        ]
        value_parts = [split_two(values[head][span]) for head in every]
        added = [dot_split(value_parts[head], carried[head], TN) for head in every]
        for head in every:
            cum_out[head, span] = cum[head]
            state_out[head] = state_out[head] * jnp.exp(total[head]) + added[head]
            total_out[head] += total[head]


def mix_kernel(
    info, tokens, normed, kv, cum_in, start, first, second, head_gain, gain,
    query_out, gate_out, mixed_out, state_out, gated_out, middle_out, normed_out, weight, out_weight,
    state_ref, gated_ref,
):
    heads = start.shape[0]
    size = HK + HV

    @pl.when(pl.program_id(0) == 0)
    def _():
        state_ref[...] = start[...]
        fill(info, first, second, ((weight, 0, size), (out_weight, size, HV)))

    made = dot(normed[...], weight[...], NT)
    causal = lower_mask()
    every = range(heads)
    for part in range(ROWS // BLOCK):
        span = slice(part * BLOCK, (part + 1) * BLOCK)
        query = [made[span, head * size : head * size + HK] * HK ** (-0.5) for head in every]
        out_gate = [made[span, head * size + HK : (head + 1) * size] for head in every]
        keys = [kv[head, span, :HK] for head in every]
        cum = [cum_in[head, span] for head in every]
        center = [item[MID : MID + 1] for item in cum]
        total = [item[BLOCK - 1 :] for item in cum]
        query_mid = [split_two(query[head] * jnp.exp(cum[head] - center[head])) for head in every]
        key_mid = [split_two(keys[head] * jnp.exp(center[head] - cum[head])) for head in every]
        scores = [dot_split(query_mid[head], key_mid[head], NT) for head in every]
        since = [split_two(query[head] * jnp.exp(cum[head])) for head in every]
        states = [state_ref[head] for head in every]
        carried = [split_two(keys[head] * jnp.exp(total[head] - cum[head])) for head in every]
        values = [split_two(kv[head, span, HK:]) for head in every]
        outer = [dot_split(since[head], split_two(states[head]), NT) for head in every]
        added = [dot_split(values[head], carried[head], TN) for head in every]
        scores = [split_two(jnp.where(causal, item, 0.0)) for item in scores]
        mixed = [dot_split(scores[head], values[head]) + outer[head] for head in every]
        for head in every:
            query_out[head, span] = query[head]
            gate_out[head, span] = out_gate[head]
            state_out[part, head] = states[head]
            state_ref[head] = states[head] * jnp.exp(total[head]) + added[head]
            mixed_out[head, span] = mixed[head]
        for head in every:
            gated_ref[span, head * HV : (head + 1) * HV] = (
                mixed[head]
                * inverse_rms(mixed[head], HEAD_EPS)
                * head_gain[...]
                * (out_gate[head] * sigmoid(out_gate[head]))
            ).astype(BF16)

    for head in every:

        @pl.when(info[2 * GROUPS + heads] == head)
        def _():
            gated_out[...] = gated_ref[:, head * HV : (head + 1) * HV]

    middle = tokens[...].astype(F32) + dot(gated_ref[...], out_weight[...])
    middle_out[...] = middle
    normed_out[...] = (middle * inverse_rms(middle, NORM_EPS) * gain[...]).astype(BF16)


def ffn_kernel(
    info, normed, back, middle, weight, gain,
    active_out, back_gate_out, back_up_out, layer_out, back_middle_out, back_attn_out, gain_out,
    ffn_ref, back_ref, active_ref, back_gate_ref, back_up_ref,
):
    step, piece = pl.program_id(0), pl.program_id(1)
    pieces = pl.num_programs(1)
    own = info[2 * GROUPS + pieces]
    units = weight.shape[2] // 3

    @pl.when((step == 0) & (piece == 0))
    def _():
        gain_out[...] = jnp.zeros_like(gain_out)

    @pl.when(piece == 0)
    def _():
        ffn_ref[...] = jnp.zeros_like(ffn_ref)
        back_ref[...] = jnp.zeros_like(back_ref)

    def rows_of(start, stop):
        return jnp.concatenate([weight[group, 0, start:stop] for group in range(GROUPS)], axis=1)

    cuts = [(start, min(start + FFN_CUT, units)) for start in range(0, units, FFN_CUT)]

    def elementwise(cut, gate_values, upward, back_active):
        at = slice(*cut)
        share = sigmoid(gate_values)
        silu = gate_values * share
        active_ref[:, at] = (silu * upward).astype(BF16)
        back_gate_ref[:, at] = (
            back_active * upward * (share * (1.0 + gate_values * (1.0 - share)))
        ).astype(BF16)
        back_up_ref[:, at] = (back_active * silu).astype(BF16)

    waiting = None
    for cut in cuts:
        start, stop = cut
        made = (
            dot(normed[...], rows_of(start, stop), NT),
            dot(normed[...], rows_of(units + start, units + stop), NT),
            dot(back[...], rows_of(2 * units + start, 2 * units + stop), NT),
        )
        if waiting is not None:
            elementwise(*waiting)
        waiting = (cut,) + made
    elementwise(*waiting)
    back_ref[...] += dot(back_gate_ref[...], rows_of(0, units)) + dot(
        back_up_ref[...], rows_of(units, 2 * units)
    )

    @pl.when(step == own)
    def _():
        ffn_ref[...] += dot(active_ref[...], rows_of(2 * units, 3 * units))

    @pl.when(piece == own)
    def _():
        active_out[...] = active_ref[...]
        back_gate_out[...] = back_gate_ref[...]
        back_up_out[...] = back_up_ref[...]

    @pl.when((piece == pieces - 1) & (step == own))
    def _():
        layer_out[...] = (middle[...] + ffn_ref[...]).astype(BF16)

    @pl.when(piece == pieces - 1)
    def _():
        mid = middle[...]
        inverse = inverse_rms(mid, NORM_EPS)
        unit = mid * inverse
        total = back_ref[...]
        weighted = total * gain[...]
        back_middle = back[...].astype(F32) + inverse * (
            weighted - unit * jnp.mean(weighted * unit, axis=-1, keepdims=True)
        )
        back_middle_out[...] = back_middle
        back_attn_out[...] = back_middle.astype(BF16)
        gain_out[...] += jnp.sum(total * unit, axis=0, keepdims=True)


def gate_back_kernel(
    back_attn, out_weight, mixed_in, gate, query_in, cum_in, head_gain,
    back_mixed_out, back_gate_out, gain_out, state_out,
):
    heads = gate.shape[0]

    @pl.when(pl.program_id(0) == 0)
    def _():
        gain_out[...] = jnp.zeros_like(gain_out)
        state_out[...] = jnp.zeros_like(state_out)

    every = range(heads)
    back_gated = [
        dot(back_attn[...], out_weight[head * HV : (head + 1) * HV], NT) for head in every
    ]
    scaled = [query_in[head] * jnp.exp(cum_in[head]) for head in every]
    back_mixed = []
    for head in every:
        mixed = mixed_in[head]
        out_gate = gate[head]
        inverse = inverse_rms(mixed, HEAD_EPS)
        unit = mixed * inverse
        share = sigmoid(out_gate)
        silu = out_gate * share
        slope = share * (1.0 + out_gate * (1.0 - share))
        shaped_back = back_gated[head] * unit
        back_gate_out[head] = (shaped_back * head_gain[...] * slope).astype(BF16)
        gain_out[...] += jnp.sum(shaped_back * silu, axis=0, keepdims=True)
        weighted = back_gated[head] * head_gain[...] * silu
        item = inverse * (weighted - unit * jnp.mean(weighted * unit, axis=-1, keepdims=True))
        back_mixed_out[head] = item
        back_mixed.append(item)
    for part in reversed(range(ROWS // BLOCK)):
        span = slice(part * BLOCK, (part + 1) * BLOCK)
        added = [
            dot_split(split_two(back_mixed[head][span]), split_two(scaled[head][span]), TN)
            for head in every
        ]
        for head in every:
            last = cum_in[head, (part + 1) * BLOCK - 1 : (part + 1) * BLOCK]
            state_out[head] = state_out[head] * jnp.exp(last) + added[head]


def mix_back_kernel(
    homes, info, tokens, back_middle, query_in, kv, cum_in, logits_in, states, back_mixed, back_gate,
    back_end, query_weight, key_weight, rank_weight, decay_out, rank, gain,
    kept_out, sent_out, rank_grad_out, input_out, decay_grad_out, bias_out, gain_out,
    state_ref, query_ref, key_ref, grad_ref, rank_ref, sum_ref,
):
    heads = back_end.shape[0]
    size = HK + HV
    ranks = rank.shape[1]

    @pl.when(pl.program_id(0) == 0)
    def _():
        state_ref[...] = back_end[...]
        sum_ref[...] = jnp.zeros_like(sum_ref)
        rank_grad_out[...] = jnp.zeros_like(rank_grad_out)
        decay_grad_out[...] = jnp.zeros_like(decay_grad_out)
        bias_out[...] = jnp.zeros_like(bias_out)
        gain_out[...] = jnp.zeros_like(gain_out)

    causal = lower_mask()
    upper = as_ones(upper_mask())
    every = range(heads)
    for part in reversed(range(ROWS // BLOCK)):
        span = slice(part * BLOCK, (part + 1) * BLOCK)
        query = [query_in[head, span] for head in every]
        keys = [kv[head, span, :HK] for head in every]
        cum = [cum_in[head, span] for head in every]
        center = [item[MID : MID + 1] for item in cum]
        total = [item[BLOCK - 1 :] for item in cum]
        grow = [jnp.exp(cum[head] - center[head]) for head in every]
        shrink = [jnp.exp(center[head] - cum[head]) for head in every]
        query_mid = [split_two(query[head] * grow[head]) for head in every]
        key_mid = [split_two(keys[head] * shrink[head]) for head in every]
        values = [split_two(kv[head, span, HK:]) for head in every]
        back = [split_two(back_mixed[head, span]) for head in every]
        scores = [dot_two(query_mid[head], key_mid[head][0], NT) for head in every]
        back_scores = [dot_split(back[head], values[head], NT) for head in every]
        since = [jnp.exp(cum[head]) for head in every]
        until = [jnp.exp(total[head] - cum[head]) for head in every]
        carried = [keys[head] * until[head] for head in every]
        back_state = [state_ref[head] for head in every]
        back_state_parts = [split_two(item) for item in back_state]
        back_carried = [dot_split(values[head], back_state_parts[head]) for head in every]
        back_since = [dot_split(back[head], split_two(states[part, head])) for head in every]
        added = [
            dot_split(back[head], split_two(query[head] * since[head]), TN) for head in every
        ]
        outer = [
            dot_two(split_two(carried[head]), back_state_parts[head][0], NT) for head in every
        ]
        scores = [split_two(jnp.where(causal, item, 0.0)) for item in scores]
        back_scores = [split_two(jnp.where(causal, item, 0.0)) for item in back_scores]
        back_query = [
            dot_split(back_scores[head], key_mid[head]) * grow[head]
            + back_since[head] * since[head]
            for head in every
        ]
        back_keys = [
            dot_split(back_scores[head], query_mid[head], TN) * shrink[head]
            + back_carried[head] * until[head]
            for head in every
        ]
        back_values = [dot_two(scores[head], back[head][0], TN) + outer[head] for head in every]
        back_total = []
        for head in every:
            decayed = back_state[head] * jnp.exp(total[head])
            back_total.append(
                jnp.sum(back_carried[head] * carried[head], axis=0, keepdims=True)
                + jnp.sum(decayed * states[part, head], axis=0, keepdims=True)
            )
            state_ref[head] = decayed + added[head]
        back_logits = [
            (
                dot_sum(upper, query[head] * back_query[head] - keys[head] * back_keys[head])
                + back_total[head]
            )
            * sigmoid(-logits_in[head, span])
            / GATE_SCALE
            for head in every
        ]
        together = jnp.concatenate(back_logits, axis=1)
        rank_back = lax.dot_general(
            together, heads_side_by_side(info, decay_out, 0, ranks), NT,
            precision=lax.Precision.HIGHEST, preferred_element_type=F32,
        )
        decay_grad_out[...] += dot_split(split_two(rank[span]), split_two(together), TN)
        bias_out[...] += jnp.sum(together, axis=0, keepdims=True)
        for head in every:
            at = head * size
            query_ref[span, at : at + HK] = (back_query[head] * HK ** (-0.5)).astype(BF16)
            query_ref[span, at + HK : at + size] = back_gate[head, span]
            key_ref[span, at : at + HK] = back_keys[head].astype(BF16)
            key_ref[span, at + HK : at + size] = back_values[head].astype(BF16)
        rank_ref[span] = rank_back.astype(BF16)

    for head in every:

        @pl.when(info[2 * GROUPS + heads] == head)
        def _():
            grad_ref[:, :size] = query_ref[:, head * size : (head + 1) * size]
            grad_ref[:, size:] = key_ref[:, head * size : (head + 1) * size]

    back_normed = (
        dot(rank_ref[...], rank_weight[...])
        + dot(query_ref[...], query_weight[...])
        + dot(key_ref[...], key_weight[...])
    )
    inputs = tokens[...].astype(F32)
    inverse = inverse_rms(inputs, NORM_EPS)
    unit = inputs * inverse
    normed = (unit * gain[...]).astype(BF16)
    sum_ref[...] += dot(normed, grad_ref[...], TN)
    rank_grad_out[...] += dot(rank_ref[...], normed, TN)
    weighted = back_normed * gain[...]
    input_out[...] = back_middle[...] + inverse * (
        weighted - unit * jnp.mean(weighted * unit, axis=-1, keepdims=True)
    )
    gain_out[...] += jnp.sum(back_normed * unit, axis=0, keepdims=True)

    @pl.when(pl.program_id(0) == pl.num_programs(0) - 1)
    def _():
        for group in range(GROUPS):
            found = slice(group * LANES, (group + 1) * LANES)
            for index, target in enumerate((kept_out, sent_out)):

                @pl.when(info[group] == index)
                def _():
                    target[homes[group]] = sum_ref[found]


def shaped(shape, kind=F32):
    return jax.ShapeDtypeStruct(shape, kind)


def call(kernel, grid, in_specs, out_specs, out_shape, scratch, operands, prefetch, flops, moved):
    return pl.pallas_call(
        kernel,
        grid_spec=pltpu.PrefetchScalarGridSpec(
            num_scalar_prefetch=prefetch,
            grid=grid,
            in_specs=in_specs,
            out_specs=out_specs,
            scratch_shapes=scratch,
        ),
        out_shape=out_shape,
        compiler_params=pltpu.CompilerParams(
            vmem_limit_bytes=VMEM_LIMIT, dimension_semantics=("arbitrary",) * len(grid)
        ),
        cost_estimate=pl.CostEstimate(flops=flops, bytes_accessed=moved, transcendentals=0),
    )(*operands)


def from_behind(value, axis, steps):
    count = lax.axis_size(axis)
    first, last = (max(0, -steps), min(count, count - steps))
    return lax.ppermute(value, axis, [(source, source + steps) for source in range(first, last)])


def carry(local, decay, steps):
    incoming = jnp.zeros_like(local)
    for _ in range(lax.axis_size("ctx") - 1):
        incoming = from_behind(decay * incoming + local, "ctx", steps)
    return incoming


def staged():
    return lax.axis_size("dp") == 4 and lax.axis_size("ctx") == 2


def swap(value, axis, distance):
    count = lax.axis_size(axis)
    return lax.ppermute(value, axis, [(source, source ^ distance) for source in range(count)])


def shift(value, axis, distance):
    count = lax.axis_size(axis)
    return lax.ppermute(
        value, axis, [(source, (source + distance) % count) for source in range(count)]
    )


def gather_plain(pack):
    rows = pack.shape[0]
    whole = lax.all_gather(lax.all_gather(pack, "tp"), ("dp", "ctx"), axis=2, tiled=True)
    return whole.reshape(whole.shape[0], rows, GROUPS, LANES).transpose(2, 0, 1, 3)


def gather_line(pack):
    count = lax.axis_size("tp")
    return jnp.stack([pack] + [shift(pack, "tp", distance) for distance in range(1, count)])


def gather_square(line):
    return [line] + [swap(line, "dp", distance) for distance in range(1, 4)]


def gather_slots(key_pack, query_pack):
    key_line = gather_line(key_pack)
    query_pack, key_line = lax.optimization_barrier((query_pack, key_line))
    key_first = jnp.stack(gather_square(key_line))
    query_line = gather_line(query_pack)
    query_line, key_first = lax.optimization_barrier((query_line, key_first))
    return key_first, swap(key_first, "ctx", 1), gather_square(query_line)


def gather_pair(pack):
    whole = gather_plain(pack)
    half = GROUPS // 2
    return whole[:half], whole[half:]


def gather_homes():
    if staged():
        return [group // 2 for group in range(GROUPS)]
    return [group % (GROUPS // 2) for group in range(GROUPS)]


def gather_info():
    count = lax.axis_size("tp")
    own = lax.axis_index("tp")
    group = jnp.arange(GROUPS, dtype=jnp.int32)
    heads = jnp.arange(count, dtype=jnp.int32)
    if staged():
        which = (group % 2) ^ lax.axis_index("ctx")
        place = (group // 2) ^ lax.axis_index("dp")
        slot = lax.rem(own - heads + count, count)
    else:
        which, place, slot = group // (GROUPS // 2), group % (GROUPS // 2), heads
    return jnp.concatenate([which, place, slot, own.reshape(1)]).astype(jnp.int32)


def gather_whole(pack):
    if staged():
        rows, share = pack.shape
        whole = lax.all_gather(pack, ("dp", "ctx", "tp"))
        return whole.reshape(-1, lax.axis_size("tp"), rows, share)
    return gather_plain(pack)


def finish_sums(kept, sent, sums, early, late):
    columns = kept.shape[-1]
    if not staged():
        whole = jnp.concatenate([kept, sent]).reshape(-1, columns)
        share = lax.psum_scatter(whole, ("dp", "ctx"), scatter_dimension=0, tiled=True)
        return share, lax.psum(sums, ("dp", "ctx")), early, late
    device = lax.axis_index("dp")
    row, column = device // 2, device % 2

    def pick(array, axis, index):
        return lax.dynamic_index_in_dim(array, index, axis, keepdims=False)

    value = kept + swap(sent, "ctx", 1)
    sums = sums + swap(sums, "ctx", 1)
    value, sums, early, late = lax.optimization_barrier((value, sums, early, late))
    value = value.reshape(2, 2, LANES, columns)
    half = LANES // 2
    upper, lower = value[:, :, :half], value[:, :, half:]
    upper = pick(upper, 1, column) + swap(pick(upper, 1, 1 - column), "dp", 1)
    lower = pick(lower, 0, row) + swap(pick(lower, 0, 1 - row), "dp", 2)
    sums = sums + swap(sums, "dp", 1)
    upper, lower, sums = lax.optimization_barrier((upper, lower, sums))
    upper = pick(upper, 0, row) + swap(pick(upper, 0, 1 - row), "dp", 2)
    lower = pick(lower, 0, column) + swap(pick(lower, 0, 1 - column), "dp", 1)
    sums = sums + swap(sums, "dp", 2)
    return jnp.concatenate([upper, lower]), sums, early, late


def adamw(weight_now, grad_now, mean_now, square_now, rate_value, decay_value):
    mean_new = BETA_ONE * mean_now + (1.0 - BETA_ONE) * grad_now
    square_new = BETA_TWO * square_now + (1.0 - BETA_TWO) * grad_now * grad_now
    mean_hat = mean_new / (1.0 - BETA_ONE**STEP)
    square_hat = square_new / (1.0 - BETA_TWO**STEP)
    weight_new = weight_now - rate_value * (
        mean_hat / (jnp.sqrt(square_hat) + ADAM_EPS) + decay_value * weight_now
    )
    return (mean_new, square_new, weight_new)


def three_parts(value):
    high = lax.reduce_precision(value, 8, 7)
    rest = value - high
    middle = lax.reduce_precision(rest, 8, 7)
    low = lax.reduce_precision(rest - middle, 8, 7)
    return [part.astype(BF16) for part in (high, middle, low)]


def body(
    tokens,
    cotangent,
    lengths,
    query_key_weight,
    query_key_mean,
    query_key_square,
    value_gate_weight,
    value_gate_mean,
    value_gate_square,
    decay_in_weight,
    decay_in_mean,
    decay_in_square,
    decay_out_weight,
    decay_out_mean,
    decay_out_square,
    decay_bias,
    decay_bias_mean,
    decay_bias_square,
    output_weight,
    output_mean,
    output_square,
    gate_up_weight,
    gate_up_mean,
    gate_up_square,
    down_weight,
    down_mean,
    down_square,
    gains,
    gains_mean,
    gains_square,
):
    rows, width = tokens.shape
    heads = lax.axis_size("tp")
    ranks = decay_in_weight.shape[1]
    units = down_weight.shape[0]
    steps = rows // ROWS
    info = gather_info()
    gain_one = gains[:width].reshape(1, width)
    gain_two = gains[width : 2 * width].reshape(1, width)
    gain_head = gains[2 * width :].reshape(1, HV)
    size = HK + HV

    small = jnp.concatenate(
        [
            decay_out_weight,
            decay_bias.reshape(1, HK),
            jnp.zeros((DECAY_ROWS - ranks - 1, HK), F32),
        ]
    )
    key_parts = [
        query_key_weight[1].T.astype(BF16),
        value_gate_weight[0].T.astype(BF16),
        decay_in_weight.T.astype(BF16),
    ]
    query_pack = jnp.concatenate(
        [query_key_weight[0].T, value_gate_weight[1].T, output_weight]
    ).astype(BF16)
    if staged():
        key_first, key_second, query_square = gather_slots(
            jnp.concatenate(key_parts + three_parts(small)), query_pack
        )
        sent = key_first[0, :, size + ranks :].astype(F32).reshape(heads, 3, DECAY_ROWS, HK)
        decay_out_full = sent[:, 0] + sent[:, 1] + sent[:, 2]
    else:
        key_first, key_second = gather_pair(jnp.concatenate(key_parts))
        query_first, query_second = gather_pair(query_pack)
        decay_out_full = lax.all_gather(small, "tp")
    ffn = gather_whole(
        jnp.concatenate([gate_up_weight[0].T, gate_up_weight[1].T, down_weight]).astype(BF16)
    )

    position = lax.axis_index("ctx") * rows + jnp.arange(rows, dtype=jnp.int32)
    back_ffn = jnp.where((position < lengths[0])[:, None], cotangent, jnp.zeros_like(cotangent))

    columns = 2 * size
    row_spec = pl.BlockSpec((ROWS, width), lambda i, *_: (i, 0))
    gain_spec = pl.BlockSpec((1, width), lambda i, *_: (0, 0))
    head_gain_spec = pl.BlockSpec((1, HV), lambda i, *_: (0, 0))
    state_spec = pl.BlockSpec((heads, HV, HK), lambda i, *_: (0, 0, 0))
    bias_spec = pl.BlockSpec((heads, 1, HK), lambda i, *_: (0, 0, 0))

    def fixed(array):
        return pl.BlockSpec(
            array.shape, lambda i, *_: (0,) * len(array.shape), pipeline_mode=pl.Buffered(1)
        )

    def by_head(length, reverse=False):
        if reverse:
            return pl.BlockSpec((heads, ROWS, length), lambda i, *_: (0, steps - 1 - i, 0))
        return pl.BlockSpec((heads, ROWS, length), lambda i, *_: (0, i, 0))

    weight_shape = shaped((heads * size, width), BF16)
    rank_shape = shaped((ranks, width), BF16)
    out_weight_shape = shaped((heads * HV, width), BF16)
    parts = ROWS // BLOCK
    normed, kv, rank, logits, cum, local_state, local_total, key_weight, rank_weight = call(
        project_kernel,
        (steps,),
        [row_spec, gain_spec, fixed(key_first), fixed(key_second), fixed(decay_out_full)],
        [
            row_spec,
            by_head(size),
            pl.BlockSpec((ROWS, ranks), lambda i, *_: (i, 0)),
            by_head(HK),
            by_head(HK),
            state_spec,
            bias_spec,
            fixed(weight_shape),
            fixed(rank_shape),
        ],
        [
            shaped((rows, width), BF16),
            shaped((heads, rows, size)),
            shaped((rows, ranks)),
            shaped((heads, rows, HK)),
            shaped((heads, rows, HK)),
            shaped((heads, HV, HK)),
            shaped((heads, 1, HK)),
            weight_shape,
            rank_shape,
        ],
        [],
        (info, tokens, gain_one, key_first, key_second, decay_out_full),
        1,
        2 * rows * width * size * heads,
        rows * heads * 4 * 1024,
    )
    if staged():
        query_square, local_state = lax.optimization_barrier((query_square, local_state))
        query_first = jnp.stack(query_square)
        query_second = swap(query_first, "ctx", 1)
    device_decay = jnp.exp(local_total)
    start_state = carry(local_state, device_decay, 1)

    query, out_gate, mixed, states, gated_own, middle, normed_two, query_weight, out_weight = call(
        mix_kernel,
        (steps,),
        [
            row_spec,
            row_spec,
            by_head(size),
            by_head(HK),
            state_spec,
            fixed(query_first),
            fixed(query_second),
            head_gain_spec,
            gain_spec,
        ],
        [
            by_head(HK),
            by_head(HV),
            by_head(HV),
            pl.BlockSpec((parts, heads, HV, HK), lambda i, *_: (i, 0, 0, 0)),
            pl.BlockSpec((ROWS, HV), lambda i, *_: (i, 0)),
            row_spec,
            row_spec,
            fixed(weight_shape),
            fixed(out_weight_shape),
        ],
        [
            shaped((heads, rows, HK)),
            shaped((heads, rows, HV)),
            shaped((heads, rows, HV)),
            shaped((steps * parts, heads, HV, HK)),
            shaped((rows, HV), BF16),
            shaped((rows, width)),
            shaped((rows, width), BF16),
            weight_shape,
            out_weight_shape,
        ],
        [pltpu.VMEM((heads, HV, HK), F32), pltpu.VMEM((ROWS, heads * HV), BF16)],
        (
            info, tokens, normed, kv, cum, start_state, query_first, query_second,
            gain_head, gain_two,
        ),
        1,
        2 * rows * width * (size + 2 * HV) * heads,
        rows * heads * 4 * 1024,
    )

    tile = rows // heads
    wide_spec = pl.BlockSpec((tile, width), lambda i, j, *_: (i, 0))
    own_spec = pl.BlockSpec((tile, units), lambda i, j, *_: (i, 0))
    wide_gain_spec = pl.BlockSpec((1, width), lambda i, j, *_: (0, 0))
    active, back_gate, back_up, layer_own, back_middle, back_attn, gain_two_part = call(
        ffn_kernel,
        (heads, heads),
        [
            wide_spec,
            wide_spec,
            wide_spec,
            pl.BlockSpec((GROUPS, 1, 3 * units, LANES), lambda i, j, *_: (0, j, 0, 0)),
            wide_gain_spec,
        ],
        [
            own_spec,
            own_spec,
            own_spec,
            pl.BlockSpec((tile, width), lambda i, j, *_: (0, 0)),
            wide_spec,
            wide_spec,
            wide_gain_spec,
        ],
        [
            shaped((rows, units), BF16),
            shaped((rows, units), BF16),
            shaped((rows, units), BF16),
            shaped((tile, width), BF16),
            shaped((rows, width)),
            shaped((rows, width), BF16),
            shaped((1, width)),
        ],
        [
            pltpu.VMEM((tile, width), F32),
            pltpu.VMEM((tile, width), F32),
            pltpu.VMEM((tile, units), BF16),
            pltpu.VMEM((tile, units), BF16),
            pltpu.VMEM((tile, units), BF16),
        ],
        (info, normed_two, back_ffn, middle, ffn, gain_two),
        1,
        10 * rows * width * units * heads,
        rows * width * 24,
    )
    layer_parts = [layer_own] + [shift(layer_own, "tp", distance) for distance in range(1, heads)]
    early_grad = jnp.concatenate(
        [
            dot(back_gate, normed_two, TN),
            dot(back_up, normed_two, TN),
            dot(active, back_ffn, TN),
            dot(gated_own, back_attn, TN),
        ]
    )
    early_grad, back_attn = lax.optimization_barrier((early_grad, back_attn))
    early_share = lax.psum_scatter(early_grad, ("dp", "ctx"), scatter_dimension=1, tiled=True)

    back_row_spec = pl.BlockSpec((ROWS, width), lambda i, *_: (steps - 1 - i, 0))
    back_mixed, back_out_gate, head_gain_part, collected = call(
        gate_back_kernel,
        (steps,),
        [
            back_row_spec,
            fixed(out_weight),
            by_head(HV, True),
            by_head(HV, True),
            by_head(HK, True),
            by_head(HK, True),
            head_gain_spec,
        ],
        [by_head(HV, True), by_head(HV, True), head_gain_spec, state_spec],
        [
            shaped((heads, rows, HV)),
            shaped((heads, rows, HV), BF16),
            shaped((1, HV)),
            shaped((heads, HV, HK)),
        ],
        [],
        (back_attn, out_weight, mixed, out_gate, query, cum, gain_head),
        0,
        2 * rows * width * HV * heads,
        rows * heads * 4 * 1024,
    )
    back_end = carry(collected, device_decay, -1)

    grad_shape = shaped((GROUPS // 2, LANES, columns))
    rank_grad_shape = shaped((ranks, width))
    kept, sent_away, rank_grad, input_grad, decay_out_grad, bias_grad, gain_one_part = call(
        functools.partial(mix_back_kernel, gather_homes()),
        (steps,),
        [
            back_row_spec,
            back_row_spec,
            by_head(HK, True),
            by_head(size, True),
            by_head(HK, True),
            by_head(HK, True),
            pl.BlockSpec((parts, heads, HV, HK), lambda i, *_: (steps - 1 - i, 0, 0, 0)),
            by_head(HV, True),
            by_head(HV, True),
            state_spec,
            fixed(query_weight),
            fixed(key_weight),
            fixed(rank_weight),
            fixed(decay_out_full),
            pl.BlockSpec((ROWS, ranks), lambda i, *_: (steps - 1 - i, 0)),
            gain_spec,
        ],
        [
            fixed(grad_shape),
            fixed(grad_shape),
            fixed(rank_grad_shape),
            back_row_spec,
            pl.BlockSpec((ranks, heads * HK), lambda i, *_: (0, 0)),
            pl.BlockSpec((1, heads * HK), lambda i, *_: (0, 0)),
            gain_spec,
        ],
        [
            grad_shape,
            grad_shape,
            rank_grad_shape,
            shaped((rows, width)),
            shaped((ranks, heads * HK)),
            shaped((1, heads * HK)),
            shaped((1, width)),
        ],
        [
            pltpu.VMEM((heads, HV, HK), F32),
            pltpu.VMEM((ROWS, heads * size), BF16),
            pltpu.VMEM((ROWS, heads * size), BF16),
            pltpu.VMEM((ROWS, columns), BF16),
            pltpu.VMEM((ROWS, ranks), BF16),
            pltpu.VMEM((width, columns), F32),
        ],
        (
            info, tokens, back_middle, query, kv, cum, logits, states, back_mixed, back_out_gate,
            back_end, query_weight, key_weight, rank_weight, decay_out_full, rank, gain_one,
        ),
        1,
        2 * rows * width * columns * heads * 2,
        rows * heads * 4 * 2048,
    )
    own = info[-1]
    decay_out_own = lax.dynamic_slice_in_dim(decay_out_grad, own * HK, HK, axis=1)
    bias_own = lax.dynamic_slice_in_dim(bias_grad, own * HK, HK, axis=1)
    sums = jnp.concatenate(
        [
            gain_one_part.reshape(-1),
            gain_two_part.reshape(-1),
            head_gain_part.reshape(-1),
            bias_own.reshape(-1),
            decay_out_own.reshape(-1),
            rank_grad.reshape(-1),
        ]
    )
    mixer_share, sums, early_share, layer_parts = finish_sums(
        kept, sent_away, sums, early_share, layer_parts
    )
    layer_order = jnp.stack(layer_parts)
    layer_out = jnp.concatenate(
        [
            lax.dynamic_index_in_dim(
                layer_order, lax.rem(own - head + heads, heads), 0, keepdims=False
            )
            for head in range(heads)
        ]
    )
    gain_count = gains.shape[0]
    decay_start = gain_count + HK
    rank_start = decay_start + ranks * HK
    gains_grad = sums[:gain_count]
    bias_total = sums[gain_count:decay_start]
    decay_out_total = sums[decay_start:rank_start].reshape(ranks, HK)
    share = decay_in_weight.shape[0]
    place = (lax.axis_index("dp") * lax.axis_size("ctx") + lax.axis_index("ctx")) * share
    decay_in_share = lax.dynamic_slice_in_dim(
        sums[rank_start:].reshape(ranks, width), place, share, axis=1
    ).T

    query_key_share = jnp.stack([mixer_share[:, :HK], mixer_share[:, size : size + HK]])
    value_gate_share = jnp.stack([mixer_share[:, size + HK : columns], mixer_share[:, HK:size]])
    gate_up_share = jnp.stack([early_share[:units].T, early_share[units : 2 * units].T])
    down_share = early_share[2 * units : 3 * units]
    output_share = early_share[3 * units :]

    updated = adamw(
        query_key_weight,
        query_key_share,
        query_key_mean,
        query_key_square,
        RATE_MATRIX,
        WEIGHT_DECAY,
    )
    updated = updated + adamw(
        value_gate_weight,
        value_gate_share,
        value_gate_mean,
        value_gate_square,
        RATE_MATRIX,
        WEIGHT_DECAY,
    )
    updated = updated + adamw(
        decay_in_weight, decay_in_share, decay_in_mean, decay_in_square, RATE_MATRIX, WEIGHT_DECAY
    )
    updated = updated + adamw(
        decay_out_weight, decay_out_total, decay_out_mean, decay_out_square, RATE_RANK, WEIGHT_DECAY
    )
    updated = updated + adamw(
        decay_bias, bias_total, decay_bias_mean, decay_bias_square, RATE_BIAS, 0.0
    )
    updated = updated + adamw(
        output_weight, output_share, output_mean, output_square, RATE_MATRIX, WEIGHT_DECAY
    )
    updated = updated + adamw(
        gate_up_weight, gate_up_share, gate_up_mean, gate_up_square, RATE_MATRIX, WEIGHT_DECAY
    )
    updated = updated + adamw(
        down_weight, down_share, down_mean, down_square, RATE_MATRIX, WEIGHT_DECAY
    )
    updated = updated + adamw(gains, gains_grad, gains_mean, gains_square, RATE_GAIN, 0.0)
    return (layer_out, input_grad) + updated


def solution(mesh):
    tokens_at = P(("dp", "ctx"), None)
    split_at = P(None, ("dp", "ctx"), "tp")
    deep_at = P("tp", ("dp", "ctx"))
    rank_out_at = P(None, "tp")
    kinds = (split_at, split_at, tokens_at, rank_out_at, P("tp"), deep_at, split_at, deep_at, P())
    params = tuple(kind for kind in kinds for _ in range(3))
    return jax.shard_map(
        body,
        mesh=mesh,
        in_specs=(tokens_at, tokens_at, P("dp")) + params,
        out_specs=(tokens_at, tokens_at) + params,
        check_vma=False,
    )
```

```python
import functools

import jax
import jax.numpy as jnp
from jax import lax
from jax.experimental import pallas as pl
from jax.experimental.pallas import tpu as pltpu
from jax.sharding import PartitionSpec as P

HK = 128
HV = 256
BLOCK = 128
LANES = 128
GROUPS = 8
MID = 63
DECAY_ROWS = 32
ROWS = 256
FFN_ROWS = 512
FFN_CUTS = 8
STEP = 10

NORM_EPS = 1e-06
HEAD_EPS = 1e-05
GATE_SCALE = 16.0
BETA_ONE = 0.9
BETA_TWO = 0.95
ADAM_EPS = 1e-08
WEIGHT_DECAY = 0.1
RATE_MATRIX = 0.03
RATE_RANK = 0.1
RATE_BIAS = 1.5
RATE_GAIN = 0.3
VMEM_LIMIT = 62 * 1024 * 1024

F32 = jnp.float32
BF16 = jnp.bfloat16
NN = (((1,), (0,)), ((), ()))
NT = (((1,), (1,)), ((), ()))
TN = (((0,), (0,)), ((), ()))


def dot(left, right, dims=NN):
    return lax.dot_general(left, right, dims, preferred_element_type=F32)


def split_two(values):
    high = values.astype(BF16)
    return high, (values - high.astype(F32)).astype(BF16)


def dot_split(left, right, dims=NN):
    axis = 1 - dims[0][0][0]
    size = left[0].shape[axis]
    both = dot(jnp.concatenate(left, axis=axis), right[0], dims)
    return both[:size] + both[size:] + dot(left[0], right[1], dims)


def dot_sum(matrix, values):
    high, low = split_two(values)
    both = dot(matrix, jnp.concatenate([high, low], axis=1))
    return both[:, : values.shape[1]] + both[:, values.shape[1] :]


def dot_two(left, right, dims=NN):
    axis = 1 - dims[0][0][0]
    size = left[0].shape[axis]
    both = dot(jnp.concatenate(left, axis=axis), right, dims)
    return both[:size] + both[size:]


def heads_side_by_side(info, decay_out, start, stop):
    heads = decay_out.shape[0]
    return jnp.concatenate(
        [decay_out[info[2 * GROUPS + head], start:stop] for head in range(heads)], axis=1
    )


def lower_mask():
    rows = lax.broadcasted_iota(jnp.int32, (BLOCK, BLOCK), 0)
    columns = lax.broadcasted_iota(jnp.int32, (BLOCK, BLOCK), 1)
    return rows >= columns


def upper_mask():
    rows = lax.broadcasted_iota(jnp.int32, (BLOCK, BLOCK), 0)
    columns = lax.broadcasted_iota(jnp.int32, (BLOCK, BLOCK), 1)
    return rows <= columns


def as_ones(mask):
    return jnp.where(mask, 1.0, 0.0).astype(BF16)


def inverse_rms(values, epsilon):
    return lax.rsqrt(jnp.mean(values * values, axis=-1, keepdims=True) + epsilon)


def sigmoid(values):
    return 0.5 + 0.5 * jnp.tanh(0.5 * values)


def fill(info, first, second, pieces):
    heads = first.shape[1]
    for head in range(heads):
        slot = info[2 * GROUPS + head]
        for group in range(GROUPS):
            lanes = slice(group * LANES, (group + 1) * LANES)
            place = info[GROUPS + group]
            for source_index, source in enumerate((first, second)):

                @pl.when(info[group] == source_index)
                def _():
                    for target, start, count in pieces:
                        if target.shape[0] == count and head > 0:
                            continue
                        at = head * count
                        target[at : at + count, lanes] = source[
                            place, slot, start : start + count
                        ]


def project_kernel(
    info, tokens, gain, first, second, decay_out,
    normed_out, kv_out, rank_out, logits_out, cum_out, state_out, total_out, weight, rank_weight,
):
    heads = first.shape[1]
    size = HK + HV
    ranks = rank_out.shape[1]

    @pl.when(pl.program_id(0) == 0)
    def _():
        state_out[...] = jnp.zeros_like(state_out)
        total_out[...] = jnp.zeros_like(total_out)
        fill(info, first, second, ((weight, 0, size), (rank_weight, size, ranks)))

    inputs = tokens[...].astype(F32)
    normed = (inputs * inverse_rms(inputs, NORM_EPS) * gain[...]).astype(BF16)
    normed_out[...] = normed
    rank = dot(normed, rank_weight[...], NT)
    rank_out[...] = rank
    lower = as_ones(lower_mask())
    made = dot(normed, weight[...], NT)
    every = range(heads)
    keys = [made[:, head * size : head * size + HK] for head in every]
    values = [made[:, head * size + HK : (head + 1) * size] for head in every]
    all_logits = lax.dot_general(
        rank, heads_side_by_side(info, decay_out, 0, ranks), NN,
        precision=lax.Precision.HIGHEST, preferred_element_type=F32,
    ) + heads_side_by_side(info, decay_out, ranks, ranks + 1)
    logits = [all_logits[:, head * HK : (head + 1) * HK] for head in every]
    for head in every:
        kv_out[head, :, :HK] = keys[head]
        kv_out[head, :, HK:] = values[head]
        logits_out[head] = logits[head]
    log_decay = [
        (jnp.minimum(item, 0.0) - jnp.log1p(jnp.exp(-jnp.abs(item)))) / GATE_SCALE
        for item in logits
    ]
    for part in range(ROWS // BLOCK):
        span = slice(part * BLOCK, (part + 1) * BLOCK)
        cum = [dot_sum(lower, log_decay[head][span]) for head in every]
        total = [item[BLOCK - 1 :] for item in cum]
        carried = [
            split_two(keys[head][span] * jnp.exp(total[head] - cum[head])) for head in every
        ]
        value_parts = [split_two(values[head][span]) for head in every]
        added = [dot_split(value_parts[head], carried[head], TN) for head in every]
        for head in every:
            cum_out[head, span] = cum[head]
            state_out[head] = state_out[head] * jnp.exp(total[head]) + added[head]
            total_out[head] += total[head]


def mix_kernel(
    info, tokens, normed, kv, cum_in, start, first, second, head_gain, gain,
    query_out, gate_out, mixed_out, state_out, gated_out, middle_out, normed_out, weight, out_weight,
    state_ref, gated_ref,
):
    heads = start.shape[0]
    size = HK + HV

    @pl.when(pl.program_id(0) == 0)
    def _():
        state_ref[...] = start[...]
        fill(info, first, second, ((weight, 0, size), (out_weight, size, HV)))

    made = dot(normed[...], weight[...], NT)
    causal = lower_mask()
    every = range(heads)
    for part in range(ROWS // BLOCK):
        span = slice(part * BLOCK, (part + 1) * BLOCK)
        query = [made[span, head * size : head * size + HK] * HK ** (-0.5) for head in every]
        out_gate = [made[span, head * size + HK : (head + 1) * size] for head in every]
        keys = [kv[head, span, :HK] for head in every]
        cum = [cum_in[head, span] for head in every]
        center = [item[MID : MID + 1] for item in cum]
        total = [item[BLOCK - 1 :] for item in cum]
        query_mid = [split_two(query[head] * jnp.exp(cum[head] - center[head])) for head in every]
        key_mid = [split_two(keys[head] * jnp.exp(center[head] - cum[head])) for head in every]
        scores = [dot_split(query_mid[head], key_mid[head], NT) for head in every]
        since = [split_two(query[head] * jnp.exp(cum[head])) for head in every]
        states = [state_ref[head] for head in every]
        carried = [split_two(keys[head] * jnp.exp(total[head] - cum[head])) for head in every]
        values = [split_two(kv[head, span, HK:]) for head in every]
        outer = [dot_split(since[head], split_two(states[head]), NT) for head in every]
        added = [dot_split(values[head], carried[head], TN) for head in every]
        scores = [split_two(jnp.where(causal, item, 0.0)) for item in scores]
        mixed = [dot_split(scores[head], values[head]) + outer[head] for head in every]
        for head in every:
            query_out[head, span] = query[head]
            gate_out[head, span] = out_gate[head]
            state_out[part, head] = states[head]
            state_ref[head] = states[head] * jnp.exp(total[head]) + added[head]
            mixed_out[head, span] = mixed[head]
        for head in every:
            gated_ref[span, head * HV : (head + 1) * HV] = (
                mixed[head]
                * inverse_rms(mixed[head], HEAD_EPS)
                * head_gain[...]
                * (out_gate[head] * sigmoid(out_gate[head]))
            ).astype(BF16)

    for head in every:

        @pl.when(info[2 * GROUPS + heads] == head)
        def _():
            gated_out[...] = gated_ref[:, head * HV : (head + 1) * HV]

    middle = tokens[...].astype(F32) + dot(gated_ref[...], out_weight[...])
    middle_out[...] = middle
    normed_out[...] = (middle * inverse_rms(middle, NORM_EPS) * gain[...]).astype(BF16)


def ffn_kernel(
    weight_pieces, info, normed, back, middle, weight, gain,
    active_out, back_gate_out, back_up_out, layer_out, back_middle_out, back_attn_out, gain_out,
    ffn_ref, back_ref, active_ref, back_gate_ref, back_up_ref,
):
    step, piece = pl.program_id(0), pl.program_id(1)
    units = weight.shape[2] // 3

    @pl.when((step == 0) & (piece == 0))
    def _():
        gain_out[...] = jnp.zeros_like(gain_out)

    @pl.when(piece == 0)
    def _():
        ffn_ref[...] = jnp.zeros_like(ffn_ref)
        back_ref[...] = jnp.zeros_like(back_ref)

    def rows_of(start):
        return jnp.concatenate(
            [weight[group, 0, start : start + units] for group in range(GROUPS)], axis=1
        )

    gate_weight, up_weight, down_weight = rows_of(0), rows_of(units), rows_of(2 * units)
    half = normed.shape[0] // 2
    third = half // FFN_CUTS

    def made(part):
        span = slice(part * half, (part + 1) * half)
        yield dot(normed[span], gate_weight, NT)
        yield dot(normed[span], up_weight, NT)
        yield dot(back[span], down_weight, NT)

    def elementwise(part, values, cut):
        span = slice(cut * third, (cut + 1) * third)
        target = slice(part * half + cut * third, part * half + (cut + 1) * third)
        gate_values, upward, back_active = [item[span] for item in values]
        share = sigmoid(gate_values)
        silu = gate_values * share
        active_ref[target] = (silu * upward).astype(BF16)
        back_gate_ref[target] = (
            back_active * upward * (share * (1.0 + gate_values * (1.0 - share)))
        ).astype(BF16)
        back_up_ref[target] = (back_active * silu).astype(BF16)

    def added(part):
        span = slice(part * half, (part + 1) * half)
        ffn_ref[span] += dot(active_ref[span], down_weight)
        yield
        back_ref[span] += dot(back_gate_ref[span], gate_weight)
        yield
        back_ref[span] += dot(back_up_ref[span], up_weight)
        yield

    first = list(made(0))
    second = []
    for index, item in enumerate(made(1)):
        second.append(item)
        for cut in range(index * FFN_CUTS // 3, (index + 1) * FFN_CUTS // 3):
            elementwise(0, first, cut)
    for index, _ in enumerate(added(0)):
        for cut in range(index * FFN_CUTS // 3, (index + 1) * FFN_CUTS // 3):
            elementwise(1, second, cut)
    for _ in added(1):
        pass

    @pl.when(piece == info[2 * GROUPS + weight_pieces])
    def _():
        active_out[...] = active_ref[...]
        back_gate_out[...] = back_gate_ref[...]
        back_up_out[...] = back_up_ref[...]

    @pl.when(piece == pl.num_programs(1) - 1)
    def _():
        mid = middle[...]
        layer_out[...] = (mid + ffn_ref[...]).astype(BF16)
        inverse = inverse_rms(mid, NORM_EPS)
        unit = mid * inverse
        total = back_ref[...]
        weighted = total * gain[...]
        back_middle = back[...].astype(F32) + inverse * (
            weighted - unit * jnp.mean(weighted * unit, axis=-1, keepdims=True)
        )
        back_middle_out[...] = back_middle
        back_attn_out[...] = back_middle.astype(BF16)
        gain_out[...] += jnp.sum(total * unit, axis=0, keepdims=True)


def gate_back_kernel(
    back_attn, out_weight, mixed_in, gate, query_in, cum_in, head_gain,
    back_mixed_out, back_gate_out, gain_out, state_out,
):
    heads = gate.shape[0]

    @pl.when(pl.program_id(0) == 0)
    def _():
        gain_out[...] = jnp.zeros_like(gain_out)
        state_out[...] = jnp.zeros_like(state_out)

    every = range(heads)
    back_gated = [
        dot(back_attn[...], out_weight[head * HV : (head + 1) * HV], NT) for head in every
    ]
    scaled = [query_in[head] * jnp.exp(cum_in[head]) for head in every]
    back_mixed = []
    for head in every:
        mixed = mixed_in[head]
        out_gate = gate[head]
        inverse = inverse_rms(mixed, HEAD_EPS)
        unit = mixed * inverse
        share = sigmoid(out_gate)
        silu = out_gate * share
        slope = share * (1.0 + out_gate * (1.0 - share))
        shaped_back = back_gated[head] * unit
        back_gate_out[head] = (shaped_back * head_gain[...] * slope).astype(BF16)
        gain_out[...] += jnp.sum(shaped_back * silu, axis=0, keepdims=True)
        weighted = back_gated[head] * head_gain[...] * silu
        item = inverse * (weighted - unit * jnp.mean(weighted * unit, axis=-1, keepdims=True))
        back_mixed_out[head] = item
        back_mixed.append(item)
    for part in reversed(range(ROWS // BLOCK)):
        span = slice(part * BLOCK, (part + 1) * BLOCK)
        added = [
            dot_split(split_two(back_mixed[head][span]), split_two(scaled[head][span]), TN)
            for head in every
        ]
        for head in every:
            last = cum_in[head, (part + 1) * BLOCK - 1 : (part + 1) * BLOCK]
            state_out[head] = state_out[head] * jnp.exp(last) + added[head]


def mix_back_kernel(
    homes, info, tokens, back_middle, query_in, kv, cum_in, logits_in, states, back_mixed, back_gate,
    back_end, query_weight, key_weight, rank_weight, decay_out, rank, gain,
    kept_out, sent_out, rank_grad_out, input_out, decay_grad_out, bias_out, gain_out,
    state_ref, query_ref, key_ref, grad_ref, rank_ref, sum_ref,
):
    heads = back_end.shape[0]
    size = HK + HV
    ranks = rank.shape[1]

    @pl.when(pl.program_id(0) == 0)
    def _():
        state_ref[...] = back_end[...]
        sum_ref[...] = jnp.zeros_like(sum_ref)
        rank_grad_out[...] = jnp.zeros_like(rank_grad_out)
        decay_grad_out[...] = jnp.zeros_like(decay_grad_out)
        bias_out[...] = jnp.zeros_like(bias_out)
        gain_out[...] = jnp.zeros_like(gain_out)

    causal = lower_mask()
    upper = as_ones(upper_mask())
    every = range(heads)
    for part in reversed(range(ROWS // BLOCK)):
        span = slice(part * BLOCK, (part + 1) * BLOCK)
        query = [query_in[head, span] for head in every]
        keys = [kv[head, span, :HK] for head in every]
        cum = [cum_in[head, span] for head in every]
        center = [item[MID : MID + 1] for item in cum]
        total = [item[BLOCK - 1 :] for item in cum]
        grow = [jnp.exp(cum[head] - center[head]) for head in every]
        shrink = [jnp.exp(center[head] - cum[head]) for head in every]
        query_mid = [split_two(query[head] * grow[head]) for head in every]
        key_mid = [split_two(keys[head] * shrink[head]) for head in every]
        values = [split_two(kv[head, span, HK:]) for head in every]
        back = [split_two(back_mixed[head, span]) for head in every]
        scores = [dot_two(query_mid[head], key_mid[head][0], NT) for head in every]
        back_scores = [dot_split(back[head], values[head], NT) for head in every]
        since = [jnp.exp(cum[head]) for head in every]
        until = [jnp.exp(total[head] - cum[head]) for head in every]
        carried = [keys[head] * until[head] for head in every]
        back_state = [state_ref[head] for head in every]
        back_state_parts = [split_two(item) for item in back_state]
        back_carried = [dot_split(values[head], back_state_parts[head]) for head in every]
        back_since = [dot_split(back[head], split_two(states[part, head])) for head in every]
        added = [
            dot_split(back[head], split_two(query[head] * since[head]), TN) for head in every
        ]
        outer = [
            dot_two(split_two(carried[head]), back_state_parts[head][0], NT) for head in every
        ]
        scores = [split_two(jnp.where(causal, item, 0.0)) for item in scores]
        back_scores = [split_two(jnp.where(causal, item, 0.0)) for item in back_scores]
        back_query = [
            dot_split(back_scores[head], key_mid[head]) * grow[head]
            + back_since[head] * since[head]
            for head in every
        ]
        back_keys = [
            dot_split(back_scores[head], query_mid[head], TN) * shrink[head]
            + back_carried[head] * until[head]
            for head in every
        ]
        back_values = [dot_two(scores[head], back[head][0], TN) + outer[head] for head in every]
        back_total = []
        for head in every:
            decayed = back_state[head] * jnp.exp(total[head])
            back_total.append(
                jnp.sum(back_carried[head] * carried[head], axis=0, keepdims=True)
                + jnp.sum(decayed * states[part, head], axis=0, keepdims=True)
            )
            state_ref[head] = decayed + added[head]
        back_logits = [
            (
                dot_sum(upper, query[head] * back_query[head] - keys[head] * back_keys[head])
                + back_total[head]
            )
            * sigmoid(-logits_in[head, span])
            / GATE_SCALE
            for head in every
        ]
        together = jnp.concatenate(back_logits, axis=1)
        rank_back = lax.dot_general(
            together, heads_side_by_side(info, decay_out, 0, ranks), NT,
            precision=lax.Precision.HIGHEST, preferred_element_type=F32,
        )
        decay_grad_out[...] += dot_split(split_two(rank[span]), split_two(together), TN)
        bias_out[...] += jnp.sum(together, axis=0, keepdims=True)
        for head in every:
            at = head * size
            query_ref[span, at : at + HK] = (back_query[head] * HK ** (-0.5)).astype(BF16)
            query_ref[span, at + HK : at + size] = back_gate[head, span]
            key_ref[span, at : at + HK] = back_keys[head].astype(BF16)
            key_ref[span, at + HK : at + size] = back_values[head].astype(BF16)
        rank_ref[span] = rank_back.astype(BF16)

    for head in every:

        @pl.when(info[2 * GROUPS + heads] == head)
        def _():
            grad_ref[:, :size] = query_ref[:, head * size : (head + 1) * size]
            grad_ref[:, size:] = key_ref[:, head * size : (head + 1) * size]

    back_normed = (
        dot(rank_ref[...], rank_weight[...])
        + dot(query_ref[...], query_weight[...])
        + dot(key_ref[...], key_weight[...])
    )
    inputs = tokens[...].astype(F32)
    inverse = inverse_rms(inputs, NORM_EPS)
    unit = inputs * inverse
    normed = (unit * gain[...]).astype(BF16)
    sum_ref[...] += dot(normed, grad_ref[...], TN)
    rank_grad_out[...] += dot(rank_ref[...], normed, TN)
    weighted = back_normed * gain[...]
    input_out[...] = back_middle[...] + inverse * (
        weighted - unit * jnp.mean(weighted * unit, axis=-1, keepdims=True)
    )
    gain_out[...] += jnp.sum(back_normed * unit, axis=0, keepdims=True)

    @pl.when(pl.program_id(0) == pl.num_programs(0) - 1)
    def _():
        for group in range(GROUPS):
            found = slice(group * LANES, (group + 1) * LANES)
            for index, target in enumerate((kept_out, sent_out)):

                @pl.when(info[group] == index)
                def _():
                    target[homes[group]] = sum_ref[found]


def shaped(shape, kind=F32):
    return jax.ShapeDtypeStruct(shape, kind)


def call(kernel, grid, in_specs, out_specs, out_shape, scratch, operands, prefetch, flops, moved):
    return pl.pallas_call(
        kernel,
        grid_spec=pltpu.PrefetchScalarGridSpec(
            num_scalar_prefetch=prefetch,
            grid=grid,
            in_specs=in_specs,
            out_specs=out_specs,
            scratch_shapes=scratch,
        ),
        out_shape=out_shape,
        compiler_params=pltpu.CompilerParams(
            vmem_limit_bytes=VMEM_LIMIT, dimension_semantics=("arbitrary",) * len(grid)
        ),
        cost_estimate=pl.CostEstimate(flops=flops, bytes_accessed=moved, transcendentals=0),
    )(*operands)


def from_behind(value, axis, steps):
    count = lax.axis_size(axis)
    first, last = (max(0, -steps), min(count, count - steps))
    return lax.ppermute(value, axis, [(source, source + steps) for source in range(first, last)])


def carry(local, decay, steps):
    incoming = jnp.zeros_like(local)
    for _ in range(lax.axis_size("ctx") - 1):
        incoming = from_behind(decay * incoming + local, "ctx", steps)
    return incoming


def staged():
    return lax.axis_size("dp") == 4 and lax.axis_size("ctx") == 2


def swap(value, axis, distance):
    count = lax.axis_size(axis)
    return lax.ppermute(value, axis, [(source, source ^ distance) for source in range(count)])


def shift(value, axis, distance):
    count = lax.axis_size(axis)
    return lax.ppermute(
        value, axis, [(source, (source + distance) % count) for source in range(count)]
    )


def gather_plain(pack):
    rows = pack.shape[0]
    whole = lax.all_gather(lax.all_gather(pack, "tp"), ("dp", "ctx"), axis=2, tiled=True)
    return whole.reshape(whole.shape[0], rows, GROUPS, LANES).transpose(2, 0, 1, 3)


def gather_line(pack):
    count = lax.axis_size("tp")
    return jnp.stack([pack] + [shift(pack, "tp", distance) for distance in range(1, count)])


def gather_square(line):
    return [line] + [swap(line, "dp", distance) for distance in range(1, 4)]


def gather_slots(key_pack, query_pack):
    key_line = gather_line(key_pack)
    query_pack, key_line = lax.optimization_barrier((query_pack, key_line))
    key_first = jnp.stack(gather_square(key_line))
    query_line = gather_line(query_pack)
    query_line, key_first = lax.optimization_barrier((query_line, key_first))
    return key_first, swap(key_first, "ctx", 1), gather_square(query_line)


def gather_pair(pack):
    whole = gather_plain(pack)
    half = GROUPS // 2
    return whole[:half], whole[half:]


def gather_homes():
    if staged():
        return [group // 2 for group in range(GROUPS)]
    return [group % (GROUPS // 2) for group in range(GROUPS)]


def gather_info():
    count = lax.axis_size("tp")
    own = lax.axis_index("tp")
    group = jnp.arange(GROUPS, dtype=jnp.int32)
    heads = jnp.arange(count, dtype=jnp.int32)
    if staged():
        which = (group % 2) ^ lax.axis_index("ctx")
        place = (group // 2) ^ lax.axis_index("dp")
        slot = lax.rem(own - heads + count, count)
    else:
        which, place, slot = group // (GROUPS // 2), group % (GROUPS // 2), heads
    return jnp.concatenate([which, place, slot, own.reshape(1)]).astype(jnp.int32)


def gather_whole(pack):
    if staged():
        rows, share = pack.shape
        whole = lax.all_gather(pack, ("dp", "ctx", "tp"))
        return whole.reshape(-1, lax.axis_size("tp"), rows, share)
    return gather_plain(pack)


def finish_sums(kept, sent, sums, early):
    columns = kept.shape[-1]
    if not staged():
        whole = jnp.concatenate([kept, sent]).reshape(-1, columns)
        share = lax.psum_scatter(whole, ("dp", "ctx"), scatter_dimension=0, tiled=True)
        return share, lax.psum(sums, ("dp", "ctx")), early
    device = lax.axis_index("dp")
    row, column = device // 2, device % 2

    def pick(array, axis, index):
        return lax.dynamic_index_in_dim(array, index, axis, keepdims=False)

    value = kept + swap(sent, "ctx", 1)
    sums = sums + swap(sums, "ctx", 1)
    value, sums, early = lax.optimization_barrier((value, sums, early))
    value = value.reshape(2, 2, LANES, columns)
    half = LANES // 2
    upper, lower = value[:, :, :half], value[:, :, half:]
    upper = pick(upper, 1, column) + swap(pick(upper, 1, 1 - column), "dp", 1)
    lower = pick(lower, 0, row) + swap(pick(lower, 0, 1 - row), "dp", 2)
    sums = sums + swap(sums, "dp", 1)
    upper, lower, sums = lax.optimization_barrier((upper, lower, sums))
    upper = pick(upper, 0, row) + swap(pick(upper, 0, 1 - row), "dp", 2)
    lower = pick(lower, 0, column) + swap(pick(lower, 0, 1 - column), "dp", 1)
    sums = sums + swap(sums, "dp", 2)
    return jnp.concatenate([upper, lower]), sums, early


def adamw(weight_now, grad_now, mean_now, square_now, rate_value, decay_value):
    mean_new = BETA_ONE * mean_now + (1.0 - BETA_ONE) * grad_now
    square_new = BETA_TWO * square_now + (1.0 - BETA_TWO) * grad_now * grad_now
    mean_hat = mean_new / (1.0 - BETA_ONE**STEP)
    square_hat = square_new / (1.0 - BETA_TWO**STEP)
    weight_new = weight_now - rate_value * (
        mean_hat / (jnp.sqrt(square_hat) + ADAM_EPS) + decay_value * weight_now
    )
    return (mean_new, square_new, weight_new)


def three_parts(value):
    high = lax.reduce_precision(value, 8, 7)
    rest = value - high
    middle = lax.reduce_precision(rest, 8, 7)
    low = lax.reduce_precision(rest - middle, 8, 7)
    return [part.astype(BF16) for part in (high, middle, low)]


def body(
    tokens,
    cotangent,
    lengths,
    query_key_weight,
    query_key_mean,
    query_key_square,
    value_gate_weight,
    value_gate_mean,
    value_gate_square,
    decay_in_weight,
    decay_in_mean,
    decay_in_square,
    decay_out_weight,
    decay_out_mean,
    decay_out_square,
    decay_bias,
    decay_bias_mean,
    decay_bias_square,
    output_weight,
    output_mean,
    output_square,
    gate_up_weight,
    gate_up_mean,
    gate_up_square,
    down_weight,
    down_mean,
    down_square,
    gains,
    gains_mean,
    gains_square,
):
    rows, width = tokens.shape
    heads = lax.axis_size("tp")
    ranks = decay_in_weight.shape[1]
    units = down_weight.shape[0]
    steps = rows // ROWS
    info = gather_info()
    gain_one = gains[:width].reshape(1, width)
    gain_two = gains[width : 2 * width].reshape(1, width)
    gain_head = gains[2 * width :].reshape(1, HV)
    size = HK + HV

    small = jnp.concatenate(
        [
            decay_out_weight,
            decay_bias.reshape(1, HK),
            jnp.zeros((DECAY_ROWS - ranks - 1, HK), F32),
        ]
    )
    key_parts = [
        query_key_weight[1].T.astype(BF16),
        value_gate_weight[0].T.astype(BF16),
        decay_in_weight.T.astype(BF16),
    ]
    query_pack = jnp.concatenate(
        [query_key_weight[0].T, value_gate_weight[1].T, output_weight]
    ).astype(BF16)
    if staged():
        key_first, key_second, query_square = gather_slots(
            jnp.concatenate(key_parts + three_parts(small)), query_pack
        )
        sent = key_first[0, :, size + ranks :].astype(F32).reshape(heads, 3, DECAY_ROWS, HK)
        decay_out_full = sent[:, 0] + sent[:, 1] + sent[:, 2]
    else:
        key_first, key_second = gather_pair(jnp.concatenate(key_parts))
        query_first, query_second = gather_pair(query_pack)
        decay_out_full = lax.all_gather(small, "tp")
    ffn = gather_whole(
        jnp.concatenate([gate_up_weight[0].T, gate_up_weight[1].T, down_weight]).astype(BF16)
    )

    position = lax.axis_index("ctx") * rows + jnp.arange(rows, dtype=jnp.int32)
    back_ffn = jnp.where((position < lengths[0])[:, None], cotangent, jnp.zeros_like(cotangent))

    columns = 2 * size
    row_spec = pl.BlockSpec((ROWS, width), lambda i, *_: (i, 0))
    gain_spec = pl.BlockSpec((1, width), lambda i, *_: (0, 0))
    head_gain_spec = pl.BlockSpec((1, HV), lambda i, *_: (0, 0))
    state_spec = pl.BlockSpec((heads, HV, HK), lambda i, *_: (0, 0, 0))
    bias_spec = pl.BlockSpec((heads, 1, HK), lambda i, *_: (0, 0, 0))

    def fixed(array):
        return pl.BlockSpec(
            array.shape, lambda i, *_: (0,) * len(array.shape), pipeline_mode=pl.Buffered(1)
        )

    def by_head(length, reverse=False):
        if reverse:
            return pl.BlockSpec((heads, ROWS, length), lambda i, *_: (0, steps - 1 - i, 0))
        return pl.BlockSpec((heads, ROWS, length), lambda i, *_: (0, i, 0))

    weight_shape = shaped((heads * size, width), BF16)
    rank_shape = shaped((ranks, width), BF16)
    out_weight_shape = shaped((heads * HV, width), BF16)
    parts = ROWS // BLOCK
    normed, kv, rank, logits, cum, local_state, local_total, key_weight, rank_weight = call(
        project_kernel,
        (steps,),
        [row_spec, gain_spec, fixed(key_first), fixed(key_second), fixed(decay_out_full)],
        [
            row_spec,
            by_head(size),
            pl.BlockSpec((ROWS, ranks), lambda i, *_: (i, 0)),
            by_head(HK),
            by_head(HK),
            state_spec,
            bias_spec,
            fixed(weight_shape),
            fixed(rank_shape),
        ],
        [
            shaped((rows, width), BF16),
            shaped((heads, rows, size)),
            shaped((rows, ranks)),
            shaped((heads, rows, HK)),
            shaped((heads, rows, HK)),
            shaped((heads, HV, HK)),
            shaped((heads, 1, HK)),
            weight_shape,
            rank_shape,
        ],
        [],
        (info, tokens, gain_one, key_first, key_second, decay_out_full),
        1,
        2 * rows * width * size * heads,
        rows * heads * 4 * 1024,
    )
    if staged():
        query_square, local_state = lax.optimization_barrier((query_square, local_state))
        query_first = jnp.stack(query_square)
        query_second = swap(query_first, "ctx", 1)
    device_decay = jnp.exp(local_total)
    start_state = carry(local_state, device_decay, 1)

    query, out_gate, mixed, states, gated_own, middle, normed_two, query_weight, out_weight = call(
        mix_kernel,
        (steps,),
        [
            row_spec,
            row_spec,
            by_head(size),
            by_head(HK),
            state_spec,
            fixed(query_first),
            fixed(query_second),
            head_gain_spec,
            gain_spec,
        ],
        [
            by_head(HK),
            by_head(HV),
            by_head(HV),
            pl.BlockSpec((parts, heads, HV, HK), lambda i, *_: (i, 0, 0, 0)),
            pl.BlockSpec((ROWS, HV), lambda i, *_: (i, 0)),
            row_spec,
            row_spec,
            fixed(weight_shape),
            fixed(out_weight_shape),
        ],
        [
            shaped((heads, rows, HK)),
            shaped((heads, rows, HV)),
            shaped((heads, rows, HV)),
            shaped((steps * parts, heads, HV, HK)),
            shaped((rows, HV), BF16),
            shaped((rows, width)),
            shaped((rows, width), BF16),
            weight_shape,
            out_weight_shape,
        ],
        [pltpu.VMEM((heads, HV, HK), F32), pltpu.VMEM((ROWS, heads * HV), BF16)],
        (
            info, tokens, normed, kv, cum, start_state, query_first, query_second,
            gain_head, gain_two,
        ),
        1,
        2 * rows * width * (size + 2 * HV) * heads,
        rows * heads * 4 * 1024,
    )

    wide_spec = pl.BlockSpec((FFN_ROWS, width), lambda i, j, *_: (i, 0))
    own_spec = pl.BlockSpec((FFN_ROWS, units), lambda i, j, *_: (i, 0))
    wide_gain_spec = pl.BlockSpec((1, width), lambda i, j, *_: (0, 0))
    active, back_gate, back_up, layer_out, back_middle, back_attn, gain_two_part = call(
        functools.partial(ffn_kernel, heads),
        (rows // FFN_ROWS, heads),
        [
            wide_spec,
            wide_spec,
            wide_spec,
            pl.BlockSpec((GROUPS, 1, 3 * units, LANES), lambda i, j, *_: (0, j, 0, 0)),
            wide_gain_spec,
        ],
        [own_spec, own_spec, own_spec, wide_spec, wide_spec, wide_spec, wide_gain_spec],
        [
            shaped((rows, units), BF16),
            shaped((rows, units), BF16),
            shaped((rows, units), BF16),
            shaped((rows, width), BF16),
            shaped((rows, width)),
            shaped((rows, width), BF16),
            shaped((1, width)),
        ],
        [
            pltpu.VMEM((FFN_ROWS, width), F32),
            pltpu.VMEM((FFN_ROWS, width), F32),
            pltpu.VMEM((FFN_ROWS, units), BF16),
            pltpu.VMEM((FFN_ROWS, units), BF16),
            pltpu.VMEM((FFN_ROWS, units), BF16),
        ],
        (info, normed_two, back_ffn, middle, ffn, gain_two),
        1,
        12 * rows * width * units * heads,
        rows * width * 24,
    )
    early_grad = jnp.concatenate(
        [
            dot(back_gate, normed_two, TN),
            dot(back_up, normed_two, TN),
            dot(active, back_ffn, TN),
            dot(gated_own, back_attn, TN),
        ]
    )
    early_grad, back_attn = lax.optimization_barrier((early_grad, back_attn))
    early_share = lax.psum_scatter(early_grad, ("dp", "ctx"), scatter_dimension=1, tiled=True)

    back_row_spec = pl.BlockSpec((ROWS, width), lambda i, *_: (steps - 1 - i, 0))
    back_mixed, back_out_gate, head_gain_part, collected = call(
        gate_back_kernel,
        (steps,),
        [
            back_row_spec,
            fixed(out_weight),
            by_head(HV, True),
            by_head(HV, True),
            by_head(HK, True),
            by_head(HK, True),
            head_gain_spec,
        ],
        [by_head(HV, True), by_head(HV, True), head_gain_spec, state_spec],
        [
            shaped((heads, rows, HV)),
            shaped((heads, rows, HV), BF16),
            shaped((1, HV)),
            shaped((heads, HV, HK)),
        ],
        [],
        (back_attn, out_weight, mixed, out_gate, query, cum, gain_head),
        0,
        2 * rows * width * HV * heads,
        rows * heads * 4 * 1024,
    )
    back_end = carry(collected, device_decay, -1)

    grad_shape = shaped((GROUPS // 2, LANES, columns))
    rank_grad_shape = shaped((ranks, width))
    kept, sent_away, rank_grad, input_grad, decay_out_grad, bias_grad, gain_one_part = call(
        functools.partial(mix_back_kernel, gather_homes()),
        (steps,),
        [
            back_row_spec,
            back_row_spec,
            by_head(HK, True),
            by_head(size, True),
            by_head(HK, True),
            by_head(HK, True),
            pl.BlockSpec((parts, heads, HV, HK), lambda i, *_: (steps - 1 - i, 0, 0, 0)),
            by_head(HV, True),
            by_head(HV, True),
            state_spec,
            fixed(query_weight),
            fixed(key_weight),
            fixed(rank_weight),
            fixed(decay_out_full),
            pl.BlockSpec((ROWS, ranks), lambda i, *_: (steps - 1 - i, 0)),
            gain_spec,
        ],
        [
            fixed(grad_shape),
            fixed(grad_shape),
            fixed(rank_grad_shape),
            back_row_spec,
            pl.BlockSpec((ranks, heads * HK), lambda i, *_: (0, 0)),
            pl.BlockSpec((1, heads * HK), lambda i, *_: (0, 0)),
            gain_spec,
        ],
        [
            grad_shape,
            grad_shape,
            rank_grad_shape,
            shaped((rows, width)),
            shaped((ranks, heads * HK)),
            shaped((1, heads * HK)),
            shaped((1, width)),
        ],
        [
            pltpu.VMEM((heads, HV, HK), F32),
            pltpu.VMEM((ROWS, heads * size), BF16),
            pltpu.VMEM((ROWS, heads * size), BF16),
            pltpu.VMEM((ROWS, columns), BF16),
            pltpu.VMEM((ROWS, ranks), BF16),
            pltpu.VMEM((width, columns), F32),
        ],
        (
            info, tokens, back_middle, query, kv, cum, logits, states, back_mixed, back_out_gate,
            back_end, query_weight, key_weight, rank_weight, decay_out_full, rank, gain_one,
        ),
        1,
        2 * rows * width * columns * heads * 2,
        rows * heads * 4 * 2048,
    )
    own = info[-1]
    decay_out_own = lax.dynamic_slice_in_dim(decay_out_grad, own * HK, HK, axis=1)
    bias_own = lax.dynamic_slice_in_dim(bias_grad, own * HK, HK, axis=1)
    sums = jnp.concatenate(
        [
            gain_one_part.reshape(-1),
            gain_two_part.reshape(-1),
            head_gain_part.reshape(-1),
            bias_own.reshape(-1),
            decay_out_own.reshape(-1),
            rank_grad.reshape(-1),
        ]
    )
    mixer_share, sums, early_share = finish_sums(kept, sent_away, sums, early_share)
    gain_count = gains.shape[0]
    decay_start = gain_count + HK
    rank_start = decay_start + ranks * HK
    gains_grad = sums[:gain_count]
    bias_total = sums[gain_count:decay_start]
    decay_out_total = sums[decay_start:rank_start].reshape(ranks, HK)
    share = decay_in_weight.shape[0]
    place = (lax.axis_index("dp") * lax.axis_size("ctx") + lax.axis_index("ctx")) * share
    decay_in_share = lax.dynamic_slice_in_dim(
        sums[rank_start:].reshape(ranks, width), place, share, axis=1
    ).T

    query_key_share = jnp.stack([mixer_share[:, :HK], mixer_share[:, size : size + HK]])
    value_gate_share = jnp.stack([mixer_share[:, size + HK : columns], mixer_share[:, HK:size]])
    gate_up_share = jnp.stack([early_share[:units].T, early_share[units : 2 * units].T])
    down_share = early_share[2 * units : 3 * units]
    output_share = early_share[3 * units :]

    updated = adamw(
        query_key_weight,
        query_key_share,
        query_key_mean,
        query_key_square,
        RATE_MATRIX,
        WEIGHT_DECAY,
    )
    updated = updated + adamw(
        value_gate_weight,
        value_gate_share,
        value_gate_mean,
        value_gate_square,
        RATE_MATRIX,
        WEIGHT_DECAY,
    )
    updated = updated + adamw(
        decay_in_weight, decay_in_share, decay_in_mean, decay_in_square, RATE_MATRIX, WEIGHT_DECAY
    )
    updated = updated + adamw(
        decay_out_weight, decay_out_total, decay_out_mean, decay_out_square, RATE_RANK, WEIGHT_DECAY
    )
    updated = updated + adamw(
        decay_bias, bias_total, decay_bias_mean, decay_bias_square, RATE_BIAS, 0.0
    )
    updated = updated + adamw(
        output_weight, output_share, output_mean, output_square, RATE_MATRIX, WEIGHT_DECAY
    )
    updated = updated + adamw(
        gate_up_weight, gate_up_share, gate_up_mean, gate_up_square, RATE_MATRIX, WEIGHT_DECAY
    )
    updated = updated + adamw(
        down_weight, down_share, down_mean, down_square, RATE_MATRIX, WEIGHT_DECAY
    )
    updated = updated + adamw(gains, gains_grad, gains_mean, gains_square, RATE_GAIN, 0.0)
    return (layer_out, input_grad) + updated


def solution(mesh):
    tokens_at = P(("dp", "ctx"), None)
    split_at = P(None, ("dp", "ctx"), "tp")
    deep_at = P("tp", ("dp", "ctx"))
    rank_out_at = P(None, "tp")
    kinds = (split_at, split_at, tokens_at, rank_out_at, P("tp"), deep_at, split_at, deep_at, P())
    params = tuple(kind for kind in kinds for _ in range(3))
    return jax.shard_map(
        body,
        mesh=mesh,
        in_specs=(tokens_at, tokens_at, P("dp")) + params,
        out_specs=(tokens_at, tokens_at) + params,
        check_vma=False,
    )
```
